256 devices in a mesh: ctx: 16 (over z, y_lo), req: 16 (over x, y_hi, core).
Axes of the slice: x: 4, y: 4 (y_hi: 2, y_lo: 2; y = y_hi * 2 + y_lo), z: 8, core: 2. Of those that a mesh axis runs over, the one named last changes fastest.
Arguments:
- hidden_in: bfloat16 [1024, 4608], P('req'), may hold values from -6 to 6
- queries: bfloat16 [1024, 4096], P('req'), may hold values from -6 to 6
- suffix_kv: bfloat16 [2, 1024, 2048], P(None, 'req'), may hold values from -6 to 6
- prefix_kv: bfloat16 [2, 32, 2048, 2048], P(None, 'req', 'ctx'), may hold values from -6 to 6
- hyp_prefix: int32 [64], P('req'), may hold values from 0 to 31, as said below
- suffix_len: int32 [64], P('req'), may hold values from 1 to 16
- prefix_len: int32 [32], P('req'), may hold values from 1 to 2048
- w_out: bfloat16 [4096, 4608], P('ctx'), may hold values from -0.09375 to 0.09375
- gain_attn: float32 [4608], replicated, may hold values from 0.25 to 1.75
- gain_pre: float32 [4608], replicated, may hold values from 0.25 to 1.75
- w_gate: bfloat16 [4608, 36864], P(None, ('req', 'ctx')), may hold values from -0.09375 to 0.09375
- w_up: bfloat16 [4608, 36864], P(None, ('req', 'ctx')), may hold values from -0.09375 to 0.09375
- w_down: bfloat16 [36864, 4608], P('req', 'ctx'), may hold values from -0.03125 to 0.03125
Outputs:
- resid: bfloat16 [1024, 4608], P('req')
- ffn_out: bfloat16 [1024, 4608], P('req', 'ctx')
The draws below stay inside these ranges and needn't reach their ends.
Inputs may be any that keep to these rules, and one draw needn't show every extreme that they name: `hyp_prefix`: hypothesis h continues a prefix of its own request group, one of (h // 4) * 2 to (h // 4) * 2 + 1.
All inputs are finite; a program needn't handle non-finite values.
Results may differ from the reference program's by a relative error of at most 0.012.
Values may be sent and summed in bfloat16 or wider, within the bound.
A program may use at most 64 MiB of HBM per device.

```python
import jax
import jax.numpy as jnp
from jax import lax

D = 4608
HEADS = 32
KV_HEADS = 16
HEAD = 128
FF = 36864
HYP_GRP = 4
SUF = 16
P_GRP = 2
HYP = 64
TOKENS = 1024
PREFIXES = 32
PREF = 2048


def draw_hyp_prefix(key, part):
    key = jax.random.fold_in(key, 11)
    local = jax.random.randint(key, (HYP,), 0, P_GRP)
    places = jnp.arange(HYP)
    local = jnp.where(places == 0, 0, jnp.where(places == HYP - 1, P_GRP - 1, local))
    return (places // HYP_GRP * P_GRP + local).astype(jnp.int32)


def draw_suffix_len(key, part):
    key = jax.random.fold_in(key, 23)
    drawn = jax.random.randint(key, (HYP,), 1, SUF + 1)
    return jnp.where(jnp.arange(HYP) == 0, SUF, drawn).astype(jnp.int32)


def draw_prefix_len(key, part):
    key = jax.random.fold_in(key, 37)
    drawn = jax.random.randint(key, (PREFIXES,), 1, PREF + 1)
    return jnp.where(jnp.arange(PREFIXES) == 0, PREF, drawn).astype(jnp.int32)


def level_of(rng, extent, shards, low, largest):
    def one(dim, parts):
        heights = jax.random.uniform(jax.random.fold_in(jax.random.fold_in(rng, 6), dim), (parts,), jnp.float32, low / len(shards), largest / len(shards))
        return jnp.repeat(jnp.exp(heights), extent[dim] // parts).reshape((-1,) + (1,) * (len(extent) - dim - 1))

    gain = one(*shards[0])
    for cut in shards[1:]:
        gain = gain * one(*cut)
    return gain


def centred(key, dims, scale, limit, cuts=(), kind=jnp.bfloat16):
    entries = jax.random.normal(key, dims, jnp.float32) * scale
    if len(cuts) > 0:
        entries = level_of(key, dims, cuts, -0.22, 0.18) * entries
    return jnp.clip(entries, min=-limit, max=limit).astype(kind)


def setup_inputs(seed: int = 0) -> dict:
    keys = jax.random.split(jax.random.key(seed), 14)
    return {
        "hidden_in": centred(keys[0], (TOKENS, D), 1.0, 6.0, ((0, 16),)),
        "queries": centred(keys[1], (TOKENS, HEADS * HEAD), 1.0, 6.0, ((0, 16),)),
        "suffix_kv": centred(keys[2], (2, TOKENS, KV_HEADS * HEAD), 1.0, 6.0, ((1, 16),)),
        "prefix_kv": centred(keys[3], (2, PREFIXES, PREF, KV_HEADS * HEAD), 1.0, 6.0, ((1, 16), (2, 16))),
        "hyp_prefix": draw_hyp_prefix(jax.random.fold_in(keys[13], 71), 0),
        "suffix_len": draw_suffix_len(jax.random.fold_in(keys[13], 71), 0),
        "prefix_len": draw_prefix_len(jax.random.fold_in(keys[13], 71), 0),
        "w_out": centred(keys[7], (HEADS * HEAD, D), (HEADS * HEAD) ** -0.5, 0.09375, ((0, 16),)),
        "gain_attn": jnp.clip(1.0 + 0.15 * jax.random.normal(keys[8], (D,), jnp.float32), 0.25, 1.75),
        "gain_pre": jnp.clip(1.0 + 0.15 * jax.random.normal(keys[9], (D,), jnp.float32), 0.25, 1.75),
        "w_gate": centred(keys[10], (D, FF), D ** -0.5, 0.09375, ((1, 256),)),
        "w_up": centred(keys[11], (D, FF), D ** -0.5, 0.09375, ((1, 256),)),
        "w_down": centred(keys[12], (FF, D), FF ** -0.5, 0.03125, ((0, 16), (1, 16))),
    }


softcap = 50.0
query_scale = 144.0 ** (-0.5)
eps = 1e-06

def capped(query_part, key_block):
    scores = jnp.einsum('skgd,nkd->skgn', query_part, key_block) * query_scale
    return softcap * jnp.tanh(scores / softcap)

def reference(hidden_in, queries, suffix_kv, prefix_kv, hyp_prefix, suffix_len, prefix_len, w_out, gain_attn, gain_pre, w_gate, w_up, w_down):
    head_group = HEADS // KV_HEADS

    def one_hyp(hyp_row):
        prefix_id = hyp_prefix[hyp_row]
        first = (hyp_row * SUF).astype(jnp.int32)
        query_part = lax.dynamic_slice_in_dim(queries, first, SUF, 0).astype(jnp.float32).reshape(SUF, KV_HEADS, head_group, HEAD)
        pre_keys = prefix_kv[0, prefix_id].astype(jnp.float32).reshape(PREF, KV_HEADS, HEAD)
        pre_vals = prefix_kv[1, prefix_id].astype(jnp.float32).reshape(PREF, KV_HEADS, HEAD)
        suf_keys = lax.dynamic_slice_in_dim(suffix_kv[0], first, SUF, 0).astype(jnp.float32).reshape(SUF, KV_HEADS, HEAD)
        suf_vals = lax.dynamic_slice_in_dim(suffix_kv[1], first, SUF, 0).astype(jnp.float32).reshape(SUF, KV_HEADS, HEAD)
        pre_ok = jnp.arange(PREF, dtype=jnp.int32) < prefix_len[prefix_id]
        pre_w = jnp.where(pre_ok[None, None, None, :], jnp.exp(capped(query_part, pre_keys)), jnp.float32(0.0))
        places = jnp.arange(SUF, dtype=jnp.int32)
        suf_ok = (places[None, :] <= places[:, None]) & (places[None, :] < suffix_len[hyp_row])
        suf_w = jnp.where(suf_ok[:, None, None, :], jnp.exp(capped(query_part, suf_keys)), jnp.float32(0.0))
        total = lax.optimization_barrier(jnp.sum(pre_w, -1)) + lax.optimization_barrier(jnp.sum(suf_w, -1))
        pre_b = lax.optimization_barrier(pre_w.astype(jnp.bfloat16)).astype(jnp.float32)
        suf_b = lax.optimization_barrier(suf_w.astype(jnp.bfloat16)).astype(jnp.float32)
        summed = jnp.einsum('skgn,nkd->skgd', pre_b, pre_vals) + jnp.einsum('skgn,nkd->skgd', suf_b, suf_vals)
        return (summed / total[..., None]).astype(jnp.bfloat16).reshape(SUF, HEADS * HEAD)
    attn = lax.map(one_hyp, jnp.arange(HYP, dtype=jnp.int32)).reshape(TOKENS, HEADS * HEAD)
    proj = jnp.dot(attn, w_out, preferred_element_type=jnp.float32)
    scale_a = lax.rsqrt(lax.optimization_barrier(jnp.mean(proj * proj, -1, keepdims=True)) + eps)
    resid = (hidden_in.astype(jnp.float32) + gain_attn * proj * scale_a).astype(jnp.bfloat16)
    resid_f = resid.astype(jnp.float32)
    scale_b = lax.rsqrt(lax.optimization_barrier(jnp.mean(resid_f * resid_f, -1, keepdims=True)) + eps)
    normed = (resid_f * scale_b * gain_pre).astype(jnp.bfloat16)
    gate = jnp.dot(normed, w_gate, preferred_element_type=jnp.float32)
    upper = jnp.dot(normed, w_up, preferred_element_type=jnp.float32)
    hidden = (jax.nn.gelu(gate, approximate=True) * upper).astype(jnp.bfloat16)
    ffn_out = jnp.dot(hidden, w_down, preferred_element_type=jnp.float32).astype(jnp.bfloat16)
    return (resid, ffn_out)
```

```python
import functools

import jax
import jax.numpy as jnp
from jax import lax
from jax.experimental import pallas as pl
from jax.experimental.pallas import tpu as pltpu
from jax.sharding import PartitionSpec as P

HEADS = 32
KV_HEADS = 16
HEAD = 128

softcap = 50.0
query_scale = 144.0 ** (-0.5)
eps = 1e-06

NT = (((1,), (1,)), ((), ()))
NN = (((1,), (0,)), ((), ()))


def weights_of(scores):
    return jnp.exp(softcap * jnp.tanh(scores * (query_scale / softcap)))


def attention_kernel(
    n,
    queries,
    suffix_kv,
    prefix_kv,
    hyp_prefix,
    suffix_len,
    prefix_len,
    w_out,
    hidden_in,
    gain_attn,
    resid_out,
    mask,
    part_send,
    part_recv,
    proj_send,
    proj_recv,
    part_ssem,
    part_rsem,
    proj_ssem,
    proj_rsem,
    resid_ssem,
    resid_rsem,
):
    me = lax.axis_index("ctx")
    req = lax.axis_index("req")
    tokens = queries.shape[0]
    prefixes, block = prefix_kv.shape[1], prefix_kv.shape[2]
    group = HEADS // KV_HEADS
    rows = group * tokens
    hyps = hyp_prefix.shape[0]
    suf = tokens // hyps
    slab = tokens // n
    width = w_out.shape[1]

    barrier = pltpu.get_barrier_semaphore()

    def greet(s, _):
        pl.semaphore_signal(
            barrier, inc=1, device_id={"ctx": lax.rem(me + s, n)}, device_id_type=pl.DeviceIdType.MESH
        )
        return 0

    lax.fori_loop(1, n, greet, 0)

    row = lax.broadcasted_iota(jnp.int32, (rows, prefixes * block), 0)
    col = lax.broadcasted_iota(jnp.int32, (rows, prefixes * block), 1)
    hyp_of_row = lax.rem(row, tokens) // suf
    row_pid = jnp.zeros_like(row)
    for h in range(hyps):
        row_pid = jnp.where(hyp_of_row == h, hyp_prefix[h] - req * prefixes, row_pid)
    col_pid = col // block
    col_len = jnp.zeros_like(row)
    for p in range(prefixes):
        col_len = jnp.where(col_pid == p, prefix_len[p], col_len)
    ok = (row_pid == col_pid) & (me * block + lax.rem(col, block) < col_len)
    mask[...] = jnp.where(ok, 1.0, 0.0)
    eye = lax.broadcasted_iota(jnp.int32, (rows, rows), 0) == lax.broadcasted_iota(jnp.int32, (rows, rows), 1)

    pl.semaphore_wait(barrier, n - 1)

    def query_rows(head):
        both = queries[:, pl.ds(pl.multiple_of(head * (group * HEAD), group * HEAD), group * HEAD)]
        return jnp.concatenate([both[:, g * HEAD : (g + 1) * HEAD] for g in range(group)], 0)

    def partial_of(head):
        lanes = pl.ds(pl.multiple_of(head * HEAD, HEAD), HEAD)
        query = query_rows(head)
        keys = prefix_kv[0, :, :, lanes].reshape(prefixes * block, HEAD)
        vals = prefix_kv[1, :, :, lanes].reshape(prefixes * block, HEAD)
        scores = lax.dot_general(query, keys, NT, preferred_element_type=jnp.float32)
        weights = jnp.where(mask[...] > 0.5, weights_of(scores), 0.0)
        summed = jnp.dot(weights.astype(jnp.bfloat16), vals, preferred_element_type=jnp.float32)
        return summed, jnp.sum(weights, 1, keepdims=True)

    def store_partial(ref, summed, total):
        ref[0:rows, :] = summed.astype(jnp.bfloat16)
        flat = jnp.sum(jnp.where(eye, total, 0.0), 0, keepdims=True)
        high = flat.astype(jnp.bfloat16).astype(jnp.float32)
        low = flat - high
        place = lax.broadcasted_iota(jnp.int32, (16, rows), 0)
        ref[rows : rows + 16, :] = jnp.where(
            place == 0, high, jnp.where(place == 1, low, 0.0)
        ).astype(jnp.bfloat16)

    def part_copy(peer):
        return pltpu.make_async_remote_copy(
            src_ref=part_send.at[peer],
            dst_ref=part_recv.at[me],
            send_sem=part_ssem.at[peer],
            recv_sem=part_rsem.at[me],
            device_id={"ctx": peer},
            device_id_type=pl.DeviceIdType.MESH,
        )

    def send_part(s, _):
        peer = lax.rem(me + s, n)
        summed, total = partial_of(peer)
        store_partial(part_send.at[peer], summed, total)
        part_copy(peer).start()
        return 0

    lax.fori_loop(1, n, send_part, 0, unroll=3)

    summed, total = partial_of(me)
    own = pl.ds(pl.multiple_of(me * HEAD, HEAD), HEAD)
    suf_row = lax.rem(lax.broadcasted_iota(jnp.int32, (rows, tokens), 0), tokens)
    suf_col = lax.broadcasted_iota(jnp.int32, (rows, tokens), 1)
    row_hyp, col_hyp = suf_row // suf, suf_col // suf
    place = suf_col - col_hyp * suf
    length = jnp.zeros_like(suf_row)
    for h in range(hyps):
        length = jnp.where(col_hyp == h, suffix_len[h], length)
    usable = (row_hyp == col_hyp) & (suf_col <= suf_row) & (place < length)
    scores = lax.dot_general(query_rows(me), suffix_kv[0, :, own], NT, preferred_element_type=jnp.float32)
    weights = jnp.where(usable, weights_of(scores), 0.0)
    summed += jnp.dot(weights.astype(jnp.bfloat16), suffix_kv[1, :, own], preferred_element_type=jnp.float32)
    total += jnp.sum(weights, 1, keepdims=True)

    def add_part(s, carry):
        summed, flat = carry
        peer = lax.rem(me + n - s, n)
        part = part_recv.at[peer]
        pltpu.make_async_remote_copy(
            src_ref=part_send.at[peer],
            dst_ref=part,
            send_sem=part_ssem.at[peer],
            recv_sem=part_rsem.at[peer],
            device_id={"ctx": peer},
            device_id_type=pl.DeviceIdType.MESH,
        ).wait_recv()
        summed = summed + part[0:rows, :].astype(jnp.float32)
        flat = flat + part[rows : rows + 16, :].astype(jnp.float32)
        return summed, flat

    summed, flat = lax.fori_loop(1, n, add_part, (summed, jnp.zeros((16, rows), jnp.float32)))
    flat = jnp.sum(flat, 0, keepdims=True)
    total += jnp.sum(jnp.where(eye, flat, 0.0), 1, keepdims=True)
    attn = (summed / total).astype(jnp.bfloat16)
    attn = jnp.concatenate([attn[g * tokens : (g + 1) * tokens] for g in range(group)], 1)

    step = 512
    for c in range(0, width, step):
        term = jnp.dot(attn, w_out[:, c : c + step], preferred_element_type=jnp.float32)
        for i in range(n):
            proj_send[i, :, c : c + step] = term[i * slab : (i + 1) * slab].astype(jnp.bfloat16)

    def proj_copy(peer, slot):
        return pltpu.make_async_remote_copy(
            src_ref=proj_send.at[peer],
            dst_ref=proj_recv.at[slot],
            send_sem=proj_ssem.at[peer],
            recv_sem=proj_rsem.at[slot],
            device_id={"ctx": peer},
            device_id_type=pl.DeviceIdType.MESH,
        )

    def send_proj(s, _):
        proj_copy(lax.rem(me + s, n), me).start()
        return 0

    lax.fori_loop(1, n, send_proj, 0)

    around = hidden_in[pl.ds(pl.multiple_of(me * slab // 16 * 16, 16), 16), :].astype(jnp.float32)
    mine = jnp.zeros((slab, width), jnp.float32)
    for g in range(16 // slab):
        mine = jnp.where(lax.rem(me, 16 // slab) == g, around[g * slab : (g + 1) * slab], mine)

    def add_proj(s, proj):
        peer = lax.rem(me + n - s, n)
        proj_copy(peer, peer).wait_recv()
        return proj + proj_recv[peer].astype(jnp.float32)

    proj = lax.fori_loop(1, n, add_proj, proj_send[me].astype(jnp.float32))
    scale_a = lax.rsqrt(jnp.mean(proj * proj, 1, keepdims=True) + eps)
    resid_out[me] = (mine + gain_attn[...] * proj * scale_a).astype(jnp.bfloat16)

    def resid_copy(peer, slot):
        return pltpu.make_async_remote_copy(
            src_ref=resid_out.at[slot],
            dst_ref=resid_out.at[slot],
            send_sem=resid_ssem.at[peer],
            recv_sem=resid_rsem.at[slot],
            device_id={"ctx": peer},
            device_id_type=pl.DeviceIdType.MESH,
        )

    def send_resid(s, _):
        resid_copy(lax.rem(me + s, n), me).start()
        return 0

    lax.fori_loop(1, n, send_resid, 0)

    def finish(s, _):
        peer = lax.rem(me + s, n)
        resid_copy(peer, peer).wait_recv()
        part_copy(peer).wait_send()
        proj_copy(peer, me).wait_send()
        resid_copy(peer, me).wait_send()
        return 0

    lax.fori_loop(1, n, finish, 0)


def attention(n, queries, suffix_kv, prefix_kv, hyp_prefix, suffix_len, prefix_len, w_out, hidden_in, gain_attn):
    tokens, width = hidden_in.shape
    rows = HEADS // KV_HEADS * tokens
    slab = tokens // n
    positions = prefix_kv.shape[1] * prefix_kv.shape[2]
    vmem = pl.BlockSpec(memory_space=pltpu.VMEM)
    smem = pl.BlockSpec(memory_space=pltpu.SMEM)
    dma = pltpu.SemaphoreType.DMA((n,))
    resid = pl.pallas_call(
        functools.partial(attention_kernel, n),
        out_shape=jax.ShapeDtypeStruct((n, slab, width), jnp.bfloat16),
        in_specs=[vmem, vmem, vmem, smem, smem, smem, vmem, vmem, vmem],
        out_specs=vmem,
        scratch_shapes=[
            pltpu.VMEM((rows, positions), jnp.float32),
            pltpu.VMEM((n, rows + 16, HEAD), jnp.bfloat16),
            pltpu.VMEM((n, rows + 16, HEAD), jnp.bfloat16),
            pltpu.VMEM((n, slab, width), jnp.bfloat16),
            pltpu.VMEM((n, slab, width), jnp.bfloat16),
            dma,
            dma,
            dma,
            dma,
            dma,
            dma,
        ],
        compiler_params=pltpu.CompilerParams(
            collective_id=0, has_side_effects=True, vmem_limit_bytes=40 * 2**20
        ),
        cost_estimate=pl.CostEstimate(flops=10**9, bytes_accessed=10**7, transcendentals=10**6),
        name="attention_projection",
    )(queries, suffix_kv, prefix_kv, hyp_prefix, suffix_len, prefix_len, w_out, hidden_in, gain_attn.reshape(1, -1))
    return resid.reshape(tokens, width)


def shards(
    hidden_in,
    queries,
    suffix_kv,
    prefix_kv,
    hyp_prefix,
    suffix_len,
    prefix_len,
    w_out,
    gain_attn,
    gain_pre,
    w_gate,
    w_up,
    w_down,
):
    n_ctx = lax.axis_size("ctx")
    resid = attention(
        n_ctx, queries, suffix_kv, prefix_kv, hyp_prefix, suffix_len, prefix_len, w_out, hidden_in, gain_attn
    )
    resid_f = resid.astype(jnp.float32)
    scale_b = lax.rsqrt(jnp.mean(resid_f * resid_f, -1, keepdims=True) + eps)
    normed = (resid_f * scale_b * gain_pre).astype(jnp.bfloat16)
    piece = lax.all_gather(normed, "req", axis=0, tiled=True)
    gate = jnp.dot(piece, w_gate, preferred_element_type=jnp.float32)
    upper = jnp.dot(piece, w_up, preferred_element_type=jnp.float32)
    hidden = (jax.nn.gelu(gate, approximate=True) * upper).astype(jnp.bfloat16)
    partial_out = jnp.dot(
        lax.all_gather(hidden, "ctx", axis=1, tiled=True),
        w_down,
        preferred_element_type=jnp.float32,
    )
    ffn_out = lax.psum_scatter(partial_out, "req", scatter_dimension=0, tiled=True).astype(
        jnp.bfloat16
    )
    return (resid, ffn_out)


def solution(mesh):
    placed = (
        P("req", None),
        P("req", None),
        P(None, "req", None),
        P(None, "req", "ctx", None),
        P("req"),
        P("req"),
        P("req"),
        P("ctx", None),
        P(),
        P(),
        P(None, ("req", "ctx")),
        P(None, ("req", "ctx")),
        P("req", "ctx"),
    )
    return jax.shard_map(
        shards,
        mesh=mesh,
        in_specs=placed,
        out_specs=(P("req", None), P("req", "ctx")),
        check_vma=False,
    )
```

```python
import functools

import jax
import jax.numpy as jnp
from jax import lax
from jax.experimental import pallas as pl
from jax.experimental.pallas import tpu as pltpu
from jax.sharding import PartitionSpec as P

HEADS = 32
KV_HEADS = 16
HEAD = 128

softcap = 50.0
query_scale = 144.0 ** (-0.5)
eps = 1e-06

NT = (((1,), (1,)), ((), ()))
NN = (((1,), (0,)), ((), ()))


def slab_of(ctx):
    return lax.rem(ctx, 2) * 8 + ctx // 2


def weights_of(scores):
    return jnp.exp(softcap * jnp.tanh(scores * (query_scale / softcap)))


def attention_kernel(
    n,
    queries,
    suffix_kv,
    prefix_kv,
    hyp_prefix,
    suffix_len,
    prefix_len,
    w_out,
    hidden_in,
    gain_attn,
    gain_pre,
    resid_out,
    normed_out,
    mask,
    part_send,
    part_recv,
    proj_send,
    proj_recv,
    part_ssem,
    part_rsem,
    proj_ssem,
    proj_rsem,
    resid_ssem,
    resid_rsem,
):
    me = lax.axis_index("ctx")
    req = lax.axis_index("req")
    tokens = queries.shape[0]
    prefixes, block = prefix_kv.shape[1], prefix_kv.shape[2]
    group = HEADS // KV_HEADS
    rows = group * tokens
    hyps = hyp_prefix.shape[0]
    suf = tokens // hyps
    slab = tokens // n
    width = w_out.shape[1]

    barrier = pltpu.get_barrier_semaphore()

    def greet(s, _):
        pl.semaphore_signal(
            barrier, inc=1, device_id={"ctx": lax.rem(me + s, n)}, device_id_type=pl.DeviceIdType.MESH
        )
        return 0

    lax.fori_loop(1, n, greet, 0)

    row = lax.broadcasted_iota(jnp.int32, (rows, prefixes * block), 0)
    col = lax.broadcasted_iota(jnp.int32, (rows, prefixes * block), 1)
    hyp_of_row = lax.rem(row, tokens) // suf
    row_pid = jnp.zeros_like(row)
    for h in range(hyps):
        row_pid = jnp.where(hyp_of_row == h, hyp_prefix[h] - req * prefixes, row_pid)
    col_pid = col // block
    col_len = jnp.zeros_like(row)
    for p in range(prefixes):
        col_len = jnp.where(col_pid == p, prefix_len[p], col_len)
    ok = (row_pid == col_pid) & (me * block + lax.rem(col, block) < col_len)
    mask[...] = jnp.where(ok, 1.0, 0.0)
    eye = lax.broadcasted_iota(jnp.int32, (rows, rows), 0) == lax.broadcasted_iota(jnp.int32, (rows, rows), 1)

    pl.semaphore_wait(barrier, n - 1)

    def query_rows(head):
        both = queries[:, pl.ds(pl.multiple_of(head * (group * HEAD), group * HEAD), group * HEAD)]
        return jnp.concatenate([both[:, g * HEAD : (g + 1) * HEAD] for g in range(group)], 0)

    def partial_of(head):
        lanes = pl.ds(pl.multiple_of(head * HEAD, HEAD), HEAD)
        query = query_rows(head)
        keys = prefix_kv[0, :, :, lanes].reshape(prefixes * block, HEAD)
        vals = prefix_kv[1, :, :, lanes].reshape(prefixes * block, HEAD)
        scores = lax.dot_general(query, keys, NT, preferred_element_type=jnp.float32)
        weights = jnp.where(mask[...] > 0.5, weights_of(scores), 0.0)
        summed = jnp.dot(weights.astype(jnp.bfloat16), vals, preferred_element_type=jnp.float32)
        return summed, jnp.sum(weights, 1, keepdims=True)

    def store_partial(ref, summed, total):
        ref[0:rows, :] = summed.astype(jnp.bfloat16)
        flat = jnp.sum(jnp.where(eye, total, 0.0), 0, keepdims=True)
        high = flat.astype(jnp.bfloat16).astype(jnp.float32)
        low = flat - high
        place = lax.broadcasted_iota(jnp.int32, (16, rows), 0)
        ref[rows : rows + 16, :] = jnp.where(
            place == 0, high, jnp.where(place == 1, low, 0.0)
        ).astype(jnp.bfloat16)

    def part_copy(peer):
        return pltpu.make_async_remote_copy(
            src_ref=part_send.at[peer],
            dst_ref=part_recv.at[me],
            send_sem=part_ssem.at[peer],
            recv_sem=part_rsem.at[me],
            device_id={"ctx": peer},
            device_id_type=pl.DeviceIdType.MESH,
        )

    def send_part(s, _):
        peer = lax.rem(me + s, n)
        summed, total = partial_of(peer)
        store_partial(part_send.at[peer], summed, total)
        part_copy(peer).start()
        return 0

    lax.fori_loop(1, n, send_part, 0, unroll=3)

    summed, total = partial_of(me)
    own = pl.ds(pl.multiple_of(me * HEAD, HEAD), HEAD)
    suf_row = lax.rem(lax.broadcasted_iota(jnp.int32, (rows, tokens), 0), tokens)
    suf_col = lax.broadcasted_iota(jnp.int32, (rows, tokens), 1)
    row_hyp, col_hyp = suf_row // suf, suf_col // suf
    place = suf_col - col_hyp * suf
    length = jnp.zeros_like(suf_row)
    for h in range(hyps):
        length = jnp.where(col_hyp == h, suffix_len[h], length)
    usable = (row_hyp == col_hyp) & (suf_col <= suf_row) & (place < length)
    scores = lax.dot_general(query_rows(me), suffix_kv[0, :, own], NT, preferred_element_type=jnp.float32)
    weights = jnp.where(usable, weights_of(scores), 0.0)
    summed += jnp.dot(weights.astype(jnp.bfloat16), suffix_kv[1, :, own], preferred_element_type=jnp.float32)
    total += jnp.sum(weights, 1, keepdims=True)

    def add_part(s, carry):
        summed, flat = carry
        peer = lax.rem(me + n - s, n)
        part = part_recv.at[peer]
        pltpu.make_async_remote_copy(
            src_ref=part_send.at[peer],
            dst_ref=part,
            send_sem=part_ssem.at[peer],
            recv_sem=part_rsem.at[peer],
            device_id={"ctx": peer},
            device_id_type=pl.DeviceIdType.MESH,
        ).wait_recv()
        summed = summed + part[0:rows, :].astype(jnp.float32)
        flat = flat + part[rows : rows + 16, :].astype(jnp.float32)
        return summed, flat

    summed, flat = lax.fori_loop(1, n, add_part, (summed, jnp.zeros((16, rows), jnp.float32)))
    flat = jnp.sum(flat, 0, keepdims=True)
    total += jnp.sum(jnp.where(eye, flat, 0.0), 1, keepdims=True)
    attn = (summed / total).astype(jnp.bfloat16)
    attn = jnp.concatenate([attn[g * tokens : (g + 1) * tokens] for g in range(group)], 1)

    step = 512
    for c in range(0, width, step):
        term = jnp.dot(attn, w_out[:, c : c + step], preferred_element_type=jnp.float32)
        for i in range(n):
            proj_send[i, :, c : c + step] = term[i * slab : (i + 1) * slab].astype(jnp.bfloat16)

    def proj_copy(peer, slot):
        return pltpu.make_async_remote_copy(
            src_ref=proj_send.at[slab_of(peer)],
            dst_ref=proj_recv.at[slot],
            send_sem=proj_ssem.at[peer],
            recv_sem=proj_rsem.at[slot],
            device_id={"ctx": peer},
            device_id_type=pl.DeviceIdType.MESH,
        )

    def send_proj(s, _):
        proj_copy(lax.rem(me + s, n), me).start()
        return 0

    lax.fori_loop(1, n, send_proj, 0)

    place = slab_of(me)
    around = hidden_in[pl.ds(pl.multiple_of(place * slab // 16 * 16, 16), 16), :].astype(jnp.float32)
    mine = jnp.zeros((slab, width), jnp.float32)
    for g in range(16 // slab):
        mine = jnp.where(lax.rem(place, 16 // slab) == g, around[g * slab : (g + 1) * slab], mine)

    def add_proj(s, proj):
        peer = lax.rem(me + n - s, n)
        proj_copy(peer, peer).wait_recv()
        return proj + proj_recv[peer].astype(jnp.float32)

    proj = lax.fori_loop(1, n, add_proj, proj_send[place].astype(jnp.float32))
    scale_a = lax.rsqrt(jnp.mean(proj * proj, 1, keepdims=True) + eps)
    resid = (mine + gain_attn[...] * proj * scale_a).astype(jnp.bfloat16)
    resid_out[place] = resid
    resid = resid.astype(jnp.float32)
    scale_b = lax.rsqrt(jnp.mean(resid * resid, 1, keepdims=True) + eps)
    normed = (resid * scale_b * gain_pre[...]).astype(jnp.bfloat16)
    for half in range(2):
        normed_out[half] = normed[:, half * (width // 2) : (half + 1) * (width // 2)]

    def resid_copy(peer, slot):
        slot = slab_of(slot)
        return pltpu.make_async_remote_copy(
            src_ref=resid_out.at[slot],
            dst_ref=resid_out.at[slot],
            send_sem=resid_ssem.at[peer],
            recv_sem=resid_rsem.at[slot],
            device_id={"ctx": peer},
            device_id_type=pl.DeviceIdType.MESH,
        )

    def send_resid(s, _):
        resid_copy(lax.rem(me + s, n), me).start()
        return 0

    lax.fori_loop(1, n, send_resid, 0)

    def finish(s, _):
        peer = lax.rem(me + s, n)
        resid_copy(peer, peer).wait_recv()
        part_copy(peer).wait_send()
        proj_copy(peer, me).wait_send()
        resid_copy(peer, me).wait_send()
        return 0

    lax.fori_loop(1, n, finish, 0)


def attention(n, queries, suffix_kv, prefix_kv, hyp_prefix, suffix_len, prefix_len, w_out, hidden_in, gain_attn, gain_pre):
    tokens, width = hidden_in.shape
    rows = HEADS // KV_HEADS * tokens
    slab = tokens // n
    positions = prefix_kv.shape[1] * prefix_kv.shape[2]
    vmem = pl.BlockSpec(memory_space=pltpu.VMEM)
    smem = pl.BlockSpec(memory_space=pltpu.SMEM)
    dma = pltpu.SemaphoreType.DMA((n,))
    resid, normed = pl.pallas_call(
        functools.partial(attention_kernel, n),
        out_shape=(
            jax.ShapeDtypeStruct((n, slab, width), jnp.bfloat16),
            jax.ShapeDtypeStruct((2, slab, width // 2), jnp.bfloat16),
        ),
        in_specs=[vmem, vmem, vmem, smem, smem, smem, vmem, vmem, vmem, vmem],
        out_specs=(vmem, vmem),
        scratch_shapes=[
            pltpu.VMEM((rows, positions), jnp.float32),
            pltpu.VMEM((n, rows + 16, HEAD), jnp.bfloat16),
            pltpu.VMEM((n, rows + 16, HEAD), jnp.bfloat16),
            pltpu.VMEM((n, slab, width), jnp.bfloat16),
            pltpu.VMEM((n, slab, width), jnp.bfloat16),
            dma,
            dma,
            dma,
            dma,
            dma,
            dma,
        ],
        compiler_params=pltpu.CompilerParams(
            collective_id=0, has_side_effects=True, vmem_limit_bytes=40 * 2**20
        ),
        cost_estimate=pl.CostEstimate(flops=10**9, bytes_accessed=10**7, transcendentals=10**6),
        name="attention_projection",
    )(
        queries,
        suffix_kv,
        prefix_kv,
        hyp_prefix,
        suffix_len,
        prefix_len,
        w_out,
        hidden_in,
        gain_attn.reshape(1, -1),
        gain_pre.reshape(1, -1),
    )
    return resid.reshape(tokens, width), normed


ARRIVALS = (
    (((0, 1), (0, 1)), ((-1, 0), (-1, 0)), ((0, -1), (0, -1)), ((1, 0), (1, 0))),
    (((1, 1), (1, 0)), ((-1, 1), (0, 1)), ((-1, -1), (-1, 0)), ((1, -1), (0, -1))),
    (((2, 0), (1, 0)), ((0, 2), (0, 1)), ((2, -1), (-1, 0)), ((1, 2), (0, -1))),
    (((2, 1), (1, 0)), ((-1, 2), (0, 1)), ((2, 2), (0, -1))),
)
OFFSETS = ((0, 0),) + tuple(offset for step in ARRIVALS for offset, _ in step)
SLOT = {(dx % 4, dy % 4): i for i, (dx, dy) in enumerate(OFFSETS)}
CHUNKS = 4


def ffn_kernel(
    normed,
    w_gate,
    w_up,
    w_down,
    out,
    gate_raw,
    up_raw,
    down_raw,
    down_other,
    w_own,
    w_send,
    slabs,
    block,
    tok,
    sib_send,
    sib_recv,
    hid,
    rs_send,
    rs_recv,
    load_sem,
    w_sem,
    slab_ssem,
    slab_rsem,
    tok_ssem,
    tok_rsem,
    sib_ssem,
    sib_rsem,
    hid_ssem,
    hid_rsem,
    rs_ssem,
    rs_rsem,
):
    ctx, req = lax.axis_index("ctx"), lax.axis_index("req")
    z, y_lo = ctx // 2, lax.rem(ctx, 2)
    x, y_hi, core = req // 4, lax.rem(req // 2, 2), lax.rem(req, 2)
    y = y_hi * 2 + y_lo
    nz = 8
    half = tok.shape[2]
    units = w_gate.shape[1]
    blocks = 16 // CHUNKS
    rows = tok.shape[1]
    chunk = blocks * rows
    plane = req * 2 + y_lo
    mesh = pl.DeviceIdType.MESH

    def chip(dx, dy):
        there_y = lax.rem(y + dy + 4, 4)
        return z * 2 + lax.rem(there_y, 2), lax.rem(x + dx + 4, 4) * 4 + there_y // 2 * 2

    def along_z(dz):
        return lax.rem(z + dz + nz, nz)

    loads = [
        pltpu.make_async_copy(src, dst, load_sem.at[i])
        for i, (src, dst) in enumerate(((w_gate, gate_raw), (w_up, up_raw), (w_down, down_raw)))
    ]
    for load in loads:
        load.start()

    barrier = pltpu.get_barrier_semaphore()

    def greet_plane(s, _):
        there = lax.rem(plane + s, 32)
        pl.semaphore_signal(
            barrier, inc=1, device_id={"ctx": z * 2 + lax.rem(there, 2), "req": there // 2}, device_id_type=mesh
        )
        return 0

    def greet_z(s, _):
        for c in range(2):
            pl.semaphore_signal(
                barrier, inc=1, device_id={"ctx": along_z(s) * 2 + y_lo, "req": req - core + c}, device_id_type=mesh
            )
        return 0

    lax.fori_loop(1, 32, greet_plane, 0)
    lax.fori_loop(1, nz, greet_z, 0)
    pl.semaphore_wait(barrier, 31 + 2 * (nz - 1))

    def slab_copy(to_z, to_core, from_z, from_core):
        return pltpu.make_async_remote_copy(
            src_ref=normed.at[to_core],
            dst_ref=slabs.at[from_core, from_z],
            send_sem=slab_ssem.at[to_core, to_z],
            recv_sem=slab_rsem.at[from_core, from_z],
            device_id={"ctx": to_z * 2 + y_lo, "req": req - core + to_core},
            device_id_type=mesh,
        )

    slab_copy(z, 1 - core, z, core).start()

    def send_slab(s, _):
        slab_copy(along_z(s), core, z, core).start()
        slab_copy(along_z(s), 1 - core, z, core).start()
        return 0

    lax.fori_loop(1, nz, send_slab, 0)
    slabs[core, z] = normed[core]

    loads[0].wait()
    loads[1].wait()
    eye = (
        lax.broadcasted_iota(jnp.int32, (units, units), 0) == lax.broadcasted_iota(jnp.int32, (units, units), 1)
    ).astype(jnp.bfloat16)
    piece = half // 2

    def transpose_to(dst, which):
        for i, raw in enumerate((gate_raw, up_raw)):
            for k in range(0, half, piece):
                part = raw[pl.ds(pl.multiple_of(which * half + k, piece), piece), :]
                dst[i * units : (i + 1) * units, k : k + piece] = lax.dot_general(
                    eye, part, NT, preferred_element_type=jnp.float32
                ).astype(jnp.bfloat16)

    transpose_to(w_send, 1 - core)
    w_copy = pltpu.make_async_remote_copy(
        src_ref=w_send,
        dst_ref=w_own.at[pl.ds(2 * units, 2 * units), :],
        send_sem=w_sem.at[0],
        recv_sem=w_sem.at[1],
        device_id={"req": req + 1 - 2 * core},
        device_id_type=mesh,
    )
    w_copy.start()
    transpose_to(w_own, core)
    loads[2].wait()
    down_copy = pltpu.make_async_remote_copy(
        src_ref=down_raw.at[:, 1 - y_lo],
        dst_ref=down_other,
        send_sem=w_sem.at[2],
        recv_sem=w_sem.at[3],
        device_id={"ctx": ctx + 1 - 2 * y_lo},
        device_id_type=mesh,
    )
    down_copy.start()

    slab_copy(z, 1 - core, z, 1 - core).wait_recv()

    def wait_slab(s, _):
        slab_copy(along_z(s), core, along_z(s), core).wait_recv()
        slab_copy(along_z(s), core, along_z(s), 1 - core).wait_recv()
        return 0

    lax.fori_loop(1, nz, wait_slab, 0)
    for c in range(2):
        for s in range(nz):
            first = (c * nz + s) * 4
            block[first : first + 4, :] = slabs[c, s].astype(jnp.float32)
    tok[0] = block[...].astype(jnp.bfloat16)

    def tok_copy(offset, link):
        source = SLOT[(offset[0] - link[0]) % 4, (offset[1] - link[1]) % 4]
        slot = SLOT[offset[0] % 4, offset[1] % 4]
        there_ctx, there_req = chip(-link[0], -link[1])
        return pltpu.make_async_remote_copy(
            src_ref=tok.at[source],
            dst_ref=tok.at[slot],
            send_sem=tok_ssem.at[slot],
            recv_sem=tok_rsem.at[slot],
            device_id={"ctx": there_ctx, "req": there_req + core},
            device_id_type=mesh,
        )

    for offset, link in ARRIVALS[0]:
        tok_copy(offset, link).start()

    def token_step(step):
        for offset, link in ARRIVALS[step]:
            tok_copy(offset, link).wait_recv()
            if step + 1 < len(ARRIVALS):
                for later, by in ARRIVALS[step + 1]:
                    if ((later[0] - by[0] - offset[0]) % 4, (later[1] - by[1] - offset[1]) % 4) == (0, 0):
                        tok_copy(later, by).start()
        if step + 1 < len(ARRIVALS):
            for later, by in ARRIVALS[step + 1]:
                source = SLOT[(later[0] - by[0]) % 4, (later[1] - by[1]) % 4]
                if source <= 4 * step:
                    tok_copy(later, by).start()

    def sib_copy(g):
        return pltpu.make_async_remote_copy(
            src_ref=sib_send.at[g],
            dst_ref=sib_recv.at[g],
            send_sem=sib_ssem.at[g],
            recv_sem=sib_rsem.at[g],
            device_id={"req": req + 1 - 2 * core},
            device_id_type=mesh,
        )

    own_part = []

    def gate_up(g):
        tokens = tok[g * blocks : (g + 1) * blocks].reshape(chunk, half)
        sib_send[g] = lax.dot_general(w_own[2 * units :, :], tokens, NT, preferred_element_type=jnp.float32)
        sib_copy(g).start()
        own_part.append(lax.dot_general(w_own[: 2 * units, :], tokens, NT, preferred_element_type=jnp.float32))

    major = 1 - 2 * core

    def hid_copy(g, hop, way):
        toward = major if way == 0 else -major
        source = along_z(-toward * (hop - 1))
        return pltpu.make_async_remote_copy(
            src_ref=hid.at[g, source],
            dst_ref=hid.at[g, source],
            send_sem=hid_ssem.at[g, hop - 1, way],
            recv_sem=hid_rsem.at[g, source],
            device_id={"ctx": along_z(toward) * 2 + y_lo},
            device_id_type=mesh,
        )

    def hid_wait(g, hop, way):
        toward = major if way == 0 else -major
        source = along_z(-toward * hop)
        pltpu.make_async_remote_copy(
            src_ref=hid.at[g, source],
            dst_ref=hid.at[g, source],
            send_sem=hid_ssem.at[g, hop - 1, way],
            recv_sem=hid_rsem.at[g, source],
            device_id={"ctx": along_z(-toward) * 2 + y_lo},
            device_id_type=mesh,
        ).wait_recv()

    hops = (nz // 2, (nz - 1) // 2)

    def hidden(g):
        sib_copy(g).wait_recv()
        both = own_part[g] + sib_recv[g]
        act = jax.nn.gelu(both[:units], approximate=True) * both[units:]
        hid[g, z] = act.astype(jnp.bfloat16)
        for way in range(2):
            hid_copy(g, 1, way).start()

    def hop(g, k):
        for way in range(2):
            if k - 1 <= hops[way]:
                hid_wait(g, k - 1, way)
                if k <= hops[way]:
                    hid_copy(g, k, way).start()

    def rs_copy(g, i, side, there_ctx, there_req, there_lo):
        return pltpu.make_async_remote_copy(
            src_ref=rs_send.at[g, side, pl.ds(i * 32, 32), :],
            dst_ref=rs_recv.at[plane, pl.ds(pl.multiple_of(there_lo * 32, 32), 32), :],
            send_sem=rs_ssem.at[g, i, side],
            recv_sem=rs_rsem.at[plane],
            device_id={"ctx": there_ctx, "req": there_req},
            device_id_type=mesh,
        )

    def each_term(g, act):
        for b in range(blocks):
            dx, dy = OFFSETS[g * blocks + b]
            block_ctx, first_req = chip(dx, dy)
            lo = lax.rem(block_ctx, 2)
            for c in range(2):
                for side in range(2):
                    to_ctx = ctx if side == 0 else ctx + 1 - 2 * y_lo
                    mine = (to_ctx == ctx) & (first_req + c == req)
                    possible = side == 0 and dx == 0 and dy in (0, 1, -1)
                    act(g, b * 2 + c, side, to_ctx, first_req + c, lo, mine if possible else None)

    def send_term(g, i, side, to_ctx, to_req, lo, mine):
        if mine is None:
            rs_copy(g, i, side, to_ctx, to_req, lo).start()
            return

        @pl.when(mine)
        def _():
            rs_recv[plane, pl.ds(pl.multiple_of(lo * 32, 32), 32), :] = rs_send[g, side, pl.ds(i * 32, 32), :]

        @pl.when(jnp.logical_not(mine))
        def _():
            rs_copy(g, i, side, to_ctx, to_req, lo).start()

    def wait_term(g, i, side, to_ctx, to_req, lo, mine):
        if mine is None:
            rs_copy(g, i, side, to_ctx, to_req, lo).wait_send()
            return

        @pl.when(jnp.logical_not(mine))
        def _():
            rs_copy(g, i, side, to_ctx, to_req, lo).wait_send()

    def down(g):
        for way in range(2):
            if way == 0 or hops[0] == hops[1]:
                hid_wait(g, hops[way], way)
        act = hid[g].reshape(nz * units, chunk).T
        for side in range(2):
            matrix = (down_raw[:, y_lo] if side == 0 else down_other[...]).reshape(nz * units, -1)
            rs_send[g, side] = jnp.dot(act, matrix, preferred_element_type=jnp.float32).astype(jnp.bfloat16)
        each_term(g, send_term)

    token_step(0)
    w_copy.wait()
    gate_up(0)
    hidden(0)
    hop(0, 2)
    token_step(1)
    gate_up(1)
    hop(0, 3)
    hidden(1)
    hop(0, 4)
    hop(1, 2)
    token_step(2)
    gate_up(2)
    hop(1, 3)
    hidden(2)
    down_copy.wait()
    down(0)
    hop(1, 4)
    hop(2, 2)
    token_step(3)
    gate_up(3)
    hop(2, 3)
    hidden(3)
    down(1)
    hop(2, 4)
    hop(3, 2)
    down(2)
    hop(3, 3)
    hop(3, 4)
    down(3)

    def add_terms(s, total):
        there = lax.rem(plane + s, 32)
        pltpu.make_async_remote_copy(
            src_ref=rs_recv.at[there],
            dst_ref=rs_recv.at[there],
            send_sem=rs_ssem.at[0, 0, 0],
            recv_sem=rs_rsem.at[there],
            device_id={"ctx": z * 2 + lax.rem(there, 2), "req": there // 2},
            device_id_type=mesh,
        ).wait_recv()
        return total + rs_recv[there].astype(jnp.float32)

    total = lax.fori_loop(1, 32, add_terms, rs_recv[plane].astype(jnp.float32))
    out[...] = total.astype(jnp.bfloat16)

    slab_copy(z, 1 - core, z, core).wait_send()

    def wait_sends(s, _):
        slab_copy(along_z(s), core, z, core).wait_send()
        slab_copy(along_z(s), 1 - core, z, core).wait_send()
        return 0

    lax.fori_loop(1, nz, wait_sends, 0)
    for step in ARRIVALS:
        for offset, link in step:
            tok_copy(offset, link).wait_send()
    for g in range(CHUNKS):
        sib_copy(g).wait_send()
        for way in range(2):
            for k in range(hops[way]):
                hid_copy(g, k + 1, way).wait_send()
        each_term(g, wait_term)


def ffn(normed, w_gate, w_up, w_down):
    half = normed.shape[2]
    units = w_gate.shape[1]
    columns = w_down.shape[1]
    vmem = pl.BlockSpec(memory_space=pltpu.VMEM)
    hbm = pl.BlockSpec(memory_space=pl.ANY)
    dma = pltpu.SemaphoreType.DMA
    bf16 = jnp.bfloat16
    chunk = 1024 // CHUNKS
    return pl.pallas_call(
        ffn_kernel,
        out_shape=jax.ShapeDtypeStruct((64, columns), bf16),
        in_specs=[vmem, hbm, hbm, hbm],
        out_specs=vmem,
        scratch_shapes=[
            pltpu.VMEM(w_gate.shape, bf16),
            pltpu.VMEM(w_up.shape, bf16),
            pltpu.VMEM((8, 2, units, columns), bf16),
            pltpu.VMEM((8, units, columns), bf16),
            pltpu.VMEM((4 * units, half), bf16),
            pltpu.VMEM((2 * units, half), bf16),
            pltpu.VMEM((2, 8, 4, half), bf16),
            pltpu.VMEM((64, half), jnp.float32),
            pltpu.VMEM((16, 64, half), bf16),
            pltpu.VMEM((CHUNKS, 2 * units, chunk), jnp.float32),
            pltpu.VMEM((CHUNKS, 2 * units, chunk), jnp.float32),
            pltpu.VMEM((CHUNKS, 8, units, chunk), bf16),
            pltpu.VMEM((CHUNKS, 2, chunk, columns), bf16),
            pltpu.VMEM((32, 64, columns), bf16),
            dma((3,)),
            dma((4,)),
            dma((2, 8)),
            dma((2, 8)),
            dma((16,)),
            dma((16,)),
            dma((CHUNKS,)),
            dma((CHUNKS,)),
            dma((CHUNKS, 4, 2)),
            dma((CHUNKS, 8)),
            dma((CHUNKS, 8, 2)),
            dma((32,)),
        ],
        compiler_params=pltpu.CompilerParams(
            collective_id=1, has_side_effects=True, vmem_limit_bytes=56 * 2**20
        ),
        cost_estimate=pl.CostEstimate(flops=4 * 10**9, bytes_accessed=10**7, transcendentals=10**6),
        name="feed_forward",
    )(normed, w_gate, w_up, w_down.reshape(8, 2, units, columns))


def shards(
    hidden_in,
    queries,
    suffix_kv,
    prefix_kv,
    hyp_prefix,
    suffix_len,
    prefix_len,
    w_out,
    gain_attn,
    gain_pre,
    w_gate,
    w_up,
    w_down,
):
    n_ctx = lax.axis_size("ctx")
    resid, normed = attention(
        n_ctx, queries, suffix_kv, prefix_kv, hyp_prefix, suffix_len, prefix_len, w_out, hidden_in, gain_attn, gain_pre
    )
    return resid, ffn(normed, w_gate, w_up, w_down)


def solution(mesh):
    placed = (
        P("req", None),
        P("req", None),
        P(None, "req", None),
        P(None, "req", "ctx", None),
        P("req"),
        P("req"),
        P("req"),
        P("ctx", None),
        P(),
        P(),
        P(None, ("req", "ctx")),
        P(None, ("req", "ctx")),
        P("req", "ctx"),
    )
    return jax.shard_map(
        shards,
        mesh=mesh,
        in_specs=placed,
        out_specs=(P("req", None), P("req", "ctx")),
        check_vma=False,
    )
```

```python
import functools

import jax
import jax.numpy as jnp
from jax import lax
from jax.experimental import pallas as pl
from jax.experimental.pallas import tpu as pltpu
from jax.sharding import PartitionSpec as P

HEADS = 32
KV_HEADS = 16
HEAD = 128

softcap = 50.0
query_scale = 144.0 ** (-0.5)
eps = 1e-06

NT = (((1,), (1,)), ((), ()))
NN = (((1,), (0,)), ((), ()))


def slab_of(ctx):
    return lax.rem(ctx, 2) * 8 + ctx // 2


def weights_of(scores):
    return jnp.exp(softcap * jnp.tanh(scores * (query_scale / softcap)))


ARRIVALS = (
    (((0, 1), (0, 1)), ((-1, 0), (-1, 0)), ((0, -1), (0, -1)), ((1, 0), (1, 0))),
    (((1, 1), (1, 0)), ((-1, 1), (0, 1)), ((-1, -1), (-1, 0)), ((1, -1), (0, -1))),
    (((2, 0), (1, 0)), ((0, 2), (0, 1)), ((2, -1), (-1, 0)), ((1, 2), (0, -1))),
    (((2, 1), (1, 0)), ((-1, 2), (0, 1)), ((2, 2), (0, -1))),
)
OFFSETS = ((0, 0),) + tuple(offset for step in ARRIVALS for offset, _ in step)
SLOT = {(dx % 4, dy % 4): i for i, (dx, dy) in enumerate(OFFSETS)}
CHUNKS = 4


MESH = pl.DeviceIdType.MESH


def layer_kernel(
    queries_in,
    suffix_in,
    prefix_in,
    hyp_prefix,
    suffix_len,
    prefix_len,
    w_out_in,
    hidden_hbm,
    gain_attn_in,
    gain_pre_in,
    w_gate,
    w_up,
    w_down,
    resid_out,
    out,
    queries,
    suffix_kv,
    prefix_kv,
    w_out,
    hidden_in,
    gains,
    mask,
    part_send,
    part_recv,
    proj_send,
    proj_recv,
    normed,
    down_raw,
    down_rows,
    down_own,
    down_other,
    w_own,
    slabs,
    block,
    tok,
    sib_send,
    sib_recv,
    hid,
    rs_send,
    rs_recv,
    load_sem,
    part_ssem,
    part_rsem,
    proj_ssem,
    proj_rsem,
    resid_ssem,
    resid_rsem,
    w_ssem,
    w_rsem,
    slab_ssem,
    slab_rsem,
    tok_ssem,
    tok_rsem,
    sib_ssem,
    sib_rsem,
    hid_ssem,
    hid_rsem,
    rs_ssem,
    rs_rsem,
):
    ctx, req = lax.axis_index("ctx"), lax.axis_index("req")
    z, y_lo = ctx // 2, lax.rem(ctx, 2)
    x, y_hi, core = req // 4, lax.rem(req // 2, 2), lax.rem(req, 2)
    y = y_hi * 2 + y_lo
    plane = req * 2 + y_lo
    n = 16
    nz = 8
    tokens = queries.shape[0]
    prefixes, positions = prefix_kv.shape[1], prefix_kv.shape[2]
    group = HEADS // KV_HEADS
    rows = group * tokens
    hyps = hyp_prefix.shape[0]
    suf = tokens // hyps
    slab = tokens // n
    width = w_out.shape[1]
    half = width // 2
    units = w_gate.shape[0]
    blocks = 16 // CHUNKS
    chunk = blocks * tokens

    def chip(dx, dy):
        there_y = lax.rem(y + dy + 4, 4)
        return z * 2 + lax.rem(there_y, 2), lax.rem(x + dx + 4, 4) * 4 + there_y // 2 * 2

    def along_z(dz):
        return lax.rem(z + dz + nz, nz)

    def remote(src, dst, ssem, rsem, **where):
        return pltpu.make_async_remote_copy(
            src_ref=src, dst_ref=dst, send_sem=ssem, recv_sem=rsem, device_id=where, device_id_type=MESH
        )

    mine = pl.ds(pl.multiple_of(core * half, half), half)
    others = pl.ds(pl.multiple_of((1 - core) * half, half), half)
    gate_rows, up_rows = pl.ds(0, units), pl.ds(units, units)
    loads = [
        pltpu.make_async_copy(src, dst, load_sem.at[i])
        for i, (src, dst) in enumerate(
            (
                (queries_in, queries),
                (prefix_in, prefix_kv),
                (suffix_in, suffix_kv),
                (w_out_in, w_out),
                (hidden_hbm, hidden_in),
                (w_down, down_raw),
                (w_gate.at[:, mine], w_own.at[gate_rows, :]),
                (w_up.at[:, mine], w_own.at[up_rows, :]),
            )
        )
    ]
    for load in loads:
        load.start()

    barrier = pltpu.get_barrier_semaphore()

    def greet(there_ctx, there_req):
        pl.semaphore_signal(barrier, inc=1, device_id={"ctx": there_ctx, "req": there_req}, device_id_type=MESH)

    def greet_ctx(s, _):
        greet(lax.rem(ctx + s, n), req)
        return 0

    def greet_core(s, _):
        greet(along_z(s) * 2 + y_lo, req + 1 - 2 * core)
        return 0

    def greet_plane(s, _):
        there = lax.rem(plane + s, 32)
        there_ctx, there_req = z * 2 + lax.rem(there, 2), there // 2

        @pl.when(there_req != req)
        def _():
            greet(there_ctx, there_req)

        return 0

    lax.fori_loop(1, n, greet_ctx, 0)
    lax.fori_loop(1, nz, greet_core, 0)
    lax.fori_loop(1, 32, greet_plane, 0)

    row = lax.broadcasted_iota(jnp.int32, (rows, prefixes * positions), 0)
    col = lax.broadcasted_iota(jnp.int32, (rows, prefixes * positions), 1)
    hyp_of_row = lax.rem(row, tokens) // suf
    row_pid = jnp.zeros_like(row)
    for h in range(hyps):
        row_pid = jnp.where(hyp_of_row == h, hyp_prefix[h] - req * prefixes, row_pid)
    col_pid = col // positions
    col_len = jnp.zeros_like(row)
    for p in range(prefixes):
        col_len = jnp.where(col_pid == p, prefix_len[p], col_len)
    ok = (row_pid == col_pid) & (ctx * positions + lax.rem(col, positions) < col_len)
    mask[...] = jnp.where(ok, 1.0, 0.0)
    eye = lax.broadcasted_iota(jnp.int32, (rows, rows), 0) == lax.broadcasted_iota(jnp.int32, (rows, rows), 1)
    for i, gain in enumerate((gain_attn_in, gain_pre_in)):
        for k in range(width // 128):
            gains[i : i + 1, k * 128 : (k + 1) * 128] = gain[k : k + 1, :]

    loads[0].wait()
    loads[1].wait()
    pl.semaphore_wait(barrier, (n - 1) + (nz - 1) + 30)

    w_copies = [
        remote(
            src.at[:, others],
            w_own.at[pl.ds((2 + i) * units, units), :],
            w_ssem.at[i],
            w_rsem.at[i],
            req=req + 1 - 2 * core,
        )
        for i, src in enumerate((w_gate, w_up))
    ]
    for copy in w_copies:
        copy.start()

    def query_rows(head):
        both = queries[:, pl.ds(pl.multiple_of(head * (group * HEAD), group * HEAD), group * HEAD)]
        return jnp.concatenate([both[:, g * HEAD : (g + 1) * HEAD] for g in range(group)], 0)

    def partial_of(head):
        lanes = pl.ds(pl.multiple_of(head * HEAD, HEAD), HEAD)
        query = query_rows(head)
        keys = prefix_kv[0, :, :, lanes].reshape(prefixes * positions, HEAD)
        vals = prefix_kv[1, :, :, lanes].reshape(prefixes * positions, HEAD)
        scores = lax.dot_general(query, keys, NT, preferred_element_type=jnp.float32)
        weights = jnp.where(mask[...] > 0.5, weights_of(scores), 0.0)
        summed = jnp.dot(weights.astype(jnp.bfloat16), vals, preferred_element_type=jnp.float32)
        return summed, jnp.sum(weights, 1, keepdims=True)

    def store_partial(ref, summed, total):
        ref[0:rows, :] = summed.astype(jnp.bfloat16)
        flat = jnp.sum(jnp.where(eye, total, 0.0), 0, keepdims=True)
        high = flat.astype(jnp.bfloat16).astype(jnp.float32)
        low = flat - high
        place = lax.broadcasted_iota(jnp.int32, (16, rows), 0)
        ref[rows : rows + 16, :] = jnp.where(place == 0, high, jnp.where(place == 1, low, 0.0)).astype(
            jnp.bfloat16
        )

    def part_copy(peer, slot):
        return remote(part_send.at[peer], part_recv.at[slot], part_ssem.at[peer], part_rsem.at[slot], ctx=peer)

    at_once = 5

    def send_part(s, _):
        peers = [lax.rem(ctx + 1 + s * at_once + i, n) for i in range(at_once)]
        parts = [partial_of(peer) for peer in peers]
        for peer, part in zip(peers, parts):
            store_partial(part_send.at[peer], *part)
        for peer in peers:
            part_copy(peer, ctx).start()
        return 0

    lax.fori_loop(0, (n - 1) // at_once, send_part, 0)

    summed, total = partial_of(ctx)
    own = pl.ds(pl.multiple_of(ctx * HEAD, HEAD), HEAD)
    suf_row = lax.rem(lax.broadcasted_iota(jnp.int32, (rows, tokens), 0), tokens)
    suf_col = lax.broadcasted_iota(jnp.int32, (rows, tokens), 1)
    row_hyp, col_hyp = suf_row // suf, suf_col // suf
    length = jnp.zeros_like(suf_row)
    for h in range(hyps):
        length = jnp.where(col_hyp == h, suffix_len[h], length)
    usable = (row_hyp == col_hyp) & (suf_col <= suf_row) & (suf_col - col_hyp * suf < length)
    loads[2].wait()
    scores = lax.dot_general(query_rows(ctx), suffix_kv[0, :, own], NT, preferred_element_type=jnp.float32)
    weights = jnp.where(usable, weights_of(scores), 0.0)
    summed += jnp.dot(weights.astype(jnp.bfloat16), suffix_kv[1, :, own], preferred_element_type=jnp.float32)
    total += jnp.sum(weights, 1, keepdims=True)

    loads[5].wait()
    tile = 128
    unit = (
        lax.broadcasted_iota(jnp.int32, (tile, tile), 0) == lax.broadcasted_iota(jnp.int32, (tile, tile), 1)
    ).astype(jnp.bfloat16)
    for k in range(0, down_raw.shape[1], tile):
        down_rows[k : k + tile, :] = lax.dot_general(
            unit, down_raw[:, k : k + tile], NT, preferred_element_type=jnp.float32
        ).astype(jnp.bfloat16)
    down_copies = [
        remote(
            down_rows.at[pl.ds(pl.multiple_of((2 * s + 1 - y_lo) * units, units), units), :],
            down_other.at[pl.ds(s * units, units), :],
            w_ssem.at[2 + s],
            w_rsem.at[2 + s],
            ctx=ctx + 1 - 2 * y_lo,
        )
        for s in range(nz)
    ]
    for copy in down_copies:
        copy.start()
    for s in range(nz):
        down_own[s * units : (s + 1) * units, :] = down_rows[
            pl.ds(pl.multiple_of((2 * s + y_lo) * units, units), units), :
        ]

    def add_part(s, carry):
        summed, flat = carry
        peer = lax.rem(ctx + n - s, n)
        part_copy(peer, peer).wait_recv()
        part = part_recv.at[peer]
        return summed + part[0:rows, :].astype(jnp.float32), flat + part[rows : rows + 16, :].astype(jnp.float32)

    summed, flat = lax.fori_loop(1, n, add_part, (summed, jnp.zeros((16, rows), jnp.float32)))
    flat = jnp.sum(flat, 0, keepdims=True)
    total += jnp.sum(jnp.where(eye, flat, 0.0), 1, keepdims=True)
    attn = (summed / total).astype(jnp.bfloat16)
    attn = jnp.concatenate([attn[g * tokens : (g + 1) * tokens] for g in range(group)], 1)

    loads[3].wait()
    step = 512
    for c in range(0, width, step):
        term = jnp.dot(attn, w_out[:, c : c + step], preferred_element_type=jnp.float32)
        for i in range(n):
            proj_send[i, :, c : c + step] = term[i * slab : (i + 1) * slab].astype(jnp.bfloat16)

    def proj_copy(peer, slot):
        return remote(
            proj_send.at[slab_of(peer)], proj_recv.at[slot], proj_ssem.at[peer], proj_rsem.at[slot], ctx=peer
        )

    def send_proj(s, _):
        proj_copy(lax.rem(ctx + s, n), ctx).start()
        return 0

    lax.fori_loop(1, n, send_proj, 0)

    place = slab_of(ctx)
    loads[4].wait()
    around = hidden_in[pl.ds(pl.multiple_of(place * slab // 16 * 16, 16), 16), :].astype(jnp.float32)
    before = jnp.zeros((slab, width), jnp.float32)
    for g in range(16 // slab):
        before = jnp.where(lax.rem(place, 16 // slab) == g, around[g * slab : (g + 1) * slab], before)

    def add_proj(s, proj):
        peer = lax.rem(ctx + n - s, n)
        proj_copy(peer, peer).wait_recv()
        return proj + proj_recv[peer].astype(jnp.float32)

    proj = lax.fori_loop(1, n, add_proj, proj_send[place].astype(jnp.float32))
    scale_a = lax.rsqrt(jnp.mean(proj * proj, 1, keepdims=True) + eps)
    resid = (before + gains[0:1, :] * proj * scale_a).astype(jnp.bfloat16)
    resid_out[place] = resid
    resid = resid.astype(jnp.float32)
    scale_b = lax.rsqrt(jnp.mean(resid * resid, 1, keepdims=True) + eps)
    tokens_normed = (resid * scale_b * gains[1:2, :]).astype(jnp.bfloat16)
    for h in range(2):
        normed[h] = tokens_normed[:, h * half : (h + 1) * half]

    def slab_copy(to_z, to_core, from_z, from_core):
        return remote(
            normed.at[to_core],
            slabs.at[from_core, from_z],
            slab_ssem.at[to_core, to_z],
            slab_rsem.at[from_core, from_z],
            ctx=to_z * 2 + y_lo,
            req=req - core + to_core,
        )

    slab_copy(z, 1 - core, z, core).start()

    def send_slab(s, _):
        slab_copy(along_z(s), core, z, core).start()
        slab_copy(along_z(s), 1 - core, z, core).start()
        return 0

    lax.fori_loop(1, nz, send_slab, 0)
    slabs[core, z] = normed[core]
    slab_copy(z, 1 - core, z, 1 - core).wait_recv()

    def wait_slab(s, _):
        slab_copy(along_z(s), core, along_z(s), core).wait_recv()
        slab_copy(along_z(s), core, along_z(s), 1 - core).wait_recv()
        return 0

    lax.fori_loop(1, nz, wait_slab, 0)
    for c in range(2):
        for s in range(nz):
            first = (c * nz + s) * slab
            block[first : first + slab, :] = slabs[c, s].astype(jnp.float32)
    tok[0] = block[...].astype(jnp.bfloat16)

    def tok_copy(offset, link):
        source = SLOT[(offset[0] - link[0]) % 4, (offset[1] - link[1]) % 4]
        slot = SLOT[offset[0] % 4, offset[1] % 4]
        there_ctx, there_req = chip(-link[0], -link[1])
        return pltpu.make_async_remote_copy(
            src_ref=tok.at[source],
            dst_ref=tok.at[slot],
            send_sem=tok_ssem.at[slot],
            recv_sem=tok_rsem.at[slot],
            device_id={"ctx": there_ctx, "req": there_req + core},
            device_id_type=MESH,
        )

    for offset, link in ARRIVALS[0]:
        tok_copy(offset, link).start()

    def resid_copy(peer, which):
        which = slab_of(which)
        return remote(
            resid_out.at[which], resid_out.at[which], resid_ssem.at[peer], resid_rsem.at[which], ctx=peer
        )

    def send_resid(s, _):
        resid_copy(lax.rem(ctx + s, n), ctx).start()
        return 0

    lax.fori_loop(1, n, send_resid, 0)

    def token_step(step):
        for offset, link in ARRIVALS[step]:
            tok_copy(offset, link).wait_recv()
            if step + 1 < len(ARRIVALS):
                for later, by in ARRIVALS[step + 1]:
                    if ((later[0] - by[0] - offset[0]) % 4, (later[1] - by[1] - offset[1]) % 4) == (0, 0):
                        tok_copy(later, by).start()
        if step + 1 < len(ARRIVALS):
            for later, by in ARRIVALS[step + 1]:
                source = SLOT[(later[0] - by[0]) % 4, (later[1] - by[1]) % 4]
                if source <= 4 * step:
                    tok_copy(later, by).start()

    def sib_copy(g):
        return pltpu.make_async_remote_copy(
            src_ref=sib_send.at[g],
            dst_ref=sib_recv.at[g],
            send_sem=sib_ssem.at[g],
            recv_sem=sib_rsem.at[g],
            device_id={"req": req + 1 - 2 * core},
            device_id_type=MESH,
        )

    own_part = []

    def gate_up(g):
        tokens = tok[g * blocks : (g + 1) * blocks].reshape(chunk, half)
        sib_send[g] = lax.dot_general(w_own[2 * units :, :], tokens, NT, preferred_element_type=jnp.float32)
        sib_copy(g).start()
        own_part.append(lax.dot_general(w_own[: 2 * units, :], tokens, NT, preferred_element_type=jnp.float32))

    major = 1 - 2 * core

    def hid_copy(g, hop, way):
        toward = major if way == 0 else -major
        source = along_z(-toward * (hop - 1))
        return pltpu.make_async_remote_copy(
            src_ref=hid.at[g, source],
            dst_ref=hid.at[g, source],
            send_sem=hid_ssem.at[g, hop - 1, way],
            recv_sem=hid_rsem.at[g, source],
            device_id={"ctx": along_z(toward) * 2 + y_lo},
            device_id_type=MESH,
        )

    def hid_wait(g, hop, way):
        toward = major if way == 0 else -major
        source = along_z(-toward * hop)
        pltpu.make_async_remote_copy(
            src_ref=hid.at[g, source],
            dst_ref=hid.at[g, source],
            send_sem=hid_ssem.at[g, hop - 1, way],
            recv_sem=hid_rsem.at[g, source],
            device_id={"ctx": along_z(-toward) * 2 + y_lo},
            device_id_type=MESH,
        ).wait_recv()

    hops = (nz // 2, (nz - 1) // 2)

    def hidden(g):
        sib_copy(g).wait_recv()
        both = own_part[g] + sib_recv[g]
        act = jax.nn.gelu(both[:units], approximate=True) * both[units:]
        hid[g, z] = act.astype(jnp.bfloat16)
        for way in range(2):
            hid_copy(g, 1, way).start()

    def hop(g, k):
        for way in range(2):
            if k - 1 <= hops[way]:
                hid_wait(g, k - 1, way)
                if k <= hops[way]:
                    hid_copy(g, k, way).start()

    def rs_copy(g, i, side, there_ctx, there_req, there_lo):
        return pltpu.make_async_remote_copy(
            src_ref=rs_send.at[g, side, pl.ds(i * 32, 32), :],
            dst_ref=rs_recv.at[plane, pl.ds(pl.multiple_of(there_lo * 32, 32), 32), :],
            send_sem=rs_ssem.at[g, i, side],
            recv_sem=rs_rsem.at[plane],
            device_id={"ctx": there_ctx, "req": there_req},
            device_id_type=MESH,
        )

    def each_term(g, act):
        for b in range(blocks):
            dx, dy = OFFSETS[g * blocks + b]
            block_ctx, first_req = chip(dx, dy)
            lo = lax.rem(block_ctx, 2)
            for c in range(2):
                for side in range(2):
                    to_ctx = ctx if side == 0 else ctx + 1 - 2 * y_lo
                    mine = (to_ctx == ctx) & (first_req + c == req)
                    possible = side == 0 and dx == 0 and dy in (0, 1, -1)
                    act(g, b * 2 + c, side, to_ctx, first_req + c, lo, mine if possible else None)

    def send_term(g, i, side, to_ctx, to_req, lo, mine):
        if mine is None:
            rs_copy(g, i, side, to_ctx, to_req, lo).start()
            return

        @pl.when(mine)
        def _():
            rs_recv[plane, pl.ds(pl.multiple_of(lo * 32, 32), 32), :] = rs_send[g, side, pl.ds(i * 32, 32), :]

        @pl.when(jnp.logical_not(mine))
        def _():
            rs_copy(g, i, side, to_ctx, to_req, lo).start()

    def wait_term(g, i, side, to_ctx, to_req, lo, mine):
        if mine is None:
            rs_copy(g, i, side, to_ctx, to_req, lo).wait_send()
            return

        @pl.when(jnp.logical_not(mine))
        def _():
            rs_copy(g, i, side, to_ctx, to_req, lo).wait_send()

    def down(g):
        for way in range(2):
            if way == 0 or hops[0] == hops[1]:
                hid_wait(g, hops[way], way)
        act = hid[g].reshape(nz * units, chunk).T
        for side in range(2):
            matrix = down_own[...] if side == 0 else down_other[...]
            rs_send[g, side] = jnp.dot(act, matrix, preferred_element_type=jnp.float32).astype(jnp.bfloat16)
        each_term(g, send_term)

    token_step(0)
    for copy in w_copies:
        copy.wait()
    loads[6].wait()
    loads[7].wait()
    gate_up(0)
    hidden(0)
    hop(0, 2)
    token_step(1)
    gate_up(1)
    hop(0, 3)
    hidden(1)
    hop(0, 4)
    hop(1, 2)
    token_step(2)
    gate_up(2)
    hop(1, 3)
    hidden(2)
    for copy in down_copies:
        copy.wait()
    down(0)
    hop(1, 4)
    hop(2, 2)
    token_step(3)
    gate_up(3)
    hop(2, 3)
    hidden(3)
    down(1)
    hop(2, 4)
    hop(3, 2)
    down(2)
    hop(3, 3)
    hop(3, 4)
    down(3)

    def add_terms(s, total):
        there = lax.rem(plane + s, 32)
        pltpu.make_async_remote_copy(
            src_ref=rs_recv.at[there],
            dst_ref=rs_recv.at[there],
            send_sem=rs_ssem.at[0, 0, 0],
            recv_sem=rs_rsem.at[there],
            device_id={"ctx": z * 2 + lax.rem(there, 2), "req": there // 2},
            device_id_type=MESH,
        ).wait_recv()
        return total + rs_recv[there].astype(jnp.float32)

    total = lax.fori_loop(1, 32, add_terms, rs_recv[plane].astype(jnp.float32))
    out[...] = total.astype(jnp.bfloat16)

    slab_copy(z, 1 - core, z, core).wait_send()

    def wait_sends(s, _):
        slab_copy(along_z(s), core, z, core).wait_send()
        slab_copy(along_z(s), 1 - core, z, core).wait_send()
        return 0

    lax.fori_loop(1, nz, wait_sends, 0)

    def finish(s, _):
        peer = lax.rem(ctx + s, n)
        resid_copy(peer, peer).wait_recv()
        part_copy(peer, ctx).wait_send()
        proj_copy(peer, ctx).wait_send()
        resid_copy(peer, ctx).wait_send()
        return 0

    lax.fori_loop(1, n, finish, 0)
    for step in ARRIVALS:
        for offset, link in step:
            tok_copy(offset, link).wait_send()
    for g in range(CHUNKS):
        sib_copy(g).wait_send()
        for way in range(2):
            for k in range(hops[way]):
                hid_copy(g, k + 1, way).wait_send()
        each_term(g, wait_term)


def layer(
    hidden_in,
    queries,
    suffix_kv,
    prefix_kv,
    hyp_prefix,
    suffix_len,
    prefix_len,
    w_out,
    gain_attn,
    gain_pre,
    w_gate,
    w_up,
    w_down,
):
    n = 16
    tokens, width = hidden_in.shape
    half = width // 2
    rows = HEADS // KV_HEADS * tokens
    slab = tokens // n
    positions = prefix_kv.shape[1] * prefix_kv.shape[2]
    units = w_gate.shape[1]
    columns = w_down.shape[1]
    chunk = 16 // CHUNKS * tokens
    vmem = pl.BlockSpec(memory_space=pltpu.VMEM)
    smem = pl.BlockSpec(memory_space=pltpu.SMEM)
    hbm = pl.BlockSpec(memory_space=pl.ANY)
    dma = pltpu.SemaphoreType.DMA
    bf16 = jnp.bfloat16
    resid, out = pl.pallas_call(
        layer_kernel,
        out_shape=(
            jax.ShapeDtypeStruct((n, slab, width), bf16),
            jax.ShapeDtypeStruct((tokens, columns), bf16),
        ),
        in_specs=[hbm, hbm, hbm, smem, smem, smem, hbm, hbm, vmem, vmem, hbm, hbm, hbm],
        out_specs=(vmem, vmem),
        scratch_shapes=[
            pltpu.VMEM(queries.shape, bf16),
            pltpu.VMEM(suffix_kv.shape, bf16),
            pltpu.VMEM(prefix_kv.shape, bf16),
            pltpu.VMEM(w_out.shape, bf16),
            pltpu.VMEM(hidden_in.shape, bf16),
            pltpu.VMEM((2, width), jnp.float32),
            pltpu.VMEM((rows, positions), jnp.float32),
            pltpu.VMEM((n, rows + 16, HEAD), bf16),
            pltpu.VMEM((n, rows + 16, HEAD), bf16),
            pltpu.VMEM((n, slab, width), bf16),
            pltpu.VMEM((n, slab, width), bf16),
            pltpu.VMEM((2, slab, half), bf16),
            pltpu.VMEM((columns, n * units), bf16),
            pltpu.VMEM((n * units, columns), bf16),
            pltpu.VMEM((8 * units, columns), bf16),
            pltpu.VMEM((8 * units, columns), bf16),
            pltpu.VMEM((4 * units, half), bf16),
            pltpu.VMEM((2, 8, slab, half), bf16),
            pltpu.VMEM((tokens, half), jnp.float32),
            pltpu.VMEM((16, tokens, half), bf16),
            pltpu.VMEM((CHUNKS, 2 * units, chunk), jnp.float32),
            pltpu.VMEM((CHUNKS, 2 * units, chunk), jnp.float32),
            pltpu.VMEM((CHUNKS, 8, units, chunk), bf16),
            pltpu.VMEM((CHUNKS, 2, chunk, columns), bf16),
            pltpu.VMEM((32, tokens, columns), bf16),
            dma((8,)),
            dma((n,)),
            dma((n,)),
            dma((n,)),
            dma((n,)),
            dma((n,)),
            dma((n,)),
            dma((10,)),
            dma((10,)),
            dma((2, 8)),
            dma((2, 8)),
            dma((16,)),
            dma((16,)),
            dma((CHUNKS,)),
            dma((CHUNKS,)),
            dma((CHUNKS, 4, 2)),
            dma((CHUNKS, 8)),
            dma((CHUNKS, 8, 2)),
            dma((32,)),
        ],
        compiler_params=pltpu.CompilerParams(
            collective_id=0, has_side_effects=True, vmem_limit_bytes=60 * 2**20
        ),
        cost_estimate=pl.CostEstimate(flops=5 * 10**9, bytes_accessed=10**7, transcendentals=10**6),
        name="layer",
    )(
        queries,
        suffix_kv,
        prefix_kv,
        hyp_prefix,
        suffix_len,
        prefix_len,
        w_out,
        hidden_in,
        gain_attn.reshape(-1, 128),
        gain_pre.reshape(-1, 128),
        w_gate.T,
        w_up.T,
        w_down.T,
    )
    return resid.reshape(tokens, width), out


def solution(mesh):
    placed = (
        P("req", None),
        P("req", None),
        P(None, "req", None),
        P(None, "req", "ctx", None),
        P("req"),
        P("req"),
        P("req"),
        P("ctx", None),
        P(),
        P(),
        P(None, ("req", "ctx")),
        P(None, ("req", "ctx")),
        P("req", "ctx"),
    )
    return jax.shard_map(
        layer,
        mesh=mesh,
        in_specs=placed,
        out_specs=(P("req", None), P("req", "ctx")),
        check_vma=False,
    )
```

```python
import functools

import jax
import jax.numpy as jnp
from jax import lax
from jax.experimental import pallas as pl
from jax.experimental.pallas import tpu as pltpu
from jax.sharding import PartitionSpec as P

HEADS = 32
KV_HEADS = 16
HEAD = 128

softcap = 50.0
query_scale = 144.0 ** (-0.5)
eps = 1e-06

NT = (((1,), (1,)), ((), ()))
MESH = pl.DeviceIdType.MESH

ARRIVALS = (
    (((0, 1), (0, 1)), ((-1, 0), (-1, 0)), ((0, -1), (0, -1)), ((1, 0), (1, 0))),
    (((1, 1), (1, 0)), ((-1, 1), (0, 1)), ((-1, -1), (-1, 0)), ((1, -1), (0, -1))),
    (((2, 0), (1, 0)), ((0, 2), (0, 1)), ((2, -1), (-1, 0)), ((1, 2), (0, -1))),
    (((2, 1), (1, 0)), ((-1, 2), (0, 1)), ((2, 2), (0, -1))),
)
OFFSETS = ((0, 0),) + tuple(offset for step in ARRIVALS for offset, _ in step)
SLOT = {(dx % 4, dy % 4): i for i, (dx, dy) in enumerate(OFFSETS)}
CHUNKS = 4
FAR_FIRST = (4, 3, 5, 2, 6, 1, 7, 0)


def weights_of(scores):
    return jnp.exp(softcap * jnp.tanh(scores * (query_scale / softcap)))


def layer_kernel(
    queries_in,
    suffix_in,
    prefix_in,
    hyp_prefix,
    suffix_len,
    prefix_len,
    w_out_in,
    hidden_hbm,
    gain_attn_in,
    gain_pre_in,
    w_gate,
    w_up,
    w_down,
    resid_out,
    out,
    queries,
    suffix_kv,
    prefix_kv,
    w_out,
    hidden_in,
    gains,
    mask,
    party_send,
    party_recv,
    part_own,
    partz_send,
    partz_recv,
    proj_send,
    projy_recv,
    projz_send,
    projz_recv,
    slab_own,
    down_raw,
    down_rows,
    down_own,
    down_other,
    w_own,
    slabs,
    block,
    tok,
    sib_send,
    sib_recv,
    hid,
    ds_send,
    ds_recv,
    rs_send,
    rs_recv,
    load_sem,
    party_sem,
    partz_sem,
    projy_sem,
    projz_sem,
    resid_sem,
    w_sem,
    slab_ssem,
    slab_rsem,
    tok_sem,
    sib_sem,
    hid_ssem,
    hid_rsem,
    ds_sem,
    rs_ssem,
    rs_rsem,
):
    ctx, req = lax.axis_index("ctx"), lax.axis_index("req")
    z, y_lo = ctx // 2, lax.rem(ctx, 2)
    x, y_hi, core = req // 4, lax.rem(req // 2, 2), lax.rem(req, 2)
    y = y_hi * 2 + y_lo
    place = x * 4 + y
    n = 16
    nz = 8
    tokens = queries.shape[0]
    prefixes, positions = prefix_kv.shape[1], prefix_kv.shape[2]
    group = HEADS // KV_HEADS
    rows = group * tokens
    hyps = hyp_prefix.shape[0]
    suf = tokens // hyps
    slab = tokens // n
    width = w_out.shape[1]
    half = width // 2
    units = w_gate.shape[0]
    blocks = 16 // CHUNKS
    part = tokens // 2
    chunk = blocks * part
    partner = ctx + 1 - 2 * y_lo
    sibling = req + 1 - 2 * core

    def chip(dx, dy):
        there_y = lax.rem(y + dy + 4, 4)
        return z * 2 + lax.rem(there_y, 2), lax.rem(x + dx + 4, 4) * 4 + there_y // 2 * 2

    def along_z(dz):
        return lax.rem(z + dz + nz, nz)

    def remote(src, dst, ssem, rsem, **where):
        return pltpu.make_async_remote_copy(
            src_ref=src, dst_ref=dst, send_sem=ssem, recv_sem=rsem, device_id=where, device_id_type=MESH
        )

    mine = pl.ds(pl.multiple_of(core * half, half), half)
    others = pl.ds(pl.multiple_of((1 - core) * half, half), half)
    loads = [
        pltpu.make_async_copy(src, dst, load_sem.at[i])
        for i, (src, dst) in enumerate(
            (
                (queries_in, queries),
                (prefix_in, prefix_kv),
                (suffix_in, suffix_kv),
                (w_out_in, w_out),
                (hidden_hbm, hidden_in),
                (w_down, down_raw),
                (w_gate.at[:, mine], w_own.at[pl.ds(0, units), :]),
                (w_up.at[:, mine], w_own.at[pl.ds(units, units), :]),
            )
        )
    ]
    for load in loads:
        load.start()

    barrier = pltpu.get_barrier_semaphore()

    def greet(there_ctx, there_req):
        pl.semaphore_signal(barrier, inc=1, device_id={"ctx": there_ctx, "req": there_req}, device_id_type=MESH)

    def greet_ctx(s, _):
        greet(lax.rem(ctx + s, n), req)
        return 0

    def greet_core(s, _):
        greet(along_z(s) * 2 + y_lo, sibling)
        return 0

    def greet_plane(s, _):
        there = lax.rem(place + s, 16)
        there_ctx, there_req = z * 2 + lax.rem(there, 2), there // 2 * 2 + core

        @pl.when(there_req != req)
        def _():
            greet(there_ctx, there_req)

        return 0

    lax.fori_loop(1, n, greet_ctx, 0)
    lax.fori_loop(0, nz, greet_core, 0)
    lax.fori_loop(1, 16, greet_plane, 0)

    row = lax.broadcasted_iota(jnp.int32, (rows, prefixes * positions), 0)
    col = lax.broadcasted_iota(jnp.int32, (rows, prefixes * positions), 1)
    hyp_of_row = lax.rem(row, tokens) // suf
    row_pid = jnp.zeros_like(row)
    for h in range(hyps):
        row_pid = jnp.where(hyp_of_row == h, hyp_prefix[h] - req * prefixes, row_pid)
    col_pid = col // positions
    col_len = jnp.zeros_like(row)
    for p in range(prefixes):
        col_len = jnp.where(col_pid == p, prefix_len[p], col_len)
    ok = (row_pid == col_pid) & (ctx * positions + lax.rem(col, positions) < col_len)
    mask[...] = jnp.where(ok, 1.0, 0.0)
    eye = lax.broadcasted_iota(jnp.int32, (rows, rows), 0) == lax.broadcasted_iota(jnp.int32, (rows, rows), 1)
    for k in range(width // 128):
        gains[0:1, k * 128 : (k + 1) * 128] = gain_attn_in[k : k + 1, :]
    for k in range(half // 128):
        gains[1:2, k * 128 : (k + 1) * 128] = jnp.where(
            core == 0, gain_pre_in[k : k + 1, :], gain_pre_in[half // 128 + k : half // 128 + k + 1, :]
        )

    def query_rows(head):
        both = queries[:, pl.ds(pl.multiple_of(head * (group * HEAD), group * HEAD), group * HEAD)]
        return jnp.concatenate([both[:, g * HEAD : (g + 1) * HEAD] for g in range(group)], 0)

    def partial_of(head):
        lanes = pl.ds(pl.multiple_of(head * HEAD, HEAD), HEAD)
        query = query_rows(head)
        keys = prefix_kv[0, :, :, lanes].reshape(prefixes * positions, HEAD)
        vals = prefix_kv[1, :, :, lanes].reshape(prefixes * positions, HEAD)
        scores = lax.dot_general(query, keys, NT, preferred_element_type=jnp.float32)
        weights = jnp.where(mask[...] > 0.5, weights_of(scores), 0.0)
        summed = jnp.dot(weights.astype(jnp.bfloat16), vals, preferred_element_type=jnp.float32)
        total = jnp.sum(weights, 1, keepdims=True)
        return summed, jnp.sum(jnp.where(eye, total, 0.0), 0, keepdims=True)

    def store_partial(ref, summed, flat):
        high = flat.astype(jnp.bfloat16).astype(jnp.float32)
        low = flat - high
        line = lax.broadcasted_iota(jnp.int32, (16, rows), 0)
        ref[0:rows, :] = summed.astype(jnp.bfloat16)
        ref[rows : rows + 16, :] = jnp.where(line == 0, high, jnp.where(line == 1, low, 0.0)).astype(jnp.bfloat16)

    def load_partial(ref):
        return (
            ref[0:rows, :].astype(jnp.float32),
            jnp.sum(ref[rows : rows + 16, :].astype(jnp.float32), 0, keepdims=True),
        )

    def distance(i):
        step = (i + 1) // 2
        return nz // 2 + step * (1 - 2 * lax.rem(i, 2))

    at_once = 4

    def others_heads(s, _):
        which = [distance(s * at_once + i) for i in range(at_once)]
        terms = [partial_of(along_z(dz) * 2 + 1 - y_lo) for dz in which]
        for dz, term in zip(which, terms):
            store_partial(party_send.at[dz], *term)
        return 0

    def own_heads(s, _):
        which = [distance(s * at_once + i) for i in range(at_once)]
        terms = [partial_of(along_z(dz) * 2 + y_lo) for dz in which]
        for dz, (summed, flat) in zip(which, terms):
            part_own[dz, 0:rows, :] = summed
            part_own[dz, rows : rows + 8, :] = jnp.broadcast_to(flat, (8, rows))
        return 0

    def party_copy(dz):
        return remote(party_send.at[dz], party_recv.at[dz], party_sem.at[0, dz], party_sem.at[1, dz], ctx=partner)

    def partz_copy(dz):
        return remote(
            partz_send.at[dz],
            partz_recv.at[dz],
            partz_sem.at[0, dz],
            partz_sem.at[1, dz],
            ctx=along_z(dz) * 2 + y_lo,
        )

    loads[0].wait()
    loads[1].wait()
    lax.fori_loop(0, nz // at_once, others_heads, 0)
    pl.semaphore_wait(barrier, (n - 1) + nz + 14)
    for dz in FAR_FIRST:
        party_copy(dz).start()

    w_copies = [
        remote(
            src.at[:, others],
            w_own.at[pl.ds((2 + i) * units, units), :],
            w_sem.at[0, i],
            w_sem.at[1, i],
            req=sibling,
        )
        for i, src in enumerate((w_gate, w_up))
    ]
    for copy in w_copies:
        copy.start()
    lax.fori_loop(0, nz // at_once, own_heads, 0)

    own = pl.ds(pl.multiple_of(ctx * HEAD, HEAD), HEAD)
    suf_row = lax.rem(lax.broadcasted_iota(jnp.int32, (rows, tokens), 0), tokens)
    suf_col = lax.broadcasted_iota(jnp.int32, (rows, tokens), 1)
    row_hyp, col_hyp = suf_row // suf, suf_col // suf
    length = jnp.zeros_like(suf_row)
    for h in range(hyps):
        length = jnp.where(col_hyp == h, suffix_len[h], length)
    usable = (row_hyp == col_hyp) & (suf_col <= suf_row) & (suf_col - col_hyp * suf < length)
    loads[2].wait()
    scores = lax.dot_general(query_rows(ctx), suffix_kv[0, :, own], NT, preferred_element_type=jnp.float32)
    weights = jnp.where(usable, weights_of(scores), 0.0)
    suf_sum = jnp.dot(weights.astype(jnp.bfloat16), suffix_kv[1, :, own], preferred_element_type=jnp.float32)
    suf_total = jnp.sum(weights, 1, keepdims=True)

    for dz in FAR_FIRST[:-1]:
        party_copy(dz).wait_recv()
        summed, flat = load_partial(party_recv.at[dz])
        store_partial(
            partz_send.at[dz], summed + part_own[dz, 0:rows, :], flat + part_own[dz, rows : rows + 1, :]
        )
        partz_copy(dz).start()

    loads[5].wait()
    tile = 128
    unit = (
        lax.broadcasted_iota(jnp.int32, (tile, tile), 0) == lax.broadcasted_iota(jnp.int32, (tile, tile), 1)
    ).astype(jnp.bfloat16)
    for k in range(0, down_raw.shape[1], tile):
        down_rows[k : k + tile, :] = lax.dot_general(
            unit, down_raw[:, k : k + tile], NT, preferred_element_type=jnp.float32
        ).astype(jnp.bfloat16)
    down_copies = [
        remote(
            down_rows.at[pl.ds(pl.multiple_of((2 * s + 1 - y_lo) * units, units), units), :],
            down_other.at[pl.ds(s * units, units), :],
            w_sem.at[0, 2 + s],
            w_sem.at[1, 2 + s],
            ctx=partner,
        )
        for s in range(nz)
    ]
    for copy in down_copies[: nz // 2]:
        copy.start()
    for s in range(nz):
        down_own[s * units : (s + 1) * units, :] = down_rows[
            pl.ds(pl.multiple_of((2 * s + y_lo) * units, units), units), :
        ]

    party_copy(0).wait_recv()
    summed, flat = load_partial(party_recv.at[0])
    summed += part_own[0, 0:rows, :] + suf_sum
    flat += part_own[0, rows : rows + 1, :]
    for dz in FAR_FIRST[:-1]:
        partz_copy(dz).wait_recv()
        more, more_flat = load_partial(partz_recv.at[dz])
        summed += more
        flat += more_flat
    total = suf_total + jnp.sum(jnp.where(eye, flat, 0.0), 1, keepdims=True)
    attn = (summed / total).astype(jnp.bfloat16)
    attn = jnp.concatenate([attn[g * tokens : (g + 1) * tokens] for g in range(group)], 1)

    loads[3].wait()
    step = 512
    for c in range(0, width, step):
        term = jnp.dot(attn, w_out[:, c : c + step], preferred_element_type=jnp.float32)
        for i in range(n):
            proj_send[i, :, c : c + step] = term[i * slab : (i + 1) * slab].astype(jnp.bfloat16)

    def projy_copy(dz):
        return remote(
            proj_send.at[(1 - y_lo) * nz + along_z(dz)],
            projy_recv.at[dz],
            projy_sem.at[0, dz],
            projy_sem.at[1, dz],
            ctx=partner,
        )

    def projz_copy(dz):
        return remote(
            projz_send.at[dz],
            projz_recv.at[dz],
            projz_sem.at[0, dz],
            projz_sem.at[1, dz],
            ctx=along_z(dz) * 2 + y_lo,
        )

    for dz in FAR_FIRST:
        projy_copy(dz).start()

    first = y_lo * nz + z
    loads[4].wait()
    around = hidden_in[pl.ds(pl.multiple_of(first * slab // 16 * 16, 16), 16), :].astype(jnp.float32)
    before = jnp.zeros((slab, width), jnp.float32)
    for g in range(16 // slab):
        before = jnp.where(lax.rem(first, 16 // slab) == g, around[g * slab : (g + 1) * slab], before)

    for dz in FAR_FIRST[:-1]:
        projy_copy(dz).wait_recv()
        both = projy_recv[dz].astype(jnp.float32) + proj_send[y_lo * nz + along_z(dz)].astype(jnp.float32)
        projz_send[dz] = both.astype(jnp.bfloat16)
        projz_copy(dz).start()

    for copy in w_copies:
        copy.wait()
    loads[6].wait()
    loads[7].wait()

    def gain_rows(i, _):
        at = pl.ds(pl.multiple_of(i * 16, 16), 16)
        w_own[at, :] = (w_own[at, :].astype(jnp.float32) * gains[1:2, :half]).astype(jnp.bfloat16)
        return 0

    lax.fori_loop(0, 4 * units // 16, gain_rows, 0)

    projy_copy(0).wait_recv()
    proj = projy_recv[0].astype(jnp.float32) + proj_send[first].astype(jnp.float32)
    for dz in FAR_FIRST[:-1]:
        projz_copy(dz).wait_recv()
        proj += projz_recv[dz].astype(jnp.float32)
    scale_a = lax.rsqrt(jnp.mean(proj * proj, 1, keepdims=True) + eps)
    resid = (before + gains[0:1, :] * proj * scale_a).astype(jnp.bfloat16)
    for h in range(2):
        slab_own[h] = resid[:, h * half : (h + 1) * half]

    def slab_copy(to_z, to_core, from_z, from_core):
        return remote(
            slab_own.at[to_core],
            slabs.at[from_core, from_z],
            slab_ssem.at[to_core, to_z],
            slab_rsem.at[from_core, from_z],
            ctx=to_z * 2 + y_lo,
            req=req - core + to_core,
        )

    for dz in FAR_FIRST[:-1]:
        slab_copy(along_z(dz), core, z, core).start()
        slab_copy(along_z(dz), 1 - core, z, core).start()
    slab_copy(z, 1 - core, z, core).start()
    for copy in down_copies[nz // 2 :]:
        copy.start()
    slabs[core, z] = slab_own[core]
    slab_copy(z, 1 - core, z, 1 - core).wait_recv()
    for dz in FAR_FIRST[:-1]:
        slab_copy(along_z(dz), core, along_z(dz), core).wait_recv()
        slab_copy(along_z(dz), core, along_z(dz), 1 - core).wait_recv()
    for c in range(2):
        for s in range(nz):
            at = (c * nz + s) * slab
            block[at : at + slab, :] = slabs[c, s].astype(jnp.float32)
        tok[c, 0] = block[c * part : (c + 1) * part, :].astype(jnp.bfloat16)

    def tok_copy(offset, link, sub):
        source = SLOT[(offset[0] - link[0]) % 4, (offset[1] - link[1]) % 4]
        slot = SLOT[offset[0] % 4, offset[1] % 4]
        there_ctx, there_req = chip(-link[0], -link[1])
        return remote(
            tok.at[sub, source],
            tok.at[sub, slot],
            tok_sem.at[0, sub, slot],
            tok_sem.at[1, sub, slot],
            ctx=there_ctx,
            req=there_req + core,
        )

    def token_step(step, sub):
        later_copies = []
        if step + 1 < len(ARRIVALS):
            for offset, link in ARRIVALS[step + 1]:
                source = SLOT[(offset[0] - link[0]) % 4, (offset[1] - link[1]) % 4]
                later_copies.append((source, tok_copy(offset, link, sub)))
        for offset, link in ARRIVALS[step]:
            tok_copy(offset, link, sub).wait_recv()
            for source, copy in later_copies:
                if source == SLOT[offset[0] % 4, offset[1] % 4]:
                    copy.start()
        for source, copy in later_copies:
            if source <= 4 * step:
                copy.start()

    def sib_copy(g, lanes):
        which = CHUNKS - 1 + lanes.start // chunk if lanes.size == chunk else g
        return remote(
            sib_send.at[g, :, lanes],
            sib_recv.at[g, :, lanes],
            sib_sem.at[0, which],
            sib_sem.at[1, which],
            req=sibling,
        )

    whole = (pl.ds(0, 2 * chunk),)
    halves = (pl.ds(0, chunk), pl.ds(chunk, chunk))
    own_part = {}
    ones = jnp.ones((16, half), jnp.bfloat16)

    def gate_up(g, lanes):
        if lanes.size == chunk:
            those = tok[lanes.start // chunk, g * blocks : (g + 1) * blocks].reshape(chunk, half)
        else:
            those = tok[:, g * blocks : (g + 1) * blocks].reshape(2 * chunk, half)
        squares = lax.dot_general(ones, those * those, NT, preferred_element_type=jnp.float32)[:8]
        sib_send[g, 2 * units :, lanes] = squares
        sib_send[g, : 2 * units, lanes] = lax.dot_general(
            w_own[2 * units :, :], those, NT, preferred_element_type=jnp.float32
        )
        sib_copy(g, lanes).start()
        products = lax.dot_general(w_own[: 2 * units, :], those, NT, preferred_element_type=jnp.float32)
        own_part[g, lanes.start] = products, squares

    major = 1 - 2 * core

    def hid_copy(g, lanes, origin, by, to):
        c = slice(None) if lanes.size != chunk else lanes.start // chunk
        which = CHUNKS - 1 + lanes.start // chunk if lanes.size == chunk else g
        source = along_z(origin)
        ref = hid.at[g, source] if lanes.size != chunk else hid.at[g, source, c]
        return remote(
            ref,
            ref,
            hid_ssem.at[which, lax.rem(to - origin + 2 * nz, nz)],
            hid_rsem.at[which, source],
            ctx=along_z(to) * 2 + y_lo,
        )

    def hidden(g, lanes):
        sib_copy(g, lanes).wait_recv()
        products, squares = own_part[g, lanes.start]
        both = products + sib_recv[g, : 2 * units, lanes]
        scale = lax.rsqrt((squares + sib_recv[g, 2 * units :, lanes])[0:1] * (1.0 / width) + eps)
        act = jax.nn.gelu(both[:units] * scale, approximate=True) * (both[units:] * scale)
        act = act.astype(jnp.bfloat16)
        for i in range(lanes.size // chunk):
            hid[g, z, lanes.start // chunk + i] = act[:, i * chunk : (i + 1) * chunk]
        for to in (2, -2, 1, -1):
            hid_copy(g, lanes, 0, 0, to).start()

    def pass_on(g, lanes):
        for way in (1, -1):
            hid_copy(g, lanes, -2 * way, 0, 0).wait_recv()

            @pl.when(major == way)
            def _():
                hid_copy(g, lanes, -2 * way, 0, 2 * way).start()

            hid_copy(g, lanes, -2 * way, 0, way).start()

    def hid_arrive(g, lanes):
        for origin in (-1, 1, -3, 3, 4):
            hid_copy(g, lanes, origin, 0, 0).wait_recv()

    def hid_sent(g, lanes):
        for to in (2, -2, 1, -1):
            hid_copy(g, lanes, 0, 0, to).wait_send()
        for way in (1, -1):

            @pl.when(major == way)
            def _():
                hid_copy(g, lanes, -2 * way, 0, 2 * way).wait_send()

            hid_copy(g, lanes, -2 * way, 0, way).wait_send()

    def ds_copy(g):
        return remote(ds_send.at[g], ds_recv.at[g], ds_sem.at[0, g], ds_sem.at[1, g], req=sibling)

    def down_terms(g, c):
        act = hid[g, :, c].reshape(nz * units, chunk).T
        return [
            jnp.dot(act, matrix[...], preferred_element_type=jnp.float32) for matrix in (down_own, down_other)
        ]

    def down(g, all_lanes):
        for lanes in all_lanes:
            hid_arrive(g, lanes)
        for side, term in enumerate(down_terms(g, 1 - core)):
            ds_send[g, side] = term.astype(jnp.bfloat16)
        ds_copy(g).start()
        return down_terms(g, core)

    def rs_copy(g, b, side):
        dx, dy = OFFSETS[g * blocks + b]
        block_ctx, first_req = chip(dx, dy)
        lo = lax.rem(block_ctx, 2)
        to_ctx = ctx if side == 0 else partner
        possible = side == 0 and dx == 0 and dy in (0, 1, -1)
        copy = remote(
            rs_send.at[g, side, pl.ds(b * part, part), :],
            rs_recv.at[place, pl.ds(pl.multiple_of(lo * part, part), part), :],
            rs_ssem.at[g, side, b],
            rs_rsem.at[place],
            ctx=to_ctx,
            req=first_req + core,
        )
        return copy, lo, (first_req + core == req) if possible else None

    def send_terms(g, terms):
        ds_copy(g).wait_recv()
        for side in range(2):
            rs_send[g, side] = (terms[side] + ds_recv[g, side].astype(jnp.float32)).astype(jnp.bfloat16)
        for b in range(blocks):
            for side in (1, 0):
                copy, lo, here = rs_copy(g, b, side)
                if here is None:
                    copy.start()
                else:

                    @pl.when(here)
                    def _():
                        rs_recv[place, pl.ds(pl.multiple_of(lo * part, part), part), :] = rs_send[
                            g, side, pl.ds(b * part, part), :
                        ]

                    @pl.when(jnp.logical_not(here))
                    def _():
                        copy.start()

    def terms_sent(g):
        for b in range(blocks):
            for side in range(2):
                copy, lo, here = rs_copy(g, b, side)
                if here is None:
                    copy.wait_send()
                else:

                    @pl.when(jnp.logical_not(here))
                    def _():
                        copy.wait_send()

    for sub in range(2):
        for offset, link in ARRIVALS[0]:
            tok_copy(offset, link, sub).start()
    token_step(0, 0)
    token_step(0, 1)
    gate_up(0, *whole)
    token_step(1, 0)
    hidden(0, *whole)
    token_step(1, 1)
    gate_up(1, *whole)
    token_step(2, 0)
    hidden(1, *whole)
    pass_on(0, *whole)
    token_step(2, 1)
    gate_up(2, *whole)
    token_step(3, 0)
    hidden(2, *whole)
    pass_on(1, *whole)
    gate_up(3, halves[0])
    token_step(3, 1)
    gate_up(3, halves[1])
    hidden(3, halves[0])
    hidden(3, halves[1])
    for copy in down_copies:
        copy.wait()
    terms = down(0, whole)
    pass_on(2, *whole)
    send_terms(0, terms)
    pass_on(3, halves[0])
    terms = down(1, whole)
    pass_on(3, halves[1])
    send_terms(1, terms)
    terms = down(2, whole)
    send_terms(2, terms)

    def resid_copy(i):
        lo, slot = (y_lo, 0) if i == 0 else (1 - y_lo, 1 + 2 * y_lo)
        return remote(
            tok.at[1 - core, slot],
            resid_out.at[pl.ds(pl.multiple_of(lo * part, part), part), mine],
            resid_sem.at[0, i],
            resid_sem.at[1, i],
            req=sibling,
        )

    for i in range(2):
        resid_copy(i).start()
        lo, slot = (y_lo, 0) if i == 0 else (1 - y_lo, 1 + 2 * y_lo)
        resid_out[pl.ds(pl.multiple_of(lo * part, part), part), mine] = tok[core, slot]

    terms = down(3, halves)
    send_terms(3, terms)

    for dz in FAR_FIRST:
        party_copy(dz).wait_send()
        projy_copy(dz).wait_send()
    for dz in FAR_FIRST[:-1]:
        partz_copy(dz).wait_send()
        projz_copy(dz).wait_send()
        slab_copy(along_z(dz), core, z, core).wait_send()
        slab_copy(along_z(dz), 1 - core, z, core).wait_send()
    slab_copy(z, 1 - core, z, core).wait_send()
    for step in ARRIVALS:
        for offset, link in step:
            for sub in range(2):
                tok_copy(offset, link, sub).wait_send()
    for g in range(CHUNKS):
        for lanes in whole if g + 1 < CHUNKS else halves:
            sib_copy(g, lanes).wait_send()
            hid_sent(g, lanes)
        ds_copy(g).wait_send()
    for i in range(2):
        resid_copy(i).wait()

    def add_terms(s, total):
        there = lax.rem(place + s, 16)
        remote(
            rs_recv.at[there],
            rs_recv.at[there],
            rs_ssem.at[0, 0, 0],
            rs_rsem.at[there],
            ctx=z * 2 + lax.rem(there, 2),
            req=there // 2 * 2 + core,
        ).wait_recv()
        return total + rs_recv[there].astype(jnp.float32)

    total = lax.fori_loop(1, 16, add_terms, rs_recv[place].astype(jnp.float32))
    out[...] = total.astype(jnp.bfloat16)
    for g in range(CHUNKS):
        terms_sent(g)


def layer(
    hidden_in,
    queries,
    suffix_kv,
    prefix_kv,
    hyp_prefix,
    suffix_len,
    prefix_len,
    w_out,
    gain_attn,
    gain_pre,
    w_gate,
    w_up,
    w_down,
):
    n = 16
    nz = 8
    tokens, width = hidden_in.shape
    half = width // 2
    rows = HEADS // KV_HEADS * tokens
    slab = tokens // n
    positions = prefix_kv.shape[1] * prefix_kv.shape[2]
    units = w_gate.shape[1]
    columns = w_down.shape[1]
    chunk = 16 // CHUNKS * tokens // 2
    vmem = pl.BlockSpec(memory_space=pltpu.VMEM)
    smem = pl.BlockSpec(memory_space=pltpu.SMEM)
    hbm = pl.BlockSpec(memory_space=pl.ANY)
    dma = pltpu.SemaphoreType.DMA
    bf16 = jnp.bfloat16
    resid, out = pl.pallas_call(
        layer_kernel,
        out_shape=(
            jax.ShapeDtypeStruct((tokens, width), bf16),
            jax.ShapeDtypeStruct((tokens, columns), bf16),
        ),
        in_specs=[hbm, hbm, hbm, smem, smem, smem, hbm, hbm, vmem, vmem, hbm, hbm, hbm],
        out_specs=(vmem, vmem),
        scratch_shapes=[
            pltpu.VMEM(queries.shape, bf16),
            pltpu.VMEM(suffix_kv.shape, bf16),
            pltpu.VMEM(prefix_kv.shape, bf16),
            pltpu.VMEM(w_out.shape, bf16),
            pltpu.VMEM(hidden_in.shape, bf16),
            pltpu.VMEM((2, width), jnp.float32),
            pltpu.VMEM((rows, positions), jnp.float32),
            pltpu.VMEM((nz, rows + 16, HEAD), bf16),
            pltpu.VMEM((nz, rows + 16, HEAD), bf16),
            pltpu.VMEM((nz, rows + 8, HEAD), jnp.float32),
            pltpu.VMEM((nz, rows + 16, HEAD), bf16),
            pltpu.VMEM((nz, rows + 16, HEAD), bf16),
            pltpu.VMEM((n, slab, width), bf16),
            pltpu.VMEM((nz, slab, width), bf16),
            pltpu.VMEM((nz, slab, width), bf16),
            pltpu.VMEM((nz, slab, width), bf16),
            pltpu.VMEM((2, slab, half), bf16),
            pltpu.VMEM((columns, n * units), bf16),
            pltpu.VMEM((n * units, columns), bf16),
            pltpu.VMEM((nz * units, columns), bf16),
            pltpu.VMEM((nz * units, columns), bf16),
            pltpu.VMEM((4 * units, half), bf16),
            pltpu.VMEM((2, nz, slab, half), bf16),
            pltpu.VMEM((tokens, half), jnp.float32),
            pltpu.VMEM((2, 16, tokens // 2, half), bf16),
            pltpu.VMEM((CHUNKS, 2 * units + 8, 2 * chunk), jnp.float32),
            pltpu.VMEM((CHUNKS, 2 * units + 8, 2 * chunk), jnp.float32),
            pltpu.VMEM((CHUNKS, nz, 2, units, chunk), bf16),
            pltpu.VMEM((CHUNKS, 2, chunk, columns), bf16),
            pltpu.VMEM((CHUNKS, 2, chunk, columns), bf16),
            pltpu.VMEM((CHUNKS, 2, chunk, columns), bf16),
            pltpu.VMEM((16, tokens, columns), bf16),
            dma((8,)),
            dma((2, nz)),
            dma((2, nz)),
            dma((2, nz)),
            dma((2, nz)),
            dma((2, 2)),
            dma((2, 2 + nz)),
            dma((2, nz)),
            dma((2, nz)),
            dma((2, 2, 16)),
            dma((2, CHUNKS + 1)),
            dma((CHUNKS + 1, nz)),
            dma((CHUNKS + 1, nz)),
            dma((2, CHUNKS)),
            dma((CHUNKS, 2, 4)),
            dma((16,)),
        ],
        compiler_params=pltpu.CompilerParams(
            collective_id=0, has_side_effects=True, vmem_limit_bytes=60 * 2**20
        ),
        cost_estimate=pl.CostEstimate(flops=5 * 10**9, bytes_accessed=10**7, transcendentals=10**6),
        name="layer",
    )(
        queries,
        suffix_kv,
        prefix_kv,
        hyp_prefix,
        suffix_len,
        prefix_len,
        w_out,
        hidden_in,
        gain_attn.reshape(-1, 128),
        gain_pre.reshape(-1, 128),
        w_gate.T,
        w_up.T,
        w_down.T,
    )
    return resid, out


def solution(mesh):
    placed = (
        P("req", None),
        P("req", None),
        P(None, "req", None),
        P(None, "req", "ctx", None),
        P("req"),
        P("req"),
        P("req"),
        P("ctx", None),
        P(),
        P(),
        P(None, ("req", "ctx")),
        P(None, ("req", "ctx")),
        P("req", "ctx"),
    )
    return jax.shard_map(
        layer,
        mesh=mesh,
        in_specs=placed,
        out_specs=(P("req", None), P("req", "ctx")),
        check_vma=False,
    )
```

```python
import functools

import jax
import jax.numpy as jnp
from jax import lax
from jax.experimental import pallas as pl
from jax.experimental.pallas import tpu as pltpu
from jax.sharding import PartitionSpec as P

HEADS = 32
KV_HEADS = 16
HEAD = 128

softcap = 50.0
query_scale = 144.0 ** (-0.5)
eps = 1e-06

NT = (((1,), (1,)), ((), ()))
MESH = pl.DeviceIdType.MESH

ARRIVALS = (
    (((0, 1), (0, 1)), ((-1, 0), (-1, 0)), ((0, -1), (0, -1)), ((1, 0), (1, 0))),
    (((1, 1), (1, 0)), ((-1, 1), (0, 1)), ((-1, -1), (-1, 0)), ((1, -1), (0, -1))),
    (((2, 0), (1, 0)), ((0, 2), (0, 1)), ((2, -1), (-1, 0)), ((1, 2), (0, -1))),
    (((2, 1), (1, 0)), ((-1, 2), (0, 1)), ((2, 2), (0, -1))),
)
OFFSETS = ((0, 0),) + tuple(offset for step in ARRIVALS for offset, _ in step)
SLOT = {(dx % 4, dy % 4): i for i, (dx, dy) in enumerate(OFFSETS)}
CHUNKS = 4
FAR_FIRST = (4, 3, 5, 2, 6, 1, 7, 0)


def weights_of(scores):
    return jnp.exp(softcap * jnp.tanh(scores * (query_scale / softcap)))


def layer_kernel(
    queries_in,
    suffix_in,
    prefix_in,
    hyp_prefix,
    suffix_len,
    prefix_len,
    w_out_in,
    hidden_hbm,
    gain_attn_in,
    gain_pre_in,
    w_gate,
    w_up,
    w_down,
    resid_out,
    out,
    queries,
    suffix_kv,
    prefix_kv,
    w_out,
    hidden_in,
    gains,
    mask,
    party_send,
    party_recv,
    part_own,
    partz_send,
    partz_recv,
    proj_send,
    projy_recv,
    projz_send,
    projz_recv,
    slab_own,
    down_raw,
    down_rows,
    down_own,
    down_other,
    w_own,
    slabs,
    block,
    tok,
    sib_send,
    sib_recv,
    hid,
    ds_send,
    ds_recv,
    rs_send,
    rs_recv,
    load_sem,
    party_sem,
    partz_sem,
    projy_sem,
    projz_sem,
    resid_sem,
    w_sem,
    slab_ssem,
    slab_rsem,
    tok_sem,
    sib_sem,
    hid_ssem,
    hid_rsem,
    ds_sem,
    rs_ssem,
    rs_rsem,
):
    ctx, req = lax.axis_index("ctx"), lax.axis_index("req")
    z, y_lo = ctx // 2, lax.rem(ctx, 2)
    x, y_hi, core = req // 4, lax.rem(req // 2, 2), lax.rem(req, 2)
    y = y_hi * 2 + y_lo
    place = x * 4 + y
    n = 16
    nz = 8
    tokens = queries.shape[0]
    prefixes, positions = prefix_kv.shape[1], prefix_kv.shape[2]
    group = HEADS // KV_HEADS
    rows = group * tokens
    hyps = hyp_prefix.shape[0]
    suf = tokens // hyps
    slab = tokens // n
    width = w_out.shape[1]
    half = width // 2
    units = w_gate.shape[0]
    blocks = 16 // CHUNKS
    part = tokens // 2
    chunk = blocks * part
    partner = ctx + 1 - 2 * y_lo
    sibling = req + 1 - 2 * core

    def chip(dx, dy):
        there_y = lax.rem(y + dy + 4, 4)
        return z * 2 + lax.rem(there_y, 2), lax.rem(x + dx + 4, 4) * 4 + there_y // 2 * 2

    def along_z(dz):
        return lax.rem(z + dz + nz, nz)

    def remote(src, dst, ssem, rsem, **where):
        return pltpu.make_async_remote_copy(
            src_ref=src, dst_ref=dst, send_sem=ssem, recv_sem=rsem, device_id=where, device_id_type=MESH
        )

    mine = pl.ds(pl.multiple_of(core * half, half), half)
    others = pl.ds(pl.multiple_of((1 - core) * half, half), half)
    loads = [
        pltpu.make_async_copy(src, dst, load_sem.at[i])
        for i, (src, dst) in enumerate(
            (
                (queries_in, queries),
                (prefix_in, prefix_kv),
                (suffix_in, suffix_kv),
                (w_out_in, w_out),
                (hidden_hbm, hidden_in),
                (w_down, down_raw),
                (w_gate.at[:, mine], w_own.at[pl.ds(0, units), :]),
                (w_up.at[:, mine], w_own.at[pl.ds(units, units), :]),
            )
        )
    ]
    for load in loads:
        load.start()

    barrier = pltpu.get_barrier_semaphore()

    def greet(there_ctx, there_req):
        pl.semaphore_signal(barrier, inc=1, device_id={"ctx": there_ctx, "req": there_req}, device_id_type=MESH)

    def greet_z(s, _):
        greet(along_z(s) * 2 + y_lo, req)
        return 0

    def greet_core(s, _):
        greet(along_z(s) * 2 + y_lo, sibling)
        return 0

    def greet_plane(s, _):
        there = lax.rem(place + s, 16)
        there_ctx, there_req = z * 2 + lax.rem(there, 2), there // 2 * 2 + core

        @pl.when(there_req != req)
        def _():
            greet(there_ctx, there_req)

        return 0

    greet(partner, req)
    lax.fori_loop(1, nz, greet_z, 0)
    lax.fori_loop(0, nz, greet_core, 0)
    lax.fori_loop(1, 16, greet_plane, 0)

    row = lax.broadcasted_iota(jnp.int32, (rows, prefixes * positions), 0)
    col = lax.broadcasted_iota(jnp.int32, (rows, prefixes * positions), 1)
    hyp_of_row = lax.rem(row, tokens) // suf
    row_pid = jnp.zeros_like(row)
    for h in range(hyps):
        row_pid = jnp.where(hyp_of_row == h, hyp_prefix[h] - req * prefixes, row_pid)
    col_pid = col // positions
    col_len = jnp.zeros_like(row)
    for p in range(prefixes):
        col_len = jnp.where(col_pid == p, prefix_len[p], col_len)
    ok = (row_pid == col_pid) & (ctx * positions + lax.rem(col, positions) < col_len)
    mask[...] = jnp.where(ok, 1.0, 0.0)
    eye = lax.broadcasted_iota(jnp.int32, (rows, rows), 0) == lax.broadcasted_iota(jnp.int32, (rows, rows), 1)
    for k in range(width // 128):
        gains[0:1, k * 128 : (k + 1) * 128] = gain_attn_in[k : k + 1, :]
    for k in range(half // 128):
        gains[1:2, k * 128 : (k + 1) * 128] = jnp.where(
            core == 0, gain_pre_in[k : k + 1, :], gain_pre_in[half // 128 + k : half // 128 + k + 1, :]
        )

    def query_rows(head):
        both = queries[:, pl.ds(pl.multiple_of(head * (group * HEAD), group * HEAD), group * HEAD)]
        return jnp.concatenate([both[:, g * HEAD : (g + 1) * HEAD] for g in range(group)], 0)

    def partial_of(head):
        lanes = pl.ds(pl.multiple_of(head * HEAD, HEAD), HEAD)
        query = query_rows(head)
        keys = prefix_kv[0, :, :, lanes].reshape(prefixes * positions, HEAD)
        vals = prefix_kv[1, :, :, lanes].reshape(prefixes * positions, HEAD)
        scores = lax.dot_general(query, keys, NT, preferred_element_type=jnp.float32)
        weights = jnp.where(mask[...] > 0.5, weights_of(scores), 0.0)
        summed = jnp.dot(weights.astype(jnp.bfloat16), vals, preferred_element_type=jnp.float32)
        total = jnp.sum(weights, 1, keepdims=True)
        return summed, jnp.sum(jnp.where(eye, total, 0.0), 0, keepdims=True)

    def store_partial(ref, summed, flat):
        high = flat.astype(jnp.bfloat16).astype(jnp.float32)
        low = flat - high
        line = lax.broadcasted_iota(jnp.int32, (16, rows), 0)
        ref[0:rows, :] = summed.astype(jnp.bfloat16)
        ref[rows : rows + 16, :] = jnp.where(line == 0, high, jnp.where(line == 1, low, 0.0)).astype(jnp.bfloat16)

    def load_partial(ref):
        return (
            ref[0:rows, :].astype(jnp.float32),
            jnp.sum(ref[rows : rows + 16, :].astype(jnp.float32), 0, keepdims=True),
        )

    def distance(i):
        step = (i + 1) // 2
        return nz // 2 + step * (1 - 2 * lax.rem(i, 2))

    at_once = 4

    def others_heads(s, _):
        which = [distance(s * at_once + i) for i in range(at_once)]
        terms = [partial_of(along_z(dz) * 2 + 1 - y_lo) for dz in which]
        for dz, term in zip(which, terms):
            store_partial(party_send.at[dz], *term)
        return 0

    def own_heads(s, _):
        which = [distance(s * at_once + i) for i in range(at_once)]
        terms = [partial_of(along_z(dz) * 2 + y_lo) for dz in which]
        for dz, (summed, flat) in zip(which, terms):
            part_own[dz, 0:rows, :] = summed
            part_own[dz, rows : rows + 8, :] = jnp.broadcast_to(flat, (8, rows))
        return 0

    def party_copy(dz):
        return remote(party_send.at[dz], party_recv.at[dz], party_sem.at[0, dz], party_sem.at[1, dz], ctx=partner)

    def partz_copy(dz):
        return remote(
            partz_send.at[dz],
            partz_recv.at[dz],
            partz_sem.at[0, dz],
            partz_sem.at[1, dz],
            ctx=along_z(dz) * 2 + y_lo,
        )

    loads[0].wait()
    loads[1].wait()
    lax.fori_loop(0, nz // at_once, others_heads, 0)
    pl.semaphore_wait(barrier, 1 + (nz - 1) + nz + 14)
    for dz in FAR_FIRST:
        party_copy(dz).start()

    w_copies = [
        remote(
            src.at[:, others],
            w_own.at[pl.ds((2 + i) * units, units), :],
            w_sem.at[0, i],
            w_sem.at[1, i],
            req=sibling,
        )
        for i, src in enumerate((w_gate, w_up))
    ]
    for copy in w_copies:
        copy.start()
    lax.fori_loop(0, nz // at_once, own_heads, 0)

    own = pl.ds(pl.multiple_of(ctx * HEAD, HEAD), HEAD)
    suf_row = lax.rem(lax.broadcasted_iota(jnp.int32, (rows, tokens), 0), tokens)
    suf_col = lax.broadcasted_iota(jnp.int32, (rows, tokens), 1)
    row_hyp, col_hyp = suf_row // suf, suf_col // suf
    length = jnp.zeros_like(suf_row)
    for h in range(hyps):
        length = jnp.where(col_hyp == h, suffix_len[h], length)
    usable = (row_hyp == col_hyp) & (suf_col <= suf_row) & (suf_col - col_hyp * suf < length)
    loads[2].wait()
    scores = lax.dot_general(query_rows(ctx), suffix_kv[0, :, own], NT, preferred_element_type=jnp.float32)
    weights = jnp.where(usable, weights_of(scores), 0.0)
    suf_sum = jnp.dot(weights.astype(jnp.bfloat16), suffix_kv[1, :, own], preferred_element_type=jnp.float32)
    suf_total = jnp.sum(weights, 1, keepdims=True)

    loads[5].wait()
    tile = 128
    unit = (
        lax.broadcasted_iota(jnp.int32, (tile, tile), 0) == lax.broadcasted_iota(jnp.int32, (tile, tile), 1)
    ).astype(jnp.bfloat16)
    for k in range(0, down_raw.shape[1], tile):
        down_rows[k : k + tile, :] = lax.dot_general(
            unit, down_raw[:, k : k + tile], NT, preferred_element_type=jnp.float32
        ).astype(jnp.bfloat16)
    down_copies = [
        remote(
            down_rows.at[pl.ds(pl.multiple_of((2 * s + 1 - y_lo) * units, units), units), :],
            down_other.at[pl.ds(s * units, units), :],
            w_sem.at[0, 2 + s],
            w_sem.at[1, 2 + s],
            ctx=partner,
        )
        for s in range(nz)
    ]
    for s in range(nz):
        down_own[s * units : (s + 1) * units, :] = down_rows[
            pl.ds(pl.multiple_of((2 * s + y_lo) * units, units), units), :
        ]

    for dz in FAR_FIRST[:-1]:
        party_copy(dz).wait_recv()
        summed, flat = load_partial(party_recv.at[dz])
        store_partial(
            partz_send.at[dz], summed + part_own[dz, 0:rows, :], flat + part_own[dz, rows : rows + 1, :]
        )
        partz_copy(dz).start()

    for copy in down_copies[:2]:
        copy.start()

    party_copy(0).wait_recv()
    summed, flat = load_partial(party_recv.at[0])
    summed += part_own[0, 0:rows, :] + suf_sum
    flat += part_own[0, rows : rows + 1, :]
    for dz in FAR_FIRST[:-1]:
        partz_copy(dz).wait_recv()
        more, more_flat = load_partial(partz_recv.at[dz])
        summed += more
        flat += more_flat
    total = suf_total + jnp.sum(jnp.where(eye, flat, 0.0), 1, keepdims=True)
    attn = (summed / total).astype(jnp.bfloat16)
    attn = jnp.concatenate([attn[g * tokens : (g + 1) * tokens] for g in range(group)], 1)

    loads[3].wait()
    step = 512
    for c in range(0, width, step):
        term = jnp.dot(attn, w_out[:, c : c + step], preferred_element_type=jnp.float32)
        for i in range(n):
            proj_send[i, :, c : c + step] = term[i * slab : (i + 1) * slab].astype(jnp.bfloat16)

    def projy_copy(dz):
        return remote(
            proj_send.at[(1 - y_lo) * nz + along_z(dz)],
            projy_recv.at[dz],
            projy_sem.at[0, dz],
            projy_sem.at[1, dz],
            ctx=partner,
        )

    def projz_copy(dz):
        return remote(
            projz_send.at[dz],
            projz_recv.at[dz],
            projz_sem.at[0, dz],
            projz_sem.at[1, dz],
            ctx=along_z(dz) * 2 + y_lo,
        )

    for dz in FAR_FIRST:
        projy_copy(dz).start()

    first = y_lo * nz + z
    loads[4].wait()
    around = hidden_in[pl.ds(pl.multiple_of(first * slab // 16 * 16, 16), 16), :].astype(jnp.float32)
    before = jnp.zeros((slab, width), jnp.float32)
    for g in range(16 // slab):
        before = jnp.where(lax.rem(first, 16 // slab) == g, around[g * slab : (g + 1) * slab], before)

    for dz in FAR_FIRST[:-1]:
        projy_copy(dz).wait_recv()
        both = projy_recv[dz].astype(jnp.float32) + proj_send[y_lo * nz + along_z(dz)].astype(jnp.float32)
        projz_send[dz] = both.astype(jnp.bfloat16)
        projz_copy(dz).start()

    for copy in down_copies[2:]:
        copy.start()

    for copy in w_copies:
        copy.wait()
    loads[6].wait()
    loads[7].wait()

    def gain_rows(i, _):
        at = pl.ds(pl.multiple_of(i * 16, 16), 16)
        w_own[at, :] = (w_own[at, :].astype(jnp.float32) * gains[1:2, :half]).astype(jnp.bfloat16)
        return 0

    lax.fori_loop(0, 4 * units // 16, gain_rows, 0)

    projy_copy(0).wait_recv()
    proj = projy_recv[0].astype(jnp.float32) + proj_send[first].astype(jnp.float32)
    for dz in FAR_FIRST[:-1]:
        projz_copy(dz).wait_recv()
        proj += projz_recv[dz].astype(jnp.float32)
    scale_a = lax.rsqrt(jnp.mean(proj * proj, 1, keepdims=True) + eps)
    resid = (before + gains[0:1, :] * proj * scale_a).astype(jnp.bfloat16)
    for h in range(2):
        slab_own[h] = resid[:, h * half : (h + 1) * half]

    def slab_copy(to_z, to_core, from_z, from_core):
        return remote(
            slab_own.at[to_core],
            slabs.at[from_core, from_z],
            slab_ssem.at[to_core, to_z],
            slab_rsem.at[from_core, from_z],
            ctx=to_z * 2 + y_lo,
            req=req - core + to_core,
        )

    def send_slabs():
        for dz in FAR_FIRST[:-1]:
            slab_copy(along_z(dz), core, z, core).start()
            slab_copy(along_z(dz), 1 - core, z, core).start()

    def near_slabs():
        for dz in (1, -1):
            slab_copy(along_z(dz), core, along_z(dz), 0).wait_recv()

    slabs[core, z] = slab_own[core]
    slab_copy(z, 1 - core, z, core).start()

    @pl.when(core == 0)
    def _():
        send_slabs()
        near_slabs()

    @pl.when(core == 1)
    def _():
        near_slabs()
        send_slabs()

    def gather_slabs(c):
        for dz in FAR_FIRST[:-1] if c == 1 else (4, 3, 5, 2, 6):
            slab_copy(along_z(dz), core, along_z(dz), c).wait_recv()

        @pl.when(core != c)
        def _():
            slab_copy(z, core, z, c).wait_recv()

        for s in range(nz):
            at = (c * nz + s) * slab
            block[at : at + slab, :] = slabs[c, s].astype(jnp.float32)
        tok[c, 0] = block[c * part : (c + 1) * part, :].astype(jnp.bfloat16)

    def tok_copy(offset, link, sub):
        source = SLOT[(offset[0] - link[0]) % 4, (offset[1] - link[1]) % 4]
        slot = SLOT[offset[0] % 4, offset[1] % 4]
        there_ctx, there_req = chip(-link[0], -link[1])
        return remote(
            tok.at[sub, source],
            tok.at[sub, slot],
            tok_sem.at[0, sub, slot],
            tok_sem.at[1, sub, slot],
            ctx=there_ctx,
            req=there_req + core,
        )

    def token_step(step, sub):
        later_copies = []
        if step + 1 < len(ARRIVALS):
            for offset, link in ARRIVALS[step + 1]:
                source = SLOT[(offset[0] - link[0]) % 4, (offset[1] - link[1]) % 4]
                later_copies.append((source, tok_copy(offset, link, sub)))
        for offset, link in ARRIVALS[step]:
            tok_copy(offset, link, sub).wait_recv()
            for source, copy in later_copies:
                if source == SLOT[offset[0] % 4, offset[1] % 4]:
                    copy.start()
        for source, copy in later_copies:
            if source <= 4 * step:
                copy.start()

    def sib_copy(i):
        return remote(sib_send.at[i], sib_recv.at[i], sib_sem.at[0, i], sib_sem.at[1, i], req=sibling)

    own_part = {}
    ones = jnp.ones((16, half), jnp.bfloat16)

    def gate_up(i):
        those = tok[i % 2, i // 2 * blocks : (i // 2 + 1) * blocks].reshape(chunk, half)
        squares = lax.dot_general(ones, those * those, NT, preferred_element_type=jnp.float32)[:8]
        sib_send[i, 2 * units :] = squares
        sib_send[i, : 2 * units] = lax.dot_general(
            w_own[2 * units :, :], those, NT, preferred_element_type=jnp.float32
        )
        sib_copy(i).start()
        products = lax.dot_general(w_own[: 2 * units, :], those, NT, preferred_element_type=jnp.float32)
        own_part[i] = products, squares

    major = 1 - 2 * core

    def hid_copy(i, origin, to):
        source = along_z(origin)
        ref = hid.at[i // 2, source, i % 2]
        return remote(
            ref,
            ref,
            hid_ssem.at[i, lax.rem(to - origin + 2 * nz, nz)],
            hid_rsem.at[i, source],
            ctx=along_z(to) * 2 + y_lo,
        )

    def hidden(i):
        sib_copy(i).wait_recv()
        products, squares = own_part[i]
        both = products + sib_recv[i, : 2 * units]
        scale = lax.rsqrt((squares + sib_recv[i, 2 * units :])[0:1] * (1.0 / width) + eps)
        act = jax.nn.gelu(both[:units] * scale, approximate=True) * (both[units:] * scale)
        hid[i // 2, z, i % 2] = act.astype(jnp.bfloat16)
        for to in (2, -2, 1, -1):
            hid_copy(i, 0, to).start()

    def pass_on(i):
        for way in (1, -1):
            hid_copy(i, -2 * way, 0).wait_recv()

            @pl.when(major == way)
            def _():
                hid_copy(i, -2 * way, 2 * way).start()

            hid_copy(i, -2 * way, way).start()

    def hid_arrive(i):
        for origin in (-1, 1, -3, 3, 4):
            hid_copy(i, origin, 0).wait_recv()

    def hid_sent(i):
        for way in (1, -1):
            for away in (1, 2, 3):
                hid_copy(i, 0, way * away).wait_send()

            @pl.when(major == way)
            def _():
                hid_copy(i, 0, way * 4).wait_send()

    def ds_copy(g):
        return remote(ds_send.at[g], ds_recv.at[g], ds_sem.at[0, g], ds_sem.at[1, g], req=sibling)

    def down_terms(g, c):
        act = hid[g, :, c].reshape(nz * units, chunk).T
        return [
            jnp.dot(act, matrix[...], preferred_element_type=jnp.float32) for matrix in (down_own, down_other)
        ]

    def down(g):
        for i in (2 * g, 2 * g + 1):
            hid_arrive(i)
        for side, term in enumerate(down_terms(g, 1 - core)):
            ds_send[g, side] = term.astype(jnp.bfloat16)
        ds_copy(g).start()
        return down_terms(g, core)

    def rs_copy(g, b, side):
        dx, dy = OFFSETS[g * blocks + b]
        block_ctx, first_req = chip(dx, dy)
        lo = lax.rem(block_ctx, 2)
        to_ctx = ctx if side == 0 else partner
        possible = side == 0 and dx == 0 and dy in (0, 1, -1)
        copy = remote(
            rs_send.at[g, side, pl.ds(b * part, part), :],
            rs_recv.at[place, pl.ds(pl.multiple_of(lo * part, part), part), :],
            rs_ssem.at[g, side, b],
            rs_rsem.at[place],
            ctx=to_ctx,
            req=first_req + core,
        )
        return copy, lo, (first_req + core == req) if possible else None

    def send_terms(g, terms):
        ds_copy(g).wait_recv()
        for side in range(2):
            rs_send[g, side] = (terms[side] + ds_recv[g, side].astype(jnp.float32)).astype(jnp.bfloat16)
        for b in range(blocks):
            for side in (1, 0):
                copy, lo, here = rs_copy(g, b, side)
                if here is None:
                    copy.start()
                else:

                    @pl.when(here)
                    def _():
                        rs_recv[place, pl.ds(pl.multiple_of(lo * part, part), part), :] = rs_send[
                            g, side, pl.ds(b * part, part), :
                        ]

                    @pl.when(jnp.logical_not(here))
                    def _():
                        copy.start()

    def terms_sent(g):
        for b in range(blocks):
            for side in range(2):
                copy, lo, here = rs_copy(g, b, side)
                if here is None:
                    copy.wait_send()
                else:

                    @pl.when(jnp.logical_not(here))
                    def _():
                        copy.wait_send()

    for sub in range(2):
        gather_slabs(sub)
        for offset, link in ARRIVALS[0]:
            tok_copy(offset, link, sub).start()
    for i in range(2 * CHUNKS):
        token_step(i // 2, i % 2)
        gate_up(i)
        if i >= 2:
            pass_on(i - 2)
        hidden(i)
        if i == 6:
            for copy in down_copies:
                copy.wait()
            first_terms = down(0)
    send_terms(0, first_terms)
    terms = down(1)
    pass_on(6)
    send_terms(1, terms)
    terms = down(2)
    pass_on(7)
    send_terms(2, terms)

    def resid_copy(i):
        lo, slot = (y_lo, 0) if i == 0 else (1 - y_lo, 1 + 2 * y_lo)
        return remote(
            tok.at[1 - core, slot],
            resid_out.at[pl.ds(pl.multiple_of(lo * part, part), part), mine],
            resid_sem.at[0, i],
            resid_sem.at[1, i],
            req=sibling,
        )

    for i in range(2):
        resid_copy(i).start()
        lo, slot = (y_lo, 0) if i == 0 else (1 - y_lo, 1 + 2 * y_lo)
        resid_out[pl.ds(pl.multiple_of(lo * part, part), part), mine] = tok[core, slot]

    terms = down(3)
    send_terms(3, terms)

    for dz in FAR_FIRST:
        party_copy(dz).wait_send()
        projy_copy(dz).wait_send()
    for dz in FAR_FIRST[:-1]:
        partz_copy(dz).wait_send()
        projz_copy(dz).wait_send()
        slab_copy(along_z(dz), core, z, core).wait_send()
        slab_copy(along_z(dz), 1 - core, z, core).wait_send()
    slab_copy(z, 1 - core, z, core).wait_send()
    for step in ARRIVALS:
        for offset, link in step:
            for sub in range(2):
                tok_copy(offset, link, sub).wait_send()
    for g in range(CHUNKS):
        for i in (2 * g, 2 * g + 1):
            sib_copy(i).wait_send()
            hid_sent(i)
        ds_copy(g).wait_send()
    for i in range(2):
        resid_copy(i).wait()

    def add_terms(s, total):
        there = lax.rem(place + s, 16)
        remote(
            rs_recv.at[there],
            rs_recv.at[there],
            rs_ssem.at[0, 0, 0],
            rs_rsem.at[there],
            ctx=z * 2 + lax.rem(there, 2),
            req=there // 2 * 2 + core,
        ).wait_recv()
        return total + rs_recv[there].astype(jnp.float32)

    total = lax.fori_loop(1, 16, add_terms, rs_recv[place].astype(jnp.float32))
    out[...] = total.astype(jnp.bfloat16)
    for g in range(CHUNKS):
        terms_sent(g)


def layer(
    hidden_in,
    queries,
    suffix_kv,
    prefix_kv,
    hyp_prefix,
    suffix_len,
    prefix_len,
    w_out,
    gain_attn,
    gain_pre,
    w_gate,
    w_up,
    w_down,
):
    n = 16
    nz = 8
    tokens, width = hidden_in.shape
    half = width // 2
    rows = HEADS // KV_HEADS * tokens
    slab = tokens // n
    positions = prefix_kv.shape[1] * prefix_kv.shape[2]
    units = w_gate.shape[1]
    columns = w_down.shape[1]
    chunk = 16 // CHUNKS * tokens // 2
    vmem = pl.BlockSpec(memory_space=pltpu.VMEM)
    smem = pl.BlockSpec(memory_space=pltpu.SMEM)
    hbm = pl.BlockSpec(memory_space=pl.ANY)
    dma = pltpu.SemaphoreType.DMA
    bf16 = jnp.bfloat16
    resid, out = pl.pallas_call(
        layer_kernel,
        out_shape=(
            jax.ShapeDtypeStruct((tokens, width), bf16),
            jax.ShapeDtypeStruct((tokens, columns), bf16),
        ),
        in_specs=[hbm, hbm, hbm, smem, smem, smem, hbm, hbm, vmem, vmem, hbm, hbm, hbm],
        out_specs=(vmem, vmem),
        scratch_shapes=[
            pltpu.VMEM(queries.shape, bf16),
            pltpu.VMEM(suffix_kv.shape, bf16),
            pltpu.VMEM(prefix_kv.shape, bf16),
            pltpu.VMEM(w_out.shape, bf16),
            pltpu.VMEM(hidden_in.shape, bf16),
            pltpu.VMEM((2, width), jnp.float32),
            pltpu.VMEM((rows, positions), jnp.float32),
            pltpu.VMEM((nz, rows + 16, HEAD), bf16),
            pltpu.VMEM((nz, rows + 16, HEAD), bf16),
            pltpu.VMEM((nz, rows + 8, HEAD), jnp.float32),
            pltpu.VMEM((nz, rows + 16, HEAD), bf16),
            pltpu.VMEM((nz, rows + 16, HEAD), bf16),
            pltpu.VMEM((n, slab, width), bf16),
            pltpu.VMEM((nz, slab, width), bf16),
            pltpu.VMEM((nz, slab, width), bf16),
            pltpu.VMEM((nz, slab, width), bf16),
            pltpu.VMEM((2, slab, half), bf16),
            pltpu.VMEM((columns, n * units), bf16),
            pltpu.VMEM((n * units, columns), bf16),
            pltpu.VMEM((nz * units, columns), bf16),
            pltpu.VMEM((nz * units, columns), bf16),
            pltpu.VMEM((4 * units, half), bf16),
            pltpu.VMEM((2, nz, slab, half), bf16),
            pltpu.VMEM((tokens, half), jnp.float32),
            pltpu.VMEM((2, 16, tokens // 2, half), bf16),
            pltpu.VMEM((2 * CHUNKS, 2 * units + 8, chunk), jnp.float32),
            pltpu.VMEM((2 * CHUNKS, 2 * units + 8, chunk), jnp.float32),
            pltpu.VMEM((CHUNKS, nz, 2, units, chunk), bf16),
            pltpu.VMEM((CHUNKS, 2, chunk, columns), bf16),
            pltpu.VMEM((CHUNKS, 2, chunk, columns), bf16),
            pltpu.VMEM((CHUNKS, 2, chunk, columns), bf16),
            pltpu.VMEM((16, tokens, columns), bf16),
            dma((8,)),
            dma((2, nz)),
            dma((2, nz)),
            dma((2, nz)),
            dma((2, nz)),
            dma((2, 2)),
            dma((2, 2 + nz)),
            dma((2, nz)),
            dma((2, nz)),
            dma((2, 2, 16)),
            dma((2, 2 * CHUNKS)),
            dma((2 * CHUNKS, nz)),
            dma((2 * CHUNKS, nz)),
            dma((2, CHUNKS)),
            dma((CHUNKS, 2, 4)),
            dma((16,)),
        ],
        compiler_params=pltpu.CompilerParams(
            collective_id=0, has_side_effects=True, vmem_limit_bytes=60 * 2**20
        ),
        cost_estimate=pl.CostEstimate(flops=5 * 10**9, bytes_accessed=10**7, transcendentals=10**6),
        name="layer",
    )(
        queries,
        suffix_kv,
        prefix_kv,
        hyp_prefix,
        suffix_len,
        prefix_len,
        w_out,
        hidden_in,
        gain_attn.reshape(-1, 128),
        gain_pre.reshape(-1, 128),
        w_gate.T,
        w_up.T,
        w_down.T,
    )
    return resid, out


def solution(mesh):
    placed = (
        P("req", None),
        P("req", None),
        P(None, "req", None),
        P(None, "req", "ctx", None),
        P("req"),
        P("req"),
        P("req"),
        P("ctx", None),
        P(),
        P(),
        P(None, ("req", "ctx")),
        P(None, ("req", "ctx")),
        P("req", "ctx"),
    )
    return jax.shard_map(
        layer,
        mesh=mesh,
        in_specs=placed,
        out_specs=(P("req", None), P("req", "ctx")),
        check_vma=False,
    )
```

```python
import functools

import jax
import jax.numpy as jnp
from jax import lax
from jax.experimental import pallas as pl
from jax.experimental.pallas import tpu as pltpu
from jax.sharding import PartitionSpec as P

HEADS = 32
KV_HEADS = 16
HEAD = 128

softcap = 50.0
query_scale = 144.0 ** (-0.5)
eps = 1e-06

NT = (((1,), (1,)), ((), ()))
MESH = pl.DeviceIdType.MESH

ARRIVALS = (
    (((0, 1), (0, 1)), ((-1, 0), (-1, 0)), ((0, -1), (0, -1)), ((1, 0), (1, 0))),
    (((1, 1), (1, 0)), ((-1, 1), (0, 1)), ((-1, -1), (-1, 0)), ((1, -1), (0, -1))),
    (((2, 0), (1, 0)), ((0, 2), (0, 1)), ((2, -1), (-1, 0)), ((1, 2), (0, -1))),
    (((2, 1), (1, 0)), ((-1, 2), (0, 1)), ((2, 2), (0, -1))),
)
OFFSETS = ((0, 0),) + tuple(offset for step in ARRIVALS for offset, _ in step)
SLOT = {(dx % 4, dy % 4): i for i, (dx, dy) in enumerate(OFFSETS)}
CHUNKS = 4
FAR_FIRST = (4, 3, 5, 2, 6, 1, 7, 0)


def weights_of(scores):
    return jnp.exp(softcap * jnp.tanh(scores * (query_scale / softcap)))


def layer_kernel(
    queries_in,
    suffix_in,
    prefix_in,
    hyp_prefix,
    suffix_len,
    prefix_len,
    w_out_in,
    hidden_hbm,
    gain_attn_in,
    gain_pre_in,
    w_gate,
    w_up,
    w_down,
    resid_out,
    out,
    queries,
    suffix_kv,
    prefix_kv,
    w_out,
    hidden_in,
    gains,
    mask,
    party_send,
    party_recv,
    part_own,
    partz_send,
    partz_recv,
    proj_send,
    projy_recv,
    projz_send,
    projz_recv,
    slab_own,
    down_raw,
    down_rows,
    down_own,
    down_other,
    w_own,
    slabs,
    block,
    tok,
    sib_send,
    sib_recv,
    hid,
    ds_send,
    ds_recv,
    rs_send,
    rs_recv,
    load_sem,
    party_sem,
    partz_sem,
    projy_sem,
    projz_sem,
    resid_sem,
    w_sem,
    slab_ssem,
    slab_rsem,
    tok_sem,
    sib_sem,
    hid_ssem,
    hid_rsem,
    ds_sem,
    rs_ssem,
    rs_rsem,
):
    ctx, req = lax.axis_index("ctx"), lax.axis_index("req")
    z, y_lo = ctx // 2, lax.rem(ctx, 2)
    x, y_hi, core = req // 4, lax.rem(req // 2, 2), lax.rem(req, 2)
    y = y_hi * 2 + y_lo
    place = x * 4 + y
    n = 16
    nz = 8
    tokens = queries.shape[0]
    prefixes, positions = prefix_kv.shape[1], prefix_kv.shape[2]
    group = HEADS // KV_HEADS
    rows = group * tokens
    hyps = hyp_prefix.shape[0]
    suf = tokens // hyps
    slab = tokens // n
    width = w_out.shape[1]
    half = width // 2
    units = w_gate.shape[0]
    blocks = 16 // CHUNKS
    part = tokens // 2
    chunk = blocks * part
    partner = ctx + 1 - 2 * y_lo
    sibling = req + 1 - 2 * core

    def chip(dx, dy):
        there_y = lax.rem(y + dy + 4, 4)
        return z * 2 + lax.rem(there_y, 2), lax.rem(x + dx + 4, 4) * 4 + there_y // 2 * 2

    def along_z(dz):
        return lax.rem(z + dz + nz, nz)

    def remote(src, dst, ssem, rsem, **where):
        return pltpu.make_async_remote_copy(
            src_ref=src, dst_ref=dst, send_sem=ssem, recv_sem=rsem, device_id=where, device_id_type=MESH
        )

    mine = pl.ds(pl.multiple_of(core * half, half), half)
    others = pl.ds(pl.multiple_of((1 - core) * half, half), half)
    loads = [
        pltpu.make_async_copy(src, dst, load_sem.at[i])
        for i, (src, dst) in enumerate(
            (
                (queries_in, queries),
                (prefix_in, prefix_kv),
                (suffix_in, suffix_kv),
                (w_out_in, w_out),
                (hidden_hbm, hidden_in),
                (w_down, down_raw),
                (w_gate.at[:, mine], w_own.at[pl.ds(0, units), :]),
                (w_up.at[:, mine], w_own.at[pl.ds(units, units), :]),
            )
        )
    ]
    for load in loads:
        load.start()

    barrier = pltpu.get_barrier_semaphore()

    def greet(there_ctx, there_req):
        pl.semaphore_signal(barrier, inc=1, device_id={"ctx": there_ctx, "req": there_req}, device_id_type=MESH)

    def greet_z(s, _):
        greet(along_z(s) * 2 + y_lo, req)
        return 0

    def greet_core(s, _):
        greet(along_z(s) * 2 + y_lo, sibling)
        return 0

    def greet_plane(s, _):
        there = lax.rem(place + s, 16)
        there_ctx, there_req = z * 2 + lax.rem(there, 2), there // 2 * 2 + core

        @pl.when(there_req != req)
        def _():
            greet(there_ctx, there_req)

        return 0

    greet(partner, req)
    lax.fori_loop(1, nz, greet_z, 0)
    lax.fori_loop(0, nz, greet_core, 0)
    lax.fori_loop(1, 16, greet_plane, 0)

    row = lax.broadcasted_iota(jnp.int32, (rows, prefixes * positions), 0)
    col = lax.broadcasted_iota(jnp.int32, (rows, prefixes * positions), 1)
    hyp_of_row = lax.rem(row, tokens) // suf
    row_pid = jnp.zeros_like(row)
    for h in range(hyps):
        row_pid = jnp.where(hyp_of_row == h, hyp_prefix[h] - req * prefixes, row_pid)
    col_pid = col // positions
    col_len = jnp.zeros_like(row)
    for p in range(prefixes):
        col_len = jnp.where(col_pid == p, prefix_len[p], col_len)
    ok = (row_pid == col_pid) & (ctx * positions + lax.rem(col, positions) < col_len)
    mask[...] = jnp.where(ok, 1.0, 0.0)
    eye = lax.broadcasted_iota(jnp.int32, (rows, rows), 0) == lax.broadcasted_iota(jnp.int32, (rows, rows), 1)
    for k in range(width // 128):
        gains[0:1, k * 128 : (k + 1) * 128] = gain_attn_in[k : k + 1, :]
    for k in range(half // 128):
        gains[1:2, k * 128 : (k + 1) * 128] = jnp.where(
            core == 0, gain_pre_in[k : k + 1, :], gain_pre_in[half // 128 + k : half // 128 + k + 1, :]
        )

    def query_rows(head):
        both = queries[:, pl.ds(pl.multiple_of(head * (group * HEAD), group * HEAD), group * HEAD)]
        return jnp.concatenate([both[:, g * HEAD : (g + 1) * HEAD] for g in range(group)], 0)

    def partial_of(head):
        lanes = pl.ds(pl.multiple_of(head * HEAD, HEAD), HEAD)
        query = query_rows(head)
        keys = prefix_kv[0, :, :, lanes].reshape(prefixes * positions, HEAD)
        vals = prefix_kv[1, :, :, lanes].reshape(prefixes * positions, HEAD)
        scores = lax.dot_general(query, keys, NT, preferred_element_type=jnp.float32)
        weights = jnp.where(mask[...] > 0.5, weights_of(scores), 0.0)
        summed = jnp.dot(weights.astype(jnp.bfloat16), vals, preferred_element_type=jnp.float32)
        total = jnp.sum(weights, 1, keepdims=True)
        return summed, jnp.sum(jnp.where(eye, total, 0.0), 0, keepdims=True)

    def store_partial(ref, summed, flat):
        high = flat.astype(jnp.bfloat16).astype(jnp.float32)
        low = flat - high
        line = lax.broadcasted_iota(jnp.int32, (16, rows), 0)
        ref[0:rows, :] = summed.astype(jnp.bfloat16)
        ref[rows : rows + 16, :] = jnp.where(line == 0, high, jnp.where(line == 1, low, 0.0)).astype(jnp.bfloat16)

    def load_partial(ref):
        return (
            ref[0:rows, :].astype(jnp.float32),
            jnp.sum(ref[rows : rows + 16, :].astype(jnp.float32), 0, keepdims=True),
        )

    def distance(i):
        step = (i + 1) // 2
        return nz // 2 + step * (1 - 2 * lax.rem(i, 2))

    at_once = 4

    def others_heads(s, _):
        which = [distance(s * at_once + i) for i in range(at_once)]
        terms = [partial_of(along_z(dz) * 2 + 1 - y_lo) for dz in which]
        for dz, term in zip(which, terms):
            store_partial(party_send.at[dz], *term)
        return 0

    def own_heads(s, _):
        which = [distance(s * at_once + i) for i in range(at_once)]
        terms = [partial_of(along_z(dz) * 2 + y_lo) for dz in which]
        for dz, (summed, flat) in zip(which, terms):
            part_own[dz, 0:rows, :] = summed
            part_own[dz, rows : rows + 8, :] = jnp.broadcast_to(flat, (8, rows))
        return 0

    def party_copy(dz):
        return remote(party_send.at[dz], party_recv.at[dz], party_sem.at[0, dz], party_sem.at[1, dz], ctx=partner)

    def partz_copy(dz):
        return remote(
            partz_send.at[dz],
            partz_recv.at[dz],
            partz_sem.at[0, dz],
            partz_sem.at[1, dz],
            ctx=along_z(dz) * 2 + y_lo,
        )

    loads[0].wait()
    loads[1].wait()
    lax.fori_loop(0, nz // at_once, others_heads, 0)
    pl.semaphore_wait(barrier, 1 + (nz - 1) + nz + 14)
    for dz in FAR_FIRST:
        party_copy(dz).start()

    w_copies = [
        remote(
            src.at[:, others],
            w_own.at[pl.ds((2 + i) * units, units), :],
            w_sem.at[0, i],
            w_sem.at[1, i],
            req=sibling,
        )
        for i, src in enumerate((w_gate, w_up))
    ]
    for copy in w_copies:
        copy.start()
    lax.fori_loop(0, nz // at_once, own_heads, 0)

    own = pl.ds(pl.multiple_of(ctx * HEAD, HEAD), HEAD)
    suf_row = lax.rem(lax.broadcasted_iota(jnp.int32, (rows, tokens), 0), tokens)
    suf_col = lax.broadcasted_iota(jnp.int32, (rows, tokens), 1)
    row_hyp, col_hyp = suf_row // suf, suf_col // suf
    length = jnp.zeros_like(suf_row)
    for h in range(hyps):
        length = jnp.where(col_hyp == h, suffix_len[h], length)
    usable = (row_hyp == col_hyp) & (suf_col <= suf_row) & (suf_col - col_hyp * suf < length)
    loads[2].wait()
    scores = lax.dot_general(query_rows(ctx), suffix_kv[0, :, own], NT, preferred_element_type=jnp.float32)
    weights = jnp.where(usable, weights_of(scores), 0.0)
    suf_sum = jnp.dot(weights.astype(jnp.bfloat16), suffix_kv[1, :, own], preferred_element_type=jnp.float32)
    suf_total = jnp.sum(weights, 1, keepdims=True)

    loads[5].wait()
    tile = 128
    unit = (
        lax.broadcasted_iota(jnp.int32, (tile, tile), 0) == lax.broadcasted_iota(jnp.int32, (tile, tile), 1)
    ).astype(jnp.bfloat16)
    for k in range(0, down_raw.shape[1], tile):
        down_rows[k : k + tile, :] = lax.dot_general(
            unit, down_raw[:, k : k + tile], NT, preferred_element_type=jnp.float32
        ).astype(jnp.bfloat16)
    down_copies = [
        remote(
            down_rows.at[pl.ds(pl.multiple_of((2 * s + 1 - y_lo) * units, units), units), :],
            down_other.at[pl.ds(s * units, units), :],
            w_sem.at[0, 2 + s],
            w_sem.at[1, 2 + s],
            ctx=partner,
        )
        for s in range(nz)
    ]
    for s in range(nz):
        down_own[s * units : (s + 1) * units, :] = down_rows[
            pl.ds(pl.multiple_of((2 * s + y_lo) * units, units), units), :
        ]

    for dz in FAR_FIRST[:-1]:
        party_copy(dz).wait_recv()
        summed, flat = load_partial(party_recv.at[dz])
        store_partial(
            partz_send.at[dz], summed + part_own[dz, 0:rows, :], flat + part_own[dz, rows : rows + 1, :]
        )
        partz_copy(dz).start()

    for copy in down_copies[:2]:
        copy.start()

    party_copy(0).wait_recv()
    summed, flat = load_partial(party_recv.at[0])
    summed += part_own[0, 0:rows, :] + suf_sum
    flat += part_own[0, rows : rows + 1, :]
    for dz in FAR_FIRST[:-1]:
        partz_copy(dz).wait_recv()
        more, more_flat = load_partial(partz_recv.at[dz])
        summed += more
        flat += more_flat
    total = suf_total + jnp.sum(jnp.where(eye, flat, 0.0), 1, keepdims=True)
    attn = (summed / total).astype(jnp.bfloat16)
    attn = jnp.concatenate([attn[g * tokens : (g + 1) * tokens] for g in range(group)], 1)

    loads[3].wait()
    step = 512
    for c in range(0, width, step):
        term = jnp.dot(attn, w_out[:, c : c + step], preferred_element_type=jnp.float32)
        for i in range(n):
            proj_send[i, :, c : c + step] = term[i * slab : (i + 1) * slab].astype(jnp.bfloat16)

    def projy_copy(dz):
        return remote(
            proj_send.at[(1 - y_lo) * nz + along_z(dz)],
            projy_recv.at[dz],
            projy_sem.at[0, dz],
            projy_sem.at[1, dz],
            ctx=partner,
        )

    def projz_copy(dz):
        return remote(
            projz_send.at[dz],
            projz_recv.at[dz],
            projz_sem.at[0, dz],
            projz_sem.at[1, dz],
            ctx=along_z(dz) * 2 + y_lo,
        )

    for dz in FAR_FIRST:
        projy_copy(dz).start()

    first = y_lo * nz + z
    loads[4].wait()
    around = hidden_in[pl.ds(pl.multiple_of(first * slab // 16 * 16, 16), 16), :].astype(jnp.float32)
    before = jnp.zeros((slab, width), jnp.float32)
    for g in range(16 // slab):
        before = jnp.where(lax.rem(first, 16 // slab) == g, around[g * slab : (g + 1) * slab], before)

    for dz in FAR_FIRST[:-1]:
        projy_copy(dz).wait_recv()
        both = projy_recv[dz].astype(jnp.float32) + proj_send[y_lo * nz + along_z(dz)].astype(jnp.float32)
        projz_send[dz] = both.astype(jnp.bfloat16)
        projz_copy(dz).start()

    for copy in down_copies[2:]:
        copy.start()

    for copy in w_copies:
        copy.wait()
    loads[6].wait()
    loads[7].wait()

    def gain_rows(i, _):
        at = pl.ds(pl.multiple_of(i * 16, 16), 16)
        w_own[at, :] = (w_own[at, :].astype(jnp.float32) * gains[1:2, :half]).astype(jnp.bfloat16)
        return 0

    lax.fori_loop(0, 4 * units // 16, gain_rows, 0)

    projy_copy(0).wait_recv()
    proj = projy_recv[0].astype(jnp.float32) + proj_send[first].astype(jnp.float32)
    for dz in FAR_FIRST[:-1]:
        projz_copy(dz).wait_recv()
        proj += projz_recv[dz].astype(jnp.float32)
    scale_a = lax.rsqrt(jnp.mean(proj * proj, 1, keepdims=True) + eps)
    resid = (before + gains[0:1, :] * proj * scale_a).astype(jnp.bfloat16)
    for h in range(2):
        slab_own[h] = resid[:, h * half : (h + 1) * half]

    def slab_copy(to_z, to_core, from_z, from_core):
        return remote(
            slab_own.at[to_core],
            slabs.at[from_core, from_z],
            slab_ssem.at[to_core, to_z],
            slab_rsem.at[from_core, from_z],
            ctx=to_z * 2 + y_lo,
            req=req - core + to_core,
        )

    def send_slabs():
        for dz in FAR_FIRST[:-1]:
            slab_copy(along_z(dz), core, z, core).start()
            slab_copy(along_z(dz), 1 - core, z, core).start()

    def near_slabs():
        for dz in (1, -1):
            slab_copy(along_z(dz), core, along_z(dz), 0).wait_recv()

    slabs[core, z] = slab_own[core]
    slab_copy(z, 1 - core, z, core).start()

    @pl.when(core == 0)
    def _():
        send_slabs()
        near_slabs()

    @pl.when(core == 1)
    def _():
        near_slabs()
        send_slabs()

    def gather_slabs(c):
        for dz in FAR_FIRST[:-1] if c == 1 else (4, 3, 5, 2, 6):
            slab_copy(along_z(dz), core, along_z(dz), c).wait_recv()

        @pl.when(core != c)
        def _():
            slab_copy(z, core, z, c).wait_recv()

        for s in range(nz):
            at = (c * nz + s) * slab
            block[at : at + slab, :] = slabs[c, s].astype(jnp.float32)
        tok[c, 0] = block[c * part : (c + 1) * part, :].astype(jnp.bfloat16)

    def tok_copy(offset, link, sub):
        source = SLOT[(offset[0] - link[0]) % 4, (offset[1] - link[1]) % 4]
        slot = SLOT[offset[0] % 4, offset[1] % 4]
        there_ctx, there_req = chip(-link[0], -link[1])
        return remote(
            tok.at[sub, source],
            tok.at[sub, slot],
            tok_sem.at[0, sub, slot],
            tok_sem.at[1, sub, slot],
            ctx=there_ctx,
            req=there_req + core,
        )

    def token_step(step, sub):
        later_copies = []
        if step + 1 < len(ARRIVALS):
            for offset, link in ARRIVALS[step + 1]:
                source = SLOT[(offset[0] - link[0]) % 4, (offset[1] - link[1]) % 4]
                later_copies.append((source, tok_copy(offset, link, sub)))
        for offset, link in ARRIVALS[step]:
            tok_copy(offset, link, sub).wait_recv()
            for source, copy in later_copies:
                if source == SLOT[offset[0] % 4, offset[1] % 4]:
                    copy.start()
        for source, copy in later_copies:
            if source <= 4 * step:
                copy.start()

    def sib_copy(i):
        return remote(sib_send.at[i], sib_recv.at[i], sib_sem.at[0, i], sib_sem.at[1, i], req=sibling)

    own_part = {}
    ones = jnp.ones((16, half), jnp.bfloat16)

    def gate_up(i):
        those = tok[i % 2, i // 2 * blocks : (i // 2 + 1) * blocks].reshape(chunk, half)
        squares = lax.dot_general(ones, those * those, NT, preferred_element_type=jnp.float32)[:8]
        sib_send[i, 2 * units :] = squares
        sib_send[i, : 2 * units] = lax.dot_general(
            w_own[2 * units :, :], those, NT, preferred_element_type=jnp.float32
        )
        sib_copy(i).start()
        products = lax.dot_general(w_own[: 2 * units, :], those, NT, preferred_element_type=jnp.float32)
        own_part[i] = products, squares

    major = 1 - 2 * core

    def hid_copy(i, origin, to):
        source = along_z(origin)
        ref = hid.at[i // 2, source, i % 2]
        return remote(
            ref,
            ref,
            hid_ssem.at[i, lax.rem(to - origin + 2 * nz, nz)],
            hid_rsem.at[i, source],
            ctx=along_z(to) * 2 + y_lo,
        )

    def hidden(i):
        sib_copy(i).wait_recv()
        products, squares = own_part[i]
        both = products + sib_recv[i, : 2 * units]
        scale = lax.rsqrt((squares + sib_recv[i, 2 * units :])[0:1] * (1.0 / width) + eps)
        act = jax.nn.gelu(both[:units] * scale, approximate=True) * (both[units:] * scale)
        hid[i // 2, z, i % 2] = act.astype(jnp.bfloat16)
        for to in (2, -2, 1, -1):
            hid_copy(i, 0, to).start()

    def pass_on(i):
        for way in (1, -1):
            hid_copy(i, -2 * way, 0).wait_recv()

            @pl.when(major == way)
            def _():
                hid_copy(i, -2 * way, 2 * way).start()

            hid_copy(i, -2 * way, way).start()

    def hid_arrive(i):
        for origin in (-1, 1, -3, 3, 4):
            hid_copy(i, origin, 0).wait_recv()

    def hid_sent(i):
        for way in (1, -1):
            for away in (1, 2, 3):
                hid_copy(i, 0, way * away).wait_send()

            @pl.when(major == way)
            def _():
                hid_copy(i, 0, way * 4).wait_send()

    def ds_copy(g):
        return remote(ds_send.at[g], ds_recv.at[g], ds_sem.at[0, g], ds_sem.at[1, g], req=sibling)

    def down_terms(g, c):
        act = hid[g, :, c].reshape(nz * units, chunk).T
        return [
            jnp.dot(act, matrix[...], preferred_element_type=jnp.float32) for matrix in (down_own, down_other)
        ]

    def down(g):
        for i in (2 * g, 2 * g + 1):
            hid_arrive(i)
        for side, term in enumerate(down_terms(g, 1 - core)):
            ds_send[g, side] = term.astype(jnp.bfloat16)
        ds_copy(g).start()
        return down_terms(g, core)

    def rs_copy(g, b, side):
        dx, dy = OFFSETS[g * blocks + b]
        block_ctx, first_req = chip(dx, dy)
        lo = lax.rem(block_ctx, 2)
        to_ctx = ctx if side == 0 else partner
        possible = side == 0 and dx == 0 and dy in (0, 1, -1)
        copy = remote(
            rs_send.at[g, side, pl.ds(b * part, part), :],
            rs_recv.at[place, pl.ds(pl.multiple_of(lo * part, part), part), :],
            rs_ssem.at[g, side, b],
            rs_rsem.at[place],
            ctx=to_ctx,
            req=first_req + core,
        )
        return copy, lo, (first_req + core == req) if possible else None

    def send_terms(g, terms):
        ds_copy(g).wait_recv()
        for side in range(2):
            rs_send[g, side] = (terms[side] + ds_recv[g, side].astype(jnp.float32)).astype(jnp.bfloat16)
        for b in range(blocks):
            for side in (1, 0):
                copy, lo, here = rs_copy(g, b, side)
                if here is None:
                    copy.start()
                else:

                    @pl.when(here)
                    def _():
                        rs_recv[place, pl.ds(pl.multiple_of(lo * part, part), part), :] = rs_send[
                            g, side, pl.ds(b * part, part), :
                        ]

                    @pl.when(jnp.logical_not(here))
                    def _():
                        copy.start()

    def terms_sent(g):
        for b in range(blocks):
            for side in range(2):
                copy, lo, here = rs_copy(g, b, side)
                if here is None:
                    copy.wait_send()
                else:

                    @pl.when(jnp.logical_not(here))
                    def _():
                        copy.wait_send()

    for sub in range(2):
        gather_slabs(sub)
        for offset, link in ARRIVALS[0]:
            tok_copy(offset, link, sub).start()
    for dz in FAR_FIRST:
        party_copy(dz).wait_send()
        projy_copy(dz).wait_send()
    for dz in FAR_FIRST[:-1]:
        partz_copy(dz).wait_send()
        projz_copy(dz).wait_send()

    def tok_sent(step, sub):
        for offset, link in ARRIVALS[step]:
            tok_copy(offset, link, sub).wait_send()

    def slabs_sent():
        for dz in FAR_FIRST[:-1]:
            slab_copy(along_z(dz), core, z, core).wait_send()
            slab_copy(along_z(dz), 1 - core, z, core).wait_send()
        slab_copy(z, 1 - core, z, core).wait_send()

    for i in range(2 * CHUNKS):
        token_step(i // 2, i % 2)
        if i >= 2:
            pass_on(i - 2)
        gate_up(i)
        hidden(i)
        if i == 1:
            slabs_sent()
        if i >= 2:
            tok_sent((i - 2) // 2, i % 2)
            sib_copy(i - 2).wait_send()
        if i >= 5:
            hid_sent(i - 5)
        if i == 6:
            for copy in down_copies:
                copy.wait()
            first_terms = down(0)
    send_terms(0, first_terms)
    terms = down(1)
    pass_on(6)
    send_terms(1, terms)
    terms = down(2)
    pass_on(7)
    send_terms(2, terms)
    for sub in range(2):
        tok_sent(3, sub)
    for i in (6, 7):
        sib_copy(i).wait_send()
    for i in (3, 4, 5):
        hid_sent(i)
    for g in range(3):
        ds_copy(g).wait_send()

    def resid_copy(i):
        lo, slot = (y_lo, 0) if i == 0 else (1 - y_lo, 1 + 2 * y_lo)
        return remote(
            tok.at[1 - core, slot],
            resid_out.at[pl.ds(pl.multiple_of(lo * part, part), part), mine],
            resid_sem.at[0, i],
            resid_sem.at[1, i],
            req=sibling,
        )

    for i in range(2):
        resid_copy(i).start()
        lo, slot = (y_lo, 0) if i == 0 else (1 - y_lo, 1 + 2 * y_lo)
        resid_out[pl.ds(pl.multiple_of(lo * part, part), part), mine] = tok[core, slot]

    for i in (6, 7):
        hid_arrive(i)
        terms = down_terms(3, i % 2)

        @pl.when(core != i % 2)
        def _():
            for side in range(2):
                ds_send[3, side] = terms[side].astype(jnp.bfloat16)
            ds_copy(3).start()

        @pl.when(core == i % 2)
        def _():
            send_terms(3, terms)

    for i in (6, 7):
        hid_sent(i)
    ds_copy(3).wait_send()
    for i in range(2):
        resid_copy(i).wait()
    for g in range(CHUNKS):
        terms_sent(g)

    def add_terms(s, total):
        there = lax.rem(place + s, 16)
        remote(
            rs_recv.at[there],
            rs_recv.at[there],
            rs_ssem.at[0, 0, 0],
            rs_rsem.at[there],
            ctx=z * 2 + lax.rem(there, 2),
            req=there // 2 * 2 + core,
        ).wait_recv()
        return total + rs_recv[there].astype(jnp.float32)

    total = lax.fori_loop(1, 16, add_terms, rs_recv[place].astype(jnp.float32))
    out[...] = total.astype(jnp.bfloat16)


def place_kernel(resid, out, resid_out, out_out, held, small, sem):
    rows = resid.shape[0] // 4
    loads, stores = [], []
    for i in range(4):
        at = pl.ds(i * rows, rows)
        loads.append(pltpu.make_async_copy(resid.at[at, :], held.at[at, :], sem.at[0, i]))
        stores.append(pltpu.make_async_copy(held.at[at, :], resid_out.at[at, :], sem.at[1, i]))
    loads.append(pltpu.make_async_copy(out, small, sem.at[0, 4]))
    stores.append(pltpu.make_async_copy(small, out_out, sem.at[1, 4]))
    for load in loads:
        load.start()
    for load, store in zip(loads, stores):
        load.wait()
        store.start()
    for store in stores:
        store.wait()


def layer(
    hidden_in,
    queries,
    suffix_kv,
    prefix_kv,
    hyp_prefix,
    suffix_len,
    prefix_len,
    w_out,
    gain_attn,
    gain_pre,
    w_gate,
    w_up,
    w_down,
):
    n = 16
    nz = 8
    tokens, width = hidden_in.shape
    half = width // 2
    rows = HEADS // KV_HEADS * tokens
    slab = tokens // n
    positions = prefix_kv.shape[1] * prefix_kv.shape[2]
    units = w_gate.shape[1]
    columns = w_down.shape[1]
    chunk = 16 // CHUNKS * tokens // 2
    vmem = pl.BlockSpec(memory_space=pltpu.VMEM)
    smem = pl.BlockSpec(memory_space=pltpu.SMEM)
    hbm = pl.BlockSpec(memory_space=pl.ANY)
    dma = pltpu.SemaphoreType.DMA
    bf16 = jnp.bfloat16
    resid, out = pl.pallas_call(
        layer_kernel,
        out_shape=(
            jax.ShapeDtypeStruct((tokens, width), bf16),
            jax.ShapeDtypeStruct((tokens, columns), bf16),
        ),
        in_specs=[hbm, hbm, hbm, smem, smem, smem, hbm, hbm, vmem, vmem, hbm, hbm, hbm],
        out_specs=(vmem, vmem),
        scratch_shapes=[
            pltpu.VMEM(queries.shape, bf16),
            pltpu.VMEM(suffix_kv.shape, bf16),
            pltpu.VMEM(prefix_kv.shape, bf16),
            pltpu.VMEM(w_out.shape, bf16),
            pltpu.VMEM(hidden_in.shape, bf16),
            pltpu.VMEM((2, width), jnp.float32),
            pltpu.VMEM((rows, positions), jnp.float32),
            pltpu.VMEM((nz, rows + 16, HEAD), bf16),
            pltpu.VMEM((nz, rows + 16, HEAD), bf16),
            pltpu.VMEM((nz, rows + 8, HEAD), jnp.float32),
            pltpu.VMEM((nz, rows + 16, HEAD), bf16),
            pltpu.VMEM((nz, rows + 16, HEAD), bf16),
            pltpu.VMEM((n, slab, width), bf16),
            pltpu.VMEM((nz, slab, width), bf16),
            pltpu.VMEM((nz, slab, width), bf16),
            pltpu.VMEM((nz, slab, width), bf16),
            pltpu.VMEM((2, slab, half), bf16),
            pltpu.VMEM((columns, n * units), bf16),
            pltpu.VMEM((n * units, columns), bf16),
            pltpu.VMEM((nz * units, columns), bf16),
            pltpu.VMEM((nz * units, columns), bf16),
            pltpu.VMEM((4 * units, half), bf16),
            pltpu.VMEM((2, nz, slab, half), bf16),
            pltpu.VMEM((tokens, half), jnp.float32),
            pltpu.VMEM((2, 16, tokens // 2, half), bf16),
            pltpu.VMEM((2 * CHUNKS, 2 * units + 8, chunk), jnp.float32),
            pltpu.VMEM((2 * CHUNKS, 2 * units + 8, chunk), jnp.float32),
            pltpu.VMEM((CHUNKS, nz, 2, units, chunk), bf16),
            pltpu.VMEM((CHUNKS, 2, chunk, columns), bf16),
            pltpu.VMEM((CHUNKS, 2, chunk, columns), bf16),
            pltpu.VMEM((CHUNKS, 2, chunk, columns), bf16),
            pltpu.VMEM((16, tokens, columns), bf16),
            dma((8,)),
            dma((2, nz)),
            dma((2, nz)),
            dma((2, nz)),
            dma((2, nz)),
            dma((2, 2)),
            dma((2, 2 + nz)),
            dma((2, nz)),
            dma((2, nz)),
            dma((2, 2, 16)),
            dma((2, 2 * CHUNKS)),
            dma((2 * CHUNKS, nz)),
            dma((2 * CHUNKS, nz)),
            dma((2, CHUNKS)),
            dma((CHUNKS, 2, 4)),
            dma((16,)),
        ],
        compiler_params=pltpu.CompilerParams(
            collective_id=0, has_side_effects=True, vmem_limit_bytes=60 * 2**20
        ),
        cost_estimate=pl.CostEstimate(flops=5 * 10**9, bytes_accessed=10**7, transcendentals=10**6),
        name="layer",
    )(
        queries,
        suffix_kv,
        prefix_kv,
        hyp_prefix,
        suffix_len,
        prefix_len,
        w_out,
        hidden_in,
        gain_attn.reshape(-1, 128),
        gain_pre.reshape(-1, 128),
        w_gate.T,
        w_up.T,
        w_down.T,
    )
    return pl.pallas_call(
        place_kernel,
        out_shape=(jax.ShapeDtypeStruct(resid.shape, bf16), jax.ShapeDtypeStruct(out.shape, bf16)),
        in_specs=[hbm, hbm],
        out_specs=(hbm, hbm),
        scratch_shapes=[pltpu.VMEM(resid.shape, bf16), pltpu.VMEM(out.shape, bf16), dma((2, 5))],
        name="place",
    )(resid, out)


def solution(mesh):
    placed = (
        P("req", None),
        P("req", None),
        P(None, "req", None),
        P(None, "req", "ctx", None),
        P("req"),
        P("req"),
        P("req"),
        P("ctx", None),
        P(),
        P(),
        P(None, ("req", "ctx")),
        P(None, ("req", "ctx")),
        P("req", "ctx"),
    )
    return jax.shard_map(
        layer,
        mesh=mesh,
        in_specs=placed,
        out_specs=(P("req", None), P("req", "ctx")),
        check_vma=False,
    )
```

```python
import functools

import jax
import jax.numpy as jnp
from jax import lax
from jax.experimental import pallas as pl
from jax.experimental.pallas import tpu as pltpu
from jax.sharding import PartitionSpec as P

HEADS = 32
KV_HEADS = 16
HEAD = 128

softcap = 50.0
query_scale = 144.0 ** (-0.5)
eps = 1e-06

NT = (((1,), (1,)), ((), ()))
MESH = pl.DeviceIdType.MESH

ARRIVALS = (
    (((0, 1), (0, 1)), ((-1, 0), (-1, 0)), ((0, -1), (0, -1)), ((1, 0), (1, 0))),
    (((1, 1), (1, 0)), ((-1, 1), (0, 1)), ((-1, -1), (-1, 0)), ((1, -1), (0, -1))),
    (((2, 0), (1, 0)), ((0, 2), (0, 1)), ((2, -1), (-1, 0)), ((1, 2), (0, -1))),
    (((2, 1), (1, 0)), ((-1, 2), (0, 1)), ((2, 2), (0, -1))),
)
OFFSETS = ((0, 0),) + tuple(offset for step in ARRIVALS for offset, _ in step)
SLOT = {(dx % 4, dy % 4): i for i, (dx, dy) in enumerate(OFFSETS)}
CHUNKS = 4
FAR_FIRST = (4, 3, 5, 2, 6, 1, 7, 0)


def weights_of(scores):
    return jnp.exp(softcap * jnp.tanh(scores * (query_scale / softcap)))


def layer_kernel(
    queries_in,
    suffix_in,
    prefix_in,
    hyp_prefix,
    suffix_len,
    prefix_len,
    w_out_in,
    hidden_hbm,
    gain_attn_in,
    gain_pre_in,
    w_gate,
    w_up,
    w_down,
    resid_out,
    out,
    queries,
    suffix_kv,
    prefix_kv,
    w_out,
    hidden_in,
    gains,
    mask,
    party_send,
    party_recv,
    part_own,
    partz_send,
    partz_recv,
    proj_send,
    projy_recv,
    projz_send,
    projz_recv,
    slab_own,
    down_raw,
    down_rows,
    down_own,
    down_other,
    w_own,
    slabs,
    block,
    tok,
    sib_send,
    sib_recv,
    hid,
    ds_send,
    ds_recv,
    rs_send,
    rs_recv,
    load_sem,
    party_sem,
    partz_sem,
    projy_sem,
    projz_sem,
    resid_sem,
    w_sem,
    slab_ssem,
    slab_rsem,
    tok_sem,
    sib_sem,
    hid_ssem,
    hid_rsem,
    ds_sem,
    rs_ssem,
    rs_rsem,
):
    ctx, req = lax.axis_index("ctx"), lax.axis_index("req")
    z, y_lo = ctx // 2, lax.rem(ctx, 2)
    x, y_hi, core = req // 4, lax.rem(req // 2, 2), lax.rem(req, 2)
    y = y_hi * 2 + y_lo
    place = x * 4 + y
    n = 16
    nz = 8
    tokens = queries.shape[0]
    prefixes, positions = prefix_kv.shape[1], prefix_kv.shape[2]
    group = HEADS // KV_HEADS
    rows = group * tokens
    hyps = hyp_prefix.shape[0]
    suf = tokens // hyps
    slab = tokens // n
    width = w_out.shape[1]
    half = width // 2
    units = w_gate.shape[0]
    blocks = 16 // CHUNKS
    part = tokens // 2
    chunk = blocks * part
    partner = ctx + 1 - 2 * y_lo
    sibling = req + 1 - 2 * core

    def chip(dx, dy):
        there_y = lax.rem(y + dy + 4, 4)
        return z * 2 + lax.rem(there_y, 2), lax.rem(x + dx + 4, 4) * 4 + there_y // 2 * 2

    def along_z(dz):
        return lax.rem(z + dz + nz, nz)

    def remote(src, dst, ssem, rsem, **where):
        return pltpu.make_async_remote_copy(
            src_ref=src, dst_ref=dst, send_sem=ssem, recv_sem=rsem, device_id=where, device_id_type=MESH
        )

    mine = pl.ds(pl.multiple_of(core * half, half), half)
    others = pl.ds(pl.multiple_of((1 - core) * half, half), half)
    loads = [
        pltpu.make_async_copy(src, dst, load_sem.at[i])
        for i, (src, dst) in enumerate(
            (
                (queries_in, queries),
                (prefix_in, prefix_kv),
                (suffix_in, suffix_kv),
                (w_out_in, w_out),
                (hidden_hbm, hidden_in),
                (w_down, down_raw),
                (w_gate.at[:, mine], w_own.at[pl.ds(0, units), :]),
                (w_up.at[:, mine], w_own.at[pl.ds(units, units), :]),
            )
        )
    ]
    for load in loads:
        load.start()

    barrier = pltpu.get_barrier_semaphore()

    def greet(there_ctx, there_req):
        pl.semaphore_signal(barrier, inc=1, device_id={"ctx": there_ctx, "req": there_req}, device_id_type=MESH)

    def greet_z(s, _):
        greet(along_z(s) * 2 + y_lo, req)
        return 0

    def greet_core(s, _):
        greet(along_z(s) * 2 + y_lo, sibling)
        return 0

    def greet_plane(s, _):
        there = lax.rem(place + s, 16)
        there_ctx, there_req = z * 2 + lax.rem(there, 2), there // 2 * 2 + core

        @pl.when(there_req != req)
        def _():
            greet(there_ctx, there_req)

        return 0

    greet(partner, req)
    lax.fori_loop(1, nz, greet_z, 0)
    lax.fori_loop(0, nz, greet_core, 0)
    lax.fori_loop(1, 16, greet_plane, 0)

    row = lax.broadcasted_iota(jnp.int32, (rows, prefixes * positions), 0)
    col = lax.broadcasted_iota(jnp.int32, (rows, prefixes * positions), 1)
    hyp_of_row = lax.rem(row, tokens) // suf
    row_pid = jnp.zeros_like(row)
    for h in range(hyps):
        row_pid = jnp.where(hyp_of_row == h, hyp_prefix[h] - req * prefixes, row_pid)
    col_pid = col // positions
    col_len = jnp.zeros_like(row)
    for p in range(prefixes):
        col_len = jnp.where(col_pid == p, prefix_len[p], col_len)
    ok = (row_pid == col_pid) & (ctx * positions + lax.rem(col, positions) < col_len)
    mask[...] = jnp.where(ok, 1.0, 0.0)
    eye = lax.broadcasted_iota(jnp.int32, (rows, rows), 0) == lax.broadcasted_iota(jnp.int32, (rows, rows), 1)
    for k in range(width // 128):
        gains[0:1, k * 128 : (k + 1) * 128] = gain_attn_in[k : k + 1, :]
    for k in range(half // 128):
        gains[1:2, k * 128 : (k + 1) * 128] = jnp.where(
            core == 0, gain_pre_in[k : k + 1, :], gain_pre_in[half // 128 + k : half // 128 + k + 1, :]
        )

    def query_rows(head):
        both = queries[:, pl.ds(pl.multiple_of(head * (group * HEAD), group * HEAD), group * HEAD)]
        return jnp.concatenate([both[:, g * HEAD : (g + 1) * HEAD] for g in range(group)], 0)

    def partial_of(head):
        lanes = pl.ds(pl.multiple_of(head * HEAD, HEAD), HEAD)
        query = query_rows(head)
        keys = prefix_kv[0, :, :, lanes].reshape(prefixes * positions, HEAD)
        vals = prefix_kv[1, :, :, lanes].reshape(prefixes * positions, HEAD)
        scores = lax.dot_general(query, keys, NT, preferred_element_type=jnp.float32)
        weights = jnp.where(mask[...] > 0.5, weights_of(scores), 0.0)
        summed = jnp.dot(weights.astype(jnp.bfloat16), vals, preferred_element_type=jnp.float32)
        total = jnp.sum(weights, 1, keepdims=True)
        return summed, jnp.sum(jnp.where(eye, total, 0.0), 0, keepdims=True)

    def store_partial(ref, summed, flat):
        high = flat.astype(jnp.bfloat16).astype(jnp.float32)
        low = flat - high
        line = lax.broadcasted_iota(jnp.int32, (16, rows), 0)
        ref[0:rows, :] = summed.astype(jnp.bfloat16)
        ref[rows : rows + 16, :] = jnp.where(line == 0, high, jnp.where(line == 1, low, 0.0)).astype(jnp.bfloat16)

    def load_partial(ref):
        return (
            ref[0:rows, :].astype(jnp.float32),
            jnp.sum(ref[rows : rows + 16, :].astype(jnp.float32), 0, keepdims=True),
        )

    def distance(i):
        step = (i + 1) // 2
        return nz // 2 + step * (1 - 2 * lax.rem(i, 2))

    at_once = 4

    def others_heads(s, _):
        which = [distance(s * at_once + i) for i in range(at_once)]
        terms = [partial_of(along_z(dz) * 2 + 1 - y_lo) for dz in which]
        for dz, term in zip(which, terms):
            store_partial(party_send.at[dz], *term)
        return 0

    def own_heads(s, _):
        which = [distance(s * at_once + i) for i in range(at_once)]
        terms = [partial_of(along_z(dz) * 2 + y_lo) for dz in which]
        for dz, (summed, flat) in zip(which, terms):
            part_own[dz, 0:rows, :] = summed
            part_own[dz, rows : rows + 8, :] = jnp.broadcast_to(flat, (8, rows))
        return 0

    def party_copy(dz):
        return remote(party_send.at[dz], party_recv.at[dz], party_sem.at[0, dz], party_sem.at[1, dz], ctx=partner)

    def partz_copy(dz):
        return remote(
            partz_send.at[dz],
            partz_recv.at[dz],
            partz_sem.at[0, dz],
            partz_sem.at[1, dz],
            ctx=along_z(dz) * 2 + y_lo,
        )

    loads[0].wait()
    loads[1].wait()
    lax.fori_loop(0, nz // at_once, others_heads, 0)
    pl.semaphore_wait(barrier, 1 + (nz - 1) + nz + 14)
    for dz in FAR_FIRST:
        party_copy(dz).start()

    w_copies = [
        remote(
            src.at[:, others],
            w_own.at[pl.ds((2 + i) * units, units), :],
            w_sem.at[0, i],
            w_sem.at[1, i],
            req=sibling,
        )
        for i, src in enumerate((w_gate, w_up))
    ]
    for copy in w_copies:
        copy.start()
    lax.fori_loop(0, nz // at_once, own_heads, 0)

    own = pl.ds(pl.multiple_of(ctx * HEAD, HEAD), HEAD)
    suf_row = lax.rem(lax.broadcasted_iota(jnp.int32, (rows, tokens), 0), tokens)
    suf_col = lax.broadcasted_iota(jnp.int32, (rows, tokens), 1)
    row_hyp, col_hyp = suf_row // suf, suf_col // suf
    length = jnp.zeros_like(suf_row)
    for h in range(hyps):
        length = jnp.where(col_hyp == h, suffix_len[h], length)
    usable = (row_hyp == col_hyp) & (suf_col <= suf_row) & (suf_col - col_hyp * suf < length)
    loads[2].wait()
    scores = lax.dot_general(query_rows(ctx), suffix_kv[0, :, own], NT, preferred_element_type=jnp.float32)
    weights = jnp.where(usable, weights_of(scores), 0.0)
    suf_sum = jnp.dot(weights.astype(jnp.bfloat16), suffix_kv[1, :, own], preferred_element_type=jnp.float32)
    suf_total = jnp.sum(weights, 1, keepdims=True)

    loads[5].wait()
    tile = 128
    unit = (
        lax.broadcasted_iota(jnp.int32, (tile, tile), 0) == lax.broadcasted_iota(jnp.int32, (tile, tile), 1)
    ).astype(jnp.bfloat16)
    for k in range(0, down_raw.shape[1], tile):
        down_rows[k : k + tile, :] = lax.dot_general(
            unit, down_raw[:, k : k + tile], NT, preferred_element_type=jnp.float32
        ).astype(jnp.bfloat16)
    down_copies = [
        remote(
            down_rows.at[pl.ds(pl.multiple_of((2 * s + 1 - y_lo) * units, units), units), :],
            down_other.at[pl.ds(s * units, units), :],
            w_sem.at[0, 2 + s],
            w_sem.at[1, 2 + s],
            ctx=partner,
        )
        for s in range(nz)
    ]
    for s in range(nz):
        down_own[s * units : (s + 1) * units, :] = down_rows[
            pl.ds(pl.multiple_of((2 * s + y_lo) * units, units), units), :
        ]

    for dz in FAR_FIRST[:-1]:
        party_copy(dz).wait_recv()
        summed, flat = load_partial(party_recv.at[dz])
        store_partial(
            partz_send.at[dz], summed + part_own[dz, 0:rows, :], flat + part_own[dz, rows : rows + 1, :]
        )
        partz_copy(dz).start()

    for copy in down_copies[:2]:
        copy.start()

    party_copy(0).wait_recv()
    summed, flat = load_partial(party_recv.at[0])
    summed += part_own[0, 0:rows, :] + suf_sum
    flat += part_own[0, rows : rows + 1, :]
    for dz in FAR_FIRST[:-1]:
        partz_copy(dz).wait_recv()
        more, more_flat = load_partial(partz_recv.at[dz])
        summed += more
        flat += more_flat
    total = suf_total + jnp.sum(jnp.where(eye, flat, 0.0), 1, keepdims=True)
    attn = (summed / total).astype(jnp.bfloat16)
    attn = jnp.concatenate([attn[g * tokens : (g + 1) * tokens] for g in range(group)], 1)

    loads[3].wait()
    step = 512
    for c in range(0, width, step):
        term = jnp.dot(attn, w_out[:, c : c + step], preferred_element_type=jnp.float32)
        for i in range(n):
            proj_send[i, :, c : c + step] = term[i * slab : (i + 1) * slab].astype(jnp.bfloat16)

    def projy_copy(dz):
        return remote(
            proj_send.at[(1 - y_lo) * nz + along_z(dz)],
            projy_recv.at[dz],
            projy_sem.at[0, dz],
            projy_sem.at[1, dz],
            ctx=partner,
        )

    def projz_copy(dz):
        return remote(
            projz_send.at[dz],
            projz_recv.at[dz],
            projz_sem.at[0, dz],
            projz_sem.at[1, dz],
            ctx=along_z(dz) * 2 + y_lo,
        )

    for dz in FAR_FIRST:
        projy_copy(dz).start()

    first = y_lo * nz + z
    loads[4].wait()
    around = hidden_in[pl.ds(pl.multiple_of(first * slab // 16 * 16, 16), 16), :].astype(jnp.float32)
    before = jnp.zeros((slab, width), jnp.float32)
    for g in range(16 // slab):
        before = jnp.where(lax.rem(first, 16 // slab) == g, around[g * slab : (g + 1) * slab], before)

    for dz in FAR_FIRST[:-1]:
        projy_copy(dz).wait_recv()
        both = projy_recv[dz].astype(jnp.float32) + proj_send[y_lo * nz + along_z(dz)].astype(jnp.float32)
        projz_send[dz] = both.astype(jnp.bfloat16)
        projz_copy(dz).start()

    for copy in down_copies[2:]:
        copy.start()

    for copy in w_copies:
        copy.wait()
    loads[6].wait()
    loads[7].wait()

    def gain_rows(i, _):
        at = pl.ds(pl.multiple_of(i * 16, 16), 16)
        w_own[at, :] = (w_own[at, :].astype(jnp.float32) * gains[1:2, :half]).astype(jnp.bfloat16)
        return 0

    lax.fori_loop(0, 4 * units // 16, gain_rows, 0)

    projy_copy(0).wait_recv()
    proj = projy_recv[0].astype(jnp.float32) + proj_send[first].astype(jnp.float32)
    for dz in FAR_FIRST[:-1]:
        projz_copy(dz).wait_recv()
        proj += projz_recv[dz].astype(jnp.float32)
    scale_a = lax.rsqrt(jnp.mean(proj * proj, 1, keepdims=True) + eps)
    resid = (before + gains[0:1, :] * proj * scale_a).astype(jnp.bfloat16)
    for h in range(2):
        slab_own[h] = resid[:, h * half : (h + 1) * half]

    def slab_copy(to_z, to_core, from_z, from_core):
        return remote(
            slab_own.at[to_core],
            slabs.at[from_core, from_z],
            slab_ssem.at[to_core, to_z],
            slab_rsem.at[from_core, from_z],
            ctx=to_z * 2 + y_lo,
            req=req - core + to_core,
        )

    def send_slabs():
        for dz in FAR_FIRST[:-1]:
            slab_copy(along_z(dz), core, z, core).start()
            slab_copy(along_z(dz), 1 - core, z, core).start()

    def near_slabs():
        for dz in (1, -1):
            slab_copy(along_z(dz), core, along_z(dz), 0).wait_recv()

    slabs[core, z] = slab_own[core]
    slab_copy(z, 1 - core, z, core).start()

    @pl.when(core == 0)
    def _():
        send_slabs()
        near_slabs()

    @pl.when(core == 1)
    def _():
        near_slabs()
        send_slabs()

    def gather_slabs(c):
        for dz in FAR_FIRST[:-1] if c == 1 else (4, 3, 5, 2, 6):
            slab_copy(along_z(dz), core, along_z(dz), c).wait_recv()

        @pl.when(core != c)
        def _():
            slab_copy(z, core, z, c).wait_recv()

        for s in range(nz):
            at = (c * nz + s) * slab
            block[at : at + slab, :] = slabs[c, s].astype(jnp.float32)
        tok[c, 0] = block[c * part : (c + 1) * part, :].astype(jnp.bfloat16)

    def tok_copy(offset, link, sub):
        source = SLOT[(offset[0] - link[0]) % 4, (offset[1] - link[1]) % 4]
        slot = SLOT[offset[0] % 4, offset[1] % 4]
        there_ctx, there_req = chip(-link[0], -link[1])
        return remote(
            tok.at[sub, source],
            tok.at[sub, slot],
            tok_sem.at[0, sub, slot],
            tok_sem.at[1, sub, slot],
            ctx=there_ctx,
            req=there_req + core,
        )

    def token_step(step, sub):
        later_copies = []
        if step + 1 < len(ARRIVALS):
            for offset, link in ARRIVALS[step + 1]:
                source = SLOT[(offset[0] - link[0]) % 4, (offset[1] - link[1]) % 4]
                later_copies.append((source, tok_copy(offset, link, sub)))
        for offset, link in ARRIVALS[step]:
            tok_copy(offset, link, sub).wait_recv()
            for source, copy in later_copies:
                if source == SLOT[offset[0] % 4, offset[1] % 4]:
                    copy.start()
        for source, copy in later_copies:
            if source <= 4 * step:
                copy.start()

    def sib_copy(i):
        return remote(sib_send.at[i], sib_recv.at[i], sib_sem.at[0, i], sib_sem.at[1, i], req=sibling)

    own_part = {}
    ones = jnp.ones((16, half), jnp.bfloat16)

    def gate_up(i):
        those = tok[i % 2, i // 2 * blocks : (i // 2 + 1) * blocks].reshape(chunk, half)
        squares = lax.dot_general(ones, those * those, NT, preferred_element_type=jnp.float32)[:8]
        sib_send[i, 2 * units :] = squares
        sib_send[i, : 2 * units] = lax.dot_general(
            w_own[2 * units :, :], those, NT, preferred_element_type=jnp.float32
        )
        sib_copy(i).start()
        products = lax.dot_general(w_own[: 2 * units, :], those, NT, preferred_element_type=jnp.float32)
        own_part[i] = products, squares

    major = 1 - 2 * core

    def hid_copy(i, origin, to):
        source = along_z(origin)
        ref = hid.at[i // 2, source, i % 2]
        return remote(
            ref,
            ref,
            hid_ssem.at[i, lax.rem(to - origin + 2 * nz, nz)],
            hid_rsem.at[i, source],
            ctx=along_z(to) * 2 + y_lo,
        )

    def hidden(i):
        sib_copy(i).wait_recv()
        products, squares = own_part[i]
        both = products + sib_recv[i, : 2 * units]
        scale = lax.rsqrt((squares + sib_recv[i, 2 * units :])[0:1] * (1.0 / width) + eps)
        act = jax.nn.gelu(both[:units] * scale, approximate=True) * (both[units:] * scale)
        hid[i // 2, z, i % 2] = act.astype(jnp.bfloat16)
        for to in (2, -2, 1, -1):
            hid_copy(i, 0, to).start()

    def pass_on(i):
        for way in (1, -1):
            hid_copy(i, -2 * way, 0).wait_recv()

            @pl.when(major == way)
            def _():
                hid_copy(i, -2 * way, 2 * way).start()

            hid_copy(i, -2 * way, way).start()

    def hid_arrive(i):
        for origin in (-1, 1, -3, 3, 4):
            hid_copy(i, origin, 0).wait_recv()

    def hid_sent(i):
        for way in (1, -1):
            for away in (1, 2, 3):
                hid_copy(i, 0, way * away).wait_send()

            @pl.when(major == way)
            def _():
                hid_copy(i, 0, way * 4).wait_send()

    def ds_copy(g):
        return remote(ds_send.at[g], ds_recv.at[g], ds_sem.at[0, g], ds_sem.at[1, g], req=sibling)

    def down_terms(g, c):
        act = hid[g, :, c].reshape(nz * units, chunk).T
        return [
            jnp.dot(act, matrix[...], preferred_element_type=jnp.float32) for matrix in (down_own, down_other)
        ]

    def down(g):
        for i in (2 * g, 2 * g + 1):
            hid_arrive(i)
        for side, term in enumerate(down_terms(g, 1 - core)):
            ds_send[g, side] = term.astype(jnp.bfloat16)
        ds_copy(g).start()
        return down_terms(g, core)

    def rs_copy(g, b, side):
        dx, dy = OFFSETS[g * blocks + b]
        block_ctx, first_req = chip(dx, dy)
        lo = lax.rem(block_ctx, 2)
        to_ctx = ctx if side == 0 else partner
        possible = side == 0 and dx == 0 and dy in (0, 1, -1)
        copy = remote(
            rs_send.at[g, side, pl.ds(b * part, part), :],
            rs_recv.at[place, pl.ds(pl.multiple_of(lo * part, part), part), :],
            rs_ssem.at[g, side, b],
            rs_rsem.at[place],
            ctx=to_ctx,
            req=first_req + core,
        )
        return copy, lo, (first_req + core == req) if possible else None

    def send_terms(g, terms):
        ds_copy(g).wait_recv()
        for side in range(2):
            rs_send[g, side] = (terms[side] + ds_recv[g, side].astype(jnp.float32)).astype(jnp.bfloat16)
        for b in range(blocks):
            for side in (1, 0):
                copy, lo, here = rs_copy(g, b, side)
                if here is None:
                    copy.start()
                else:

                    @pl.when(here)
                    def _():
                        rs_recv[place, pl.ds(pl.multiple_of(lo * part, part), part), :] = rs_send[
                            g, side, pl.ds(b * part, part), :
                        ]

                    @pl.when(jnp.logical_not(here))
                    def _():
                        copy.start()

    def terms_sent(g):
        for b in range(blocks):
            for side in range(2):
                copy, lo, here = rs_copy(g, b, side)
                if here is None:
                    copy.wait_send()
                else:

                    @pl.when(jnp.logical_not(here))
                    def _():
                        copy.wait_send()

    for sub in range(2):
        gather_slabs(sub)
        for offset, link in ARRIVALS[0]:
            tok_copy(offset, link, sub).start()
    for dz in FAR_FIRST:
        party_copy(dz).wait_send()
        projy_copy(dz).wait_send()
    for dz in FAR_FIRST[:-1]:
        partz_copy(dz).wait_send()
        projz_copy(dz).wait_send()

    def tok_sent(step, sub):
        for offset, link in ARRIVALS[step]:
            tok_copy(offset, link, sub).wait_send()

    def slabs_sent():
        for dz in FAR_FIRST[:-1]:
            slab_copy(along_z(dz), core, z, core).wait_send()
            slab_copy(along_z(dz), 1 - core, z, core).wait_send()
        slab_copy(z, 1 - core, z, core).wait_send()

    for i in range(2 * CHUNKS):
        token_step(i // 2, i % 2)
        if i >= 2:
            pass_on(i - 2)
        gate_up(i)
        hidden(i)
        if i == 1:
            slabs_sent()
        if i >= 2:
            tok_sent((i - 2) // 2, i % 2)
            sib_copy(i - 2).wait_send()
        if i >= 5:
            hid_sent(i - 5)
        if i == 5:
            for copy in down_copies:
                copy.wait()
            first_terms = down(0)
        if i == 6:
            send_terms(0, first_terms)
            second_terms = down(1)
    pass_on(6)
    send_terms(1, second_terms)
    terms = down(2)
    pass_on(7)
    send_terms(2, terms)
    for sub in range(2):
        tok_sent(3, sub)
    for i in (6, 7):
        sib_copy(i).wait_send()
    for i in (3, 4, 5):
        hid_sent(i)
    for g in range(3):
        ds_copy(g).wait_send()

    def resid_copy(i):
        lo, slot = (y_lo, 0) if i == 0 else (1 - y_lo, 1 + 2 * y_lo)
        return remote(
            tok.at[1 - core, slot],
            resid_out.at[pl.ds(pl.multiple_of(lo * part, part), part), mine],
            resid_sem.at[0, i],
            resid_sem.at[1, i],
            req=sibling,
        )

    for i in range(2):
        resid_copy(i).start()
        lo, slot = (y_lo, 0) if i == 0 else (1 - y_lo, 1 + 2 * y_lo)
        resid_out[pl.ds(pl.multiple_of(lo * part, part), part), mine] = tok[core, slot]

    for i in (6, 7):
        hid_arrive(i)
        terms = down_terms(3, i % 2)

        @pl.when(core != i % 2)
        def _():
            for side in range(2):
                ds_send[3, side] = terms[side].astype(jnp.bfloat16)
            ds_copy(3).start()

        @pl.when(core == i % 2)
        def _():
            send_terms(3, terms)

    for i in (6, 7):
        hid_sent(i)
    ds_copy(3).wait_send()
    for i in range(2):
        resid_copy(i).wait()
    for g in range(CHUNKS):
        terms_sent(g)

    def add_terms(s, total):
        there = lax.rem(place + s, 16)
        remote(
            rs_recv.at[there],
            rs_recv.at[there],
            rs_ssem.at[0, 0, 0],
            rs_rsem.at[there],
            ctx=z * 2 + lax.rem(there, 2),
            req=there // 2 * 2 + core,
        ).wait_recv()
        return total + rs_recv[there].astype(jnp.float32)

    total = lax.fori_loop(1, 16, add_terms, rs_recv[place].astype(jnp.float32))
    out[...] = total.astype(jnp.bfloat16)


def place_kernel(resid, out, resid_out, out_out, held, small, sem):
    rows = resid.shape[0] // 4
    loads, stores = [], []
    for i in range(4):
        at = pl.ds(i * rows, rows)
        loads.append(pltpu.make_async_copy(resid.at[at, :], held.at[at, :], sem.at[0, i]))
        stores.append(pltpu.make_async_copy(held.at[at, :], resid_out.at[at, :], sem.at[1, i]))
    loads.append(pltpu.make_async_copy(out, small, sem.at[0, 4]))
    stores.append(pltpu.make_async_copy(small, out_out, sem.at[1, 4]))
    for load in loads:
        load.start()
    for load, store in zip(loads, stores):
        load.wait()
        store.start()
    for store in stores:
        store.wait()


def layer(
    hidden_in,
    queries,
    suffix_kv,
    prefix_kv,
    hyp_prefix,
    suffix_len,
    prefix_len,
    w_out,
    gain_attn,
    gain_pre,
    w_gate,
    w_up,
    w_down,
):
    n = 16
    nz = 8
    tokens, width = hidden_in.shape
    half = width // 2
    rows = HEADS // KV_HEADS * tokens
    slab = tokens // n
    positions = prefix_kv.shape[1] * prefix_kv.shape[2]
    units = w_gate.shape[1]
    columns = w_down.shape[1]
    chunk = 16 // CHUNKS * tokens // 2
    vmem = pl.BlockSpec(memory_space=pltpu.VMEM)
    smem = pl.BlockSpec(memory_space=pltpu.SMEM)
    hbm = pl.BlockSpec(memory_space=pl.ANY)
    dma = pltpu.SemaphoreType.DMA
    bf16 = jnp.bfloat16
    resid, out = pl.pallas_call(
        layer_kernel,
        out_shape=(
            jax.ShapeDtypeStruct((tokens, width), bf16),
            jax.ShapeDtypeStruct((tokens, columns), bf16),
        ),
        in_specs=[hbm, hbm, hbm, smem, smem, smem, hbm, hbm, vmem, vmem, hbm, hbm, hbm],
        out_specs=(vmem, vmem),
        scratch_shapes=[
            pltpu.VMEM(queries.shape, bf16),
            pltpu.VMEM(suffix_kv.shape, bf16),
            pltpu.VMEM(prefix_kv.shape, bf16),
            pltpu.VMEM(w_out.shape, bf16),
            pltpu.VMEM(hidden_in.shape, bf16),
            pltpu.VMEM((2, width), jnp.float32),
            pltpu.VMEM((rows, positions), jnp.float32),
            pltpu.VMEM((nz, rows + 16, HEAD), bf16),
            pltpu.VMEM((nz, rows + 16, HEAD), bf16),
            pltpu.VMEM((nz, rows + 8, HEAD), jnp.float32),
            pltpu.VMEM((nz, rows + 16, HEAD), bf16),
            pltpu.VMEM((nz, rows + 16, HEAD), bf16),
            pltpu.VMEM((n, slab, width), bf16),
            pltpu.VMEM((nz, slab, width), bf16),
            pltpu.VMEM((nz, slab, width), bf16),
            pltpu.VMEM((nz, slab, width), bf16),
            pltpu.VMEM((2, slab, half), bf16),
            pltpu.VMEM((columns, n * units), bf16),
            pltpu.VMEM((n * units, columns), bf16),
            pltpu.VMEM((nz * units, columns), bf16),
            pltpu.VMEM((nz * units, columns), bf16),
            pltpu.VMEM((4 * units, half), bf16),
            pltpu.VMEM((2, nz, slab, half), bf16),
            pltpu.VMEM((tokens, half), jnp.float32),
            pltpu.VMEM((2, 16, tokens // 2, half), bf16),
            pltpu.VMEM((2 * CHUNKS, 2 * units + 8, chunk), jnp.float32),
            pltpu.VMEM((2 * CHUNKS, 2 * units + 8, chunk), jnp.float32),
            pltpu.VMEM((CHUNKS, nz, 2, units, chunk), bf16),
            pltpu.VMEM((CHUNKS, 2, chunk, columns), bf16),
            pltpu.VMEM((CHUNKS, 2, chunk, columns), bf16),
            pltpu.VMEM((CHUNKS, 2, chunk, columns), bf16),
            pltpu.VMEM((16, tokens, columns), bf16),
            dma((8,)),
            dma((2, nz)),
            dma((2, nz)),
            dma((2, nz)),
            dma((2, nz)),
            dma((2, 2)),
            dma((2, 2 + nz)),
            dma((2, nz)),
            dma((2, nz)),
            dma((2, 2, 16)),
            dma((2, 2 * CHUNKS)),
            dma((2 * CHUNKS, nz)),
            dma((2 * CHUNKS, nz)),
            dma((2, CHUNKS)),
            dma((CHUNKS, 2, 4)),
            dma((16,)),
        ],
        compiler_params=pltpu.CompilerParams(
            collective_id=0, has_side_effects=True, vmem_limit_bytes=60 * 2**20
        ),
        cost_estimate=pl.CostEstimate(flops=5 * 10**9, bytes_accessed=10**7, transcendentals=10**6),
        name="layer",
    )(
        queries,
        suffix_kv,
        prefix_kv,
        hyp_prefix,
        suffix_len,
        prefix_len,
        w_out,
        hidden_in,
        gain_attn.reshape(-1, 128),
        gain_pre.reshape(-1, 128),
        w_gate.T,
        w_up.T,
        w_down.T,
    )
    return pl.pallas_call(
        place_kernel,
        out_shape=(jax.ShapeDtypeStruct(resid.shape, bf16), jax.ShapeDtypeStruct(out.shape, bf16)),
        in_specs=[hbm, hbm],
        out_specs=(hbm, hbm),
        scratch_shapes=[pltpu.VMEM(resid.shape, bf16), pltpu.VMEM(out.shape, bf16), dma((2, 5))],
        name="place",
    )(resid, out)


def solution(mesh):
    placed = (
        P("req", None),
        P("req", None),
        P(None, "req", None),
        P(None, "req", "ctx", None),
        P("req"),
        P("req"),
        P("req"),
        P("ctx", None),
        P(),
        P(),
        P(None, ("req", "ctx")),
        P(None, ("req", "ctx")),
        P("req", "ctx"),
    )
    return jax.shard_map(
        layer,
        mesh=mesh,
        in_specs=placed,
        out_specs=(P("req", None), P("req", "ctx")),
        check_vma=False,
    )
```
